512 devices in a mesh: dom: 128 (over y, x_lo, z), sub: 4 (over x_hi, core).
Axes of the slice: x: 4 (x_hi: 2, x_lo: 2; x = x_hi * 2 + x_lo), y: 4, z: 16, core: 2. Of those that a mesh axis runs over, the one named last changes fastest.
Arguments:
- initial_field: float32 [64, 256, 1024], P(None, 'dom', 'sub'), may hold values from -6 to 6
- adjoint_source: float32 [64, 256, 1024], P(None, 'dom', 'sub'), may hold values from -6 to 6
- moduli: float32 [3, 64, 256, 1024], P(None, None, 'dom', 'sub'), may hold values from 0.5 to 2
- node_mass: float32 [64, 256, 1024], P(None, 'dom', 'sub'), may hold values from 1 to 4
- block_owner: int32 [256, 1024], P('dom', 'sub'), may hold values from 0 to 511
- spline_basis: float32 [64, 64], replicated, may hold values from -0.75 to 0.75
Outputs:
- forward_final: float32 [64, 256, 1024], P(None, 'dom', 'sub')
- adjoint_final: float32 [64, 256, 1024], P(None, 'dom', 'sub')
- kernel: float32 [64, 65536], P(None, ('dom', 'sub'))
The draws below stay inside these ranges and needn't reach their ends.
Inputs may be any that keep to these rules, and one draw needn't show every extreme that they name: block_owner names a block of the element's own partition.
All inputs are finite; a program needn't handle non-finite values.
Results may differ from the reference program's by a relative error of at most 0.0001.
Values sent between devices are 32-bit elements; how exact they have to be, the bound alone decides.
No kernel may reach another device: no remote copies, remote signals or barrier semaphores. Data moves between devices by JAX's collectives and lax.ppermute only.
A program may use at most 64 MiB of HBM per device.

```python
import math
import jax
import jax.numpy as jnp
import numpy as np
from jax import lax

NODES = 64
EX_DEV = 2
STEPS = 4
NEX = 256
NEY = 1024
NBP = 512
NB = 65536


def touch_ends(drawn, stream_key, smallest, top_value):
    index_at = [jax.random.randint(jax.random.fold_in(stream_key, axis), (), 0, length) for axis, length in enumerate(drawn.shape)]
    main_axis = drawn.shape.index(max(drawn.shape))
    beside = index_at[:main_axis] + [(index_at[main_axis] + 1) % drawn.shape[main_axis]] + index_at[main_axis + 1:]
    return drawn.at[tuple(index_at)].set(smallest).at[tuple(beside)].set(top_value)


def shard_levels(rng, dims, cuts, smallest, top_value):
    level, own = 1.0, jax.random.fold_in(rng, 6)
    for position, blocks in cuts:
        steps = jnp.exp(jax.random.uniform(jax.random.fold_in(own, position), (blocks,), jnp.float32, smallest / len(cuts), top_value / len(cuts)))
        level = level * jnp.repeat(steps, dims[position] // blocks).reshape([-1 if axis == position else 1 for axis in range(len(dims))])
    return level


def normal_values(own_key, dims, width, reach, shards=(), kind=jnp.bfloat16):
    result = width * jax.random.normal(own_key, dims, jnp.float32)
    if shards:
        result = result * shard_levels(own_key, dims, shards, -0.22, 0.18)
    return jnp.clip(result, -reach, reach).astype(kind)


def setup_inputs(seed: int = 0) -> dict:
    key_of = jax.random.split(jax.random.key(seed), 7)
    initial_field = normal_values(key_of[0], (NODES, NEX, NEY), 1.0, 6.0, ((1, 128), (2, 4)), jnp.float32)
    adjoint_source = normal_values(key_of[1], (NODES, NEX, NEY), 1.0, 6.0, ((1, 128), (2, 4)), jnp.float32)
    moduli = jnp.clip(jnp.exp(math.log(2.0) - 1.3862944 * jax.random.uniform(key_of[2], (3, NODES, NEX, NEY), jnp.float32) ** shard_levels(key_of[2], (3, NODES, NEX, NEY), ((2, 128), (3, 4)), -0.2, 0.2)), 0.5, 2.0)
    node_mass = jnp.clip(jnp.exp(math.log(4.0) - 1.3862944 * jax.random.uniform(key_of[3], (NODES, NEX, NEY), jnp.float32) ** shard_levels(key_of[3], (NODES, NEX, NEY), ((1, 128), (2, 4)), -0.2, 0.2)), 1.0, 4.0)
    block_owner = touch_ends(jax.random.randint(key_of[4], (NEX, NEY), 0, NBP), jax.random.fold_in(key_of[4], 1), 0, NBP - 1).astype(jnp.int32)
    spline_basis = normal_values(key_of[5], (NODES, NODES), NODES ** -0.5, 0.75, (), jnp.float32)
    return dict(initial_field=initial_field, adjoint_source=adjoint_source, moduli=moduli, node_mass=node_mass, block_owner=block_owner, spline_basis=spline_basis)


DERIVATIVE = np.array([[-3.0, 4.04508497187474, -1.54508497187474, 0.5],
                       [-0.80901699437495, 0.0, 1.11803398874989, -0.30901699437495],
                       [0.30901699437495, -1.11803398874989, 0.0, 0.80901699437495],
                       [-0.5, 1.54508497187474, -4.04508497187474, 3.0]])
IDENTITY_FOUR = np.eye(4)
GRADIENT_TABLE = np.concatenate([np.kron(np.kron(DERIVATIVE, IDENTITY_FOUR), IDENTITY_FOUR),
                                 np.kron(np.kron(IDENTITY_FOUR, DERIVATIVE), IDENTITY_FOUR),
                                 np.kron(np.kron(IDENTITY_FOUR, IDENTITY_FOUR), DERIVATIVE)], axis=0).astype(np.float32)
TIME_STEP = 0.1
KERNEL_SCALE = 0.05


def stiffness_apply(displace, moduli):
    count = displace.shape[1] * displace.shape[2]
    flat = displace.reshape(64, count)
    gradients = jnp.dot(GRADIENT_TABLE, flat, precision=lax.Precision.HIGHEST)
    fluxes = moduli.reshape(192, count) * gradients
    forces = jnp.dot(GRADIENT_TABLE.T, fluxes, precision=lax.Precision.HIGHEST)
    return forces.reshape(displace.shape), gradients


def add_along_x(values, from_left, from_right):
    lower_face = values[0]
    upper_face = values[3]
    upper_prev = jnp.concatenate([from_left, upper_face[:, :-1]], axis=1)
    lower_next = jnp.concatenate([lower_face[:, 1:], from_right], axis=1)
    return jnp.concatenate([(lower_face + upper_prev)[None], values[1:3], (upper_face + lower_next)[None]], axis=0)


def add_along_y(values, from_below, from_above):
    lower_face = values[:, 0]
    upper_face = values[:, 3]
    upper_prev = jnp.concatenate([from_below, upper_face[..., :-1]], axis=3)
    lower_next = jnp.concatenate([lower_face[..., 1:], from_above], axis=3)
    return jnp.concatenate([(lower_face + upper_prev)[:, None], values[:, 1:3], (upper_face + lower_next)[:, None]], axis=1)


def assemble_zero_rim(values):
    rows_x, rows_y = values.shape[1], values.shape[2]
    split_x = values.reshape(4, 16, rows_x, rows_y)
    empty_x = jnp.zeros((16, 1, rows_y), values.dtype)
    merged = add_along_x(split_x, empty_x, empty_x)
    split_y = merged.reshape(4, 4, 4, rows_x, rows_y)
    empty_y = jnp.zeros((4, 4, rows_x, 1), values.dtype)
    return add_along_y(split_y, empty_y, empty_y).reshape(64, rows_x, rows_y)


def run_steps(start, moduli, mass_total):
    displace = start
    velocity = jnp.zeros_like(start)
    saved = []
    for index_step in range(STEPS):
        forces, gradients = stiffness_apply(displace, moduli)
        saved.append(gradients)
        velocity = velocity - TIME_STEP * assemble_zero_rim(forces) / mass_total
        displace = displace + TIME_STEP * velocity
    return displace, saved


def reference(initial_field, adjoint_source, moduli, node_mass, block_owner, spline_basis):
    mass_total = assemble_zero_rim(node_mass)
    forward_final, forward_saved = run_steps(initial_field, moduli, mass_total)
    count = NEX * NEY
    last_grad = jnp.dot(GRADIENT_TABLE, forward_final.reshape(64, count), precision=lax.Precision.HIGHEST)
    partner = [last_grad] + [forward_saved[STEPS - m] for m in range(1, STEPS)]
    adjoint_final, adjoint_saved = run_steps(adjoint_source, moduli, mass_total)
    flat_moduli = moduli.reshape(192, count)
    density = jnp.zeros((64, count), jnp.float32)
    for m in range(STEPS):
        density = density + (flat_moduli * adjoint_saved[m] * partner[m]).reshape(3, 64, count).sum(axis=0)
    segment_ids = ((jnp.arange(NEX)[:, None] // EX_DEV) * NBP + block_owner).astype(jnp.int32)
    sums = jax.ops.segment_sum(density.T, segment_ids.reshape(-1), num_segments=NB)
    kernel = jnp.dot(spline_basis.T, sums.T, precision=lax.Precision.HIGHEST) * KERNEL_SCALE
    return forward_final, adjoint_final, kernel
```

```python
import jax
import jax.numpy as jnp
import numpy as np
from jax import lax
from jax.experimental import pallas as pl
from jax.experimental.pallas import tpu as pltpu
from jax.sharding import PartitionSpec as P

STEPS = 4
TIME_STEP = 0.1
KERNEL_SCALE = 0.05
PUSH = TIME_STEP * TIME_STEP

DERIVATIVE = np.array(
    [
        [-3.0, 4.04508497187474, -1.54508497187474, 0.5],
        [-0.80901699437495, 0.0, 1.11803398874989, -0.30901699437495],
        [0.30901699437495, -1.11803398874989, 0.0, 0.80901699437495],
        [-0.5, 1.54508497187474, -4.04508497187474, 3.0],
    ]
)
IDENTITY_FOUR = np.eye(4)
GRADIENT_TABLE = np.concatenate(
    [
        np.kron(np.kron(DERIVATIVE, IDENTITY_FOUR), IDENTITY_FOUR),
        np.kron(np.kron(IDENTITY_FOUR, DERIVATIVE), IDENTITY_FOUR),
        np.kron(np.kron(IDENTITY_FOUR, IDENTITY_FOUR), DERIVATIVE),
    ],
    axis=0,
).astype(np.float32)

HALF_AMB = float((DERIVATIVE[0, 1] - DERIVATIVE[0, 2]) / 2)
HALF_CME = float((DERIVATIVE[1, 0] - DERIVATIVE[1, 3]) / 2)
HALF_D = float(DERIVATIVE[1, 2] / 2)

RAW, FAR, MFAR, ZST, SFAR, SMFAR, MSG = 0, 96, 104, 112, 120, 122, 124
MSG_B = 20


def sub_iota():
    return lax.broadcasted_iota(jnp.int32, (8, 128), 0)


def lane_iota(rows=8):
    return lax.broadcasted_iota(jnp.int32, (rows, 128), 1)


def rs(x, shift):
    return pltpu.roll(x, shift, 0)


def rl(x, shift):
    return pltpu.roll(x, shift, 1)


def masks():
    s = sub_iota()
    lane = lane_iota()
    return dict(
        even=(s % 2) == 0,
        lo=s < 4,
        ct0=((s // 2) % 2) == 0,
        first=lane == 0,
        last=lane == 127,
    )


def d_line(x0, x1, x2, x3):
    p, m, q, n = x0 + x3, x0 - x3, x1 + x2, x1 - x2
    r = q - p
    s1 = -1.75 * m + HALF_AMB * n
    s2 = HALF_CME * m - HALF_D * n
    r1, r2 = 1.25 * r, HALF_D * r
    return s1 + r1, s2 + r2, s2 - r2, s1 - r1


def dt_line(x0, x1, x2, x3):
    p, m, q, n = x0 + x3, x0 - x3, x1 + x2, x1 - x2
    t = 1.25 * m + HALF_D * n
    q1 = HALF_CME * q - 1.75 * p
    q2 = HALF_AMB * p - HALF_D * q
    return q1 - t, t + q2, t - q2, -(q1 + t)


def line_nodes(direction, a, b):
    if direction == 0:
        return [16 * i + 4 * a + b for i in range(4)]
    if direction == 1:
        return [16 * a + 4 * j + b for j in range(4)]
    return [16 * a + 4 * b + k for k in range(4)]


def node_moduli(mod, h, g, mk):
    x = mod[h, g // 2]
    if g % 2 == 0:
        return jnp.where(mk["lo"], x, rs(x, 4))
    return jnp.where(mk["lo"], rs(x, 4), x)


def forces(u, f, mod, h, mk):
    for direction in (2, 1, 0):
        for a in range(4):
            for b in range(4):
                nodes = line_nodes(direction, a, b)
                g = d_line(*[u[h, n] for n in nodes])
                t = [
                    node_moduli(mod, h, 64 * direction + n, mk) * gn for n, gn in zip(nodes, g)
                ]
                out = dt_line(*t)
                for n, o in zip(nodes, out):
                    f[h, n] = o if direction == 2 else f[h, n] + o


def far_pack(f, mk):
    left, right = [], []
    for p in range(8):
        left.append(jnp.where(mk["even"], rs(f(2 * p), 7), f(2 * p + 1)))
        right.append(jnp.where(mk["even"], f(48 + 2 * p), rs(f(48 + 2 * p + 1), 1)))
    return left, right


def x_assemble(f, mk, from_right=None, from_left=None, base=0):
    even = mk["even"]
    for q in range(16):
        ao, bo, a_s, b_s = f[0, 48 + q], f[0, q], f[1, 48 + q], f[1, q]
        f[0, 48 + q] = ao + jnp.where(even, rs(bo, 7), rs(b_s, 1))
        f[0, q] = bo + jnp.where(even, rs(a_s, 7), rs(ao, 1))
        if from_right is not None:
            fr, fl = from_right[base + q // 2], from_left[base + q // 2]
            if q % 2 == 0:
                fl = rs(fl, 1)
            else:
                fr = rs(fr, 7)
            f[1, 48 + q] = a_s + jnp.where(even, fr, rs(bo, 1))
            f[1, q] = b_s + jnp.where(even, rs(ao, 7), fl)


def y_assemble(f, strip, h, mk):
    shift = 4 if h else 68
    for i in range(4):
        for k in range(4):
            na, nb = 16 * i + 12 + k, 16 * i + k
            inj_low = pltpu.roll(
                jnp.broadcast_to(strip[na : na + 1, :], (8, 128)), shift, 1, stride=8, stride_axis=0
            )
            inj_high = pltpu.roll(
                jnp.broadcast_to(strip[nb : nb + 1, :], (8, 128)), shift, 1, stride=8, stride_axis=0
            )
            a, b = f[h, na], f[h, nb]
            up, down = rl(b, 127), rl(a, 1)
            up = jnp.where(mk["last"], jnp.where(mk["ct0"], rs(up, 6), inj_high), up)
            down = jnp.where(mk["first"], jnp.where(mk["ct0"], inj_low, rs(down, 2)), down)
            f[h, na] = a + up
            f[h, nb] = b + down


def update(u, v, f, inv, h, first=False):
    for n in range(64):
        push = inv[h, n] * f[h, n]
        vel = -push if first else v[h, n] - push
        v[h, n] = vel
        u[h, n] = u[h, n] + vel


def strip_forces(us, mods, table, table_t):
    g = jnp.dot(table, us, precision=lax.Precision.HIGHEST, preferred_element_type=jnp.float32)
    return jnp.dot(
        table_t, mods * g, precision=lax.Precision.HIGHEST, preferred_element_type=jnp.float32
    )


def strip_x(f, far_right, far_left):
    lane = lane_iota(16)
    even, own = ((lane // 8) % 2) == 1, lane < 64
    b, a = f[0:16], f[48:64]
    na = a + jnp.where(even, jnp.where(own, rl(b, 8), rl(far_right, 72)), rl(b, 56))
    nb = b + jnp.where(even, rl(a, 72), jnp.where(own, rl(a, 120), rl(far_left, 56)))
    return jnp.concatenate([nb, f[16:48], na], axis=0)


def strip_y(f):
    low = sub_iota() < 4
    parts = []
    for i in range(4):
        x, y = f[16 * i : 16 * i + 8], f[16 * i + 8 : 16 * i + 16]
        parts.append(x + jnp.where(low, rs(rl(y, 1), 4), 0.0))
        parts.append(y + jnp.where(low, 0.0, rs(rl(x, 127), 4)))
    return jnp.concatenate(parts, axis=0)


def inverse_mass(m):
    return jnp.where(m > 0.5, PUSH / jnp.where(m > 0.5, m, 1.0), 0.0)


def strip_arrays(z1o, z2o, z1s, z2s):
    q = lane_iota(64) // 32

    def four(a, b, c, d):
        return jnp.where(q < 2, jnp.where(q == 0, a, b), jnp.where(q == 2, c, d))

    us = jnp.where(q < 2, z1o, rl(z1s, 64))
    m0 = four(rl(z1o, 64), rl(z1o, 96), z1s, rl(z1s, 32))
    m1 = four(rl(z1o, 32), rl(z1o, 64), rl(z1s, 96), z1s)
    m2 = four(z2o, rl(z2o, 32), rl(z2s, 64), rl(z2s, 96))
    mass = four(rl(z2o, 96), z2o, rl(z2s, 32), rl(z2s, 64))
    return us, jnp.concatenate([m0, m1, m2], axis=0), mass


def pair_expand(x, mk):
    r = rs(x, 4)
    return jnp.where(mk["lo"], x, r), jnp.where(mk["lo"], r, x)


def state_expand(xu, xw, mk):
    return jnp.where(mk["lo"], xu, rs(xw, 4)), jnp.where(mk["lo"], rs(xu, 4), xw)


def edge_kernel(u_ref, w_ref, m_ref, mass_ref, z_ref):
    lane = lane_iota(64)
    pieces = (
        (w_ref, 0, 0, 0),
        (u_ref, 0, 0, 1),
        (m_ref, 0, 0, 2),
        (m_ref, 256, 0, 3),
        (m_ref, 512, 1, 0),
        (mass_ref, 0, 1, 1),
    )
    z = [jnp.zeros((64, 128), jnp.float32), jnp.zeros((64, 128), jnp.float32)]
    for ref, base, half, slot in pieces:
        for side in range(2):
            for r in range(2):
                rows = ref[pl.ds(base + 2 * (1 - side) + r, 64, stride=4), :]
                dest = slot * 32 + (1 - side) * 16 + (1 - r) * 8 + (3 if side else 1)
                src = 0 if side else 124
                moved = rl(rows, (dest - src) % 128)
                z[half] = jnp.where((lane >= dest) & (lane < dest + 4), moved, z[half])
    z_ref[0] = z[0]
    z_ref[1] = z[1]


def first_kernel(u_ref, w_ref, mod_ref, state_ref, f_ref):
    mk = masks()
    for p in range(32):
        a, b = state_expand(u_ref[p], w_ref[p], mk)
        state_ref[0, 2 * p] = a
        state_ref[0, 2 * p + 1] = b
    forces(state_ref, f_ref, mod_ref, 0, mk)


def send_kernel(
    sub_ref, u_ref, w_ref, mod_ref, mass_ref, f_ref, z_ref, table_ref, tablet_ref,
    left_ref, right_ref, zo_ref,
):
    mk = masks()
    even = mk["even"]
    sub = sub_ref[0]
    base = 0
    for ref in (u_ref, w_ref, mod_ref, mass_ref):
        count = ref.shape[0] // 2
        for p in range(count):
            x, y = ref[2 * p], ref[2 * p + 1]
            left_ref[base + p] = jnp.where(even, x, rs(y, 1))
            right_ref[base + p] = jnp.where(even, rs(x, 7), y)
        base += count
    left, right = far_pack(lambda n: f_ref[0, n], mk)
    for p in range(8):
        left_ref[FAR + p] = left[p]
        right_ref[FAR + p] = right[p]

    def mass_node(n):
        return pair_expand(mass_ref[n // 2], mk)[n % 2]

    left, right = far_pack(mass_node, mk)
    for p in range(8):
        left_ref[MFAR + p] = left[p]
        right_ref[MFAR + p] = right[p]
    lane = lane_iota(64)
    side0 = ((lane // 16) % 2) == 1
    c = lane % 8
    below, above = jnp.maximum(sub - 1, 0), jnp.minimum(sub + 1, 3)
    zs = []
    for half in range(2):
        own = z_ref[sub, half]
        zl = jnp.where(sub > 0, z_ref[below, half], 0.0)
        zr = jnp.where(sub < 3, z_ref[above, half], 0.0)
        low = jnp.where(c == 0, 0.0, jnp.where(c <= 4, zl, rl(own, 18)))
        high = jnp.where(c <= 2, rl(own, 110), jnp.where(c == 7, 0.0, zr))
        z = jnp.where(side0, low, high)
        zo_ref[half] = z
        zs.append(z)
    zero = jnp.zeros((64, 128), jnp.float32)
    us, mods, mass = strip_arrays(zs[0], zs[1], zero, zero)
    fs = strip_forces(us, mods, table_ref[...], tablet_ref[...])
    evg = ((lane // 8) % 2) == 0
    wl = jnp.where(evg, rl(zs[1], 120), zs[0])
    wr = jnp.where(evg, zs[0], rl(zs[1], 8))
    for p in range(8):
        left_ref[ZST + p] = wl[8 * p : 8 * p + 8]
        right_ref[ZST + p] = wr[8 * p : 8 * p + 8]
    for p in range(2):
        left_ref[SFAR + p] = fs[8 * p : 8 * p + 8]
        right_ref[SFAR + p] = fs[48 + 8 * p : 56 + 8 * p]
        left_ref[SMFAR + p] = mass[8 * p : 8 * p + 8]
        right_ref[SMFAR + p] = mass[48 + 8 * p : 56 + 8 * p]


def rows16(ref, at):
    return jnp.concatenate([ref[at], ref[at + 1]], axis=0)


def middle_kernel(
    mod_ref, mass_ref, u0_ref, f0_ref, zo_ref, mr_ref, ml_ref, table_ref, tablet_ref,
    bl_ref, br_ref, mm_ref, inv_ref, u1_ref, v1_ref, f1_ref, u2_ref, v2_ref, f2_ref,
    smod_ref, sinv_ref, sstate_ref,
    u, v, f, sx,
):
    mk = masks()
    even, lo = mk["even"], mk["lo"]
    table, tablet = table_ref[...], tablet_ref[...]

    def shadow(p):
        r, l = mr_ref[p], ml_ref[p]
        return jnp.where(even, r, rs(l, 1)), jnp.where(even, rs(r, 7), l)

    for p in range(16):
        su, sw = shadow(p), shadow(16 + p)
        for e in range(2):
            u[1, 4 * p + 2 * e], u[1, 4 * p + 2 * e + 1] = state_expand(su[e], sw[e], mk)
    for p in range(48):
        mm_ref[1, 2 * p], mm_ref[1, 2 * p + 1] = shadow(32 + p)
    for p in range(96):
        mm_ref[0, p] = mod_ref[0, p]
    for p in range(16):
        sm = shadow(80 + p)
        for e in range(2):
            f[1, 4 * p + 2 * e], f[1, 4 * p + 2 * e + 1] = pair_expand(sm[e], mk)
    for p in range(32):
        f[0, 2 * p], f[0, 2 * p + 1] = pair_expand(mass_ref[p], mk)
    wr = jnp.concatenate([mr_ref[ZST + p] for p in range(8)], axis=0)
    wl = jnp.concatenate([ml_ref[ZST + p] for p in range(8)], axis=0)
    evg = ((lane_iota(64) // 8) % 2) == 0
    z1s = jnp.where(evg, wl, wr)
    z2s = jnp.where(evg, rl(wl, 120), rl(wr, 8))
    us, mods, smass = strip_arrays(zo_ref[0], zo_ref[1], z1s, z2s)
    smod_ref[...] = mods
    smass = strip_x(smass, rows16(mr_ref, SMFAR), rows16(ml_ref, SMFAR))
    sx[...] = smass
    x_assemble(f, mk, mr_ref, ml_ref, MFAR)
    for h in range(2):
        y_assemble(f, sx, h, mk)
    sinv = inverse_mass(strip_y(smass))
    sinv_ref[...] = sinv

    def invert(n, carry):
        inv_ref[0, n] = inverse_mass(f[0, n])
        inv_ref[1, n] = inverse_mass(f[1, n])
        return carry

    lax.fori_loop(0, 64, invert, 0, unroll=8)
    for n in range(64):
        f[0, n] = f0_ref[0, n]
        u[0, n] = u0_ref[0, n]
    forces(u, f, mm_ref, 1, mk)
    fs = strip_forces(us, mods, table, tablet)
    fs = strip_x(fs, rows16(mr_ref, SFAR), rows16(ml_ref, SFAR))
    sx[...] = fs
    x_assemble(f, mk, mr_ref, ml_ref, FAR)
    for h in range(2):
        y_assemble(f, sx, h, mk)
    svel = -sinv * strip_y(fs)
    us = us + svel
    for h in range(2):
        update(u, v, f, inv_ref, h, first=True)
    for n in range(64):
        for h in range(2):
            u1_ref[h, n] = u[h, n]
        v1_ref[1, n] = v[1, n]
        v1_ref[0, n] = v[0, n]
    lax.fori_loop(0, 2, lambda h, c: (forces(u, f, mm_ref, h, mk), c)[1], 0)
    fs = strip_forces(us, mods, table, tablet)
    sstate_ref[0] = us
    sstate_ref[1] = svel
    sstate_ref[2] = fs
    left, right = far_pack(lambda n: f[0, n], mk)
    for p in range(8):
        bl_ref[p] = left[p]
        br_ref[p] = right[p]
    for p in range(2):
        bl_ref[16 + p] = fs[8 * p : 8 * p + 8]
        br_ref[16 + p] = fs[48 + 8 * p : 56 + 8 * p]
    for n in range(64):
        for h in range(2):
            f1_ref[h, n] = f[h, n]
    zero = jnp.zeros((16, 128), jnp.float32)
    fs = strip_x(fs, zero, zero)
    sx[...] = fs
    x_assemble(f, mk)
    y_assemble(f, sx, 0, mk)
    svel = svel - sinv * strip_y(fs)
    us = us + svel
    update(u, v, f, inv_ref, 0)
    for n in range(64):
        u2_ref[n] = u[0, n]
        v2_ref[n] = v[0, n]
    forces(u, f, mm_ref, 0, mk)
    fs = strip_forces(us, mods, table, tablet)
    left, right = far_pack(lambda n: f[0, n], mk)
    for p in range(8):
        bl_ref[8 + p] = left[p]
        br_ref[8 + p] = right[p]
    for p in range(2):
        bl_ref[18 + p] = fs[8 * p : 8 * p + 8]
        br_ref[18 + p] = fs[48 + 8 * p : 56 + 8 * p]
    for n in range(64):
        f2_ref[n] = f[0, n]


def last_kernel(
    br_ref, bl_ref, mm_ref, inv_ref, u0_ref, u1_ref, v1_ref, f1_ref, u2_ref, v2_ref, f2_ref,
    smod_ref, sinv_ref, sstate_ref, owner_ref, table_ref, tablet_ref,
    out_u_ref, out_w_ref, sums_ref,
    u, v, f, sx, u3, dens, hot,
):
    mk = masks()
    lo = mk["lo"]
    table, tablet = table_ref[...], tablet_ref[...]
    mods, sinv = smod_ref[...], sinv_ref[...]
    us, svel, fs = sstate_ref[0], sstate_ref[1], sstate_ref[2]
    for n in range(64):
        f[0, n] = f1_ref[0, n]
        f[1, n] = f1_ref[1, n]
        u[1, n] = u1_ref[1, n]
        v[1, n] = v1_ref[1, n]
    fs = strip_x(fs, rows16(br_ref, 16), rows16(bl_ref, 16))
    sx[...] = fs
    x_assemble(f, mk, br_ref, bl_ref, 0)
    y_assemble(f, sx, 1, mk)
    svel = svel - sinv * strip_y(fs)
    us = us + svel
    update(u, v, f, inv_ref, 1)
    for n in range(64):
        f[0, n] = f2_ref[n]
        u[0, n] = u2_ref[n]
        v[0, n] = v2_ref[n]
    forces(u, f, mm_ref, 1, mk)
    fs = strip_forces(us, mods, table, tablet)
    fs = strip_x(fs, rows16(br_ref, 18), rows16(bl_ref, 18))
    sx[...] = fs
    x_assemble(f, mk, br_ref, bl_ref, 8)
    for h in range(2):
        y_assemble(f, sx, h, mk)
    svel = svel - sinv * strip_y(fs)
    us = us + svel
    for h in range(2):
        update(u, v, f, inv_ref, h)
    for n in range(64):
        u3[0, n] = u[0, n]
    lax.fori_loop(0, 2, lambda h, c: (forces(u, f, mm_ref, h, mk), c)[1], 0)
    fs = strip_forces(us, mods, table, tablet)
    zero = jnp.zeros((16, 128), jnp.float32)
    sx[...] = strip_x(fs, zero, zero)
    x_assemble(f, mk)
    y_assemble(f, sx, 0, mk)
    update(u, v, f, inv_ref, 0)
    for p in range(32):
        a, b = u[0, 2 * p], u[0, 2 * p + 1]
        out_u_ref[p] = jnp.where(lo, a, rs(b, 4))
        out_w_ref[p] = jnp.where(lo, rs(a, 4), b)
    for direction in (2, 1, 0):
        for a in range(4):
            for b in range(4):
                nodes = line_nodes(direction, a, b)
                g0 = d_line(*[u0_ref[0, n] for n in nodes])
                g1 = d_line(*[u1_ref[0, n] for n in nodes])
                g2 = d_line(*[u2_ref[n] for n in nodes])
                g3 = d_line(*[u3[0, n] for n in nodes])
                g4 = d_line(*[u[0, n] for n in nodes])
                for e, n in enumerate(nodes):
                    t = g1[e] * rs(g3[e], 4) + jnp.where(
                        lo, g2[e] * rs(g2[e], 4), g0[e] * rs(g4[e], 4)
                    )
                    t = t * node_moduli(mm_ref, 0, 64 * direction + n, mk)
                    at = pl.ds(8 * n, 8)
                    dens[at, :] = t if direction == 2 else dens[at, :] + t
    block = lax.broadcasted_iota(jnp.int32, (512, 128), 0)
    cols = []
    for s in range(4):
        cols.append(
            dens[pl.ds(s, 64, stride=8), :] + dens[pl.ds(s + 4, 64, stride=8), :]
        )
        owner = jnp.broadcast_to(owner_ref[s : s + 1, :], (512, 128))
        hot[:, 128 * s : 128 * s + 128] = (block == owner).astype(jnp.float32).astype(jnp.bfloat16)
    d = jnp.concatenate(cols, axis=1)
    hi = d.astype(jnp.bfloat16)
    rest = d - hi.astype(jnp.float32)
    mid = rest.astype(jnp.bfloat16)
    low = (rest - mid.astype(jnp.float32)).astype(jnp.bfloat16)
    split = jnp.concatenate([hi, mid, low], axis=0)
    res = lax.dot_general(
        split, hot[...], (((1,), (1,)), ((), ())), preferred_element_type=jnp.float32
    )
    sums = res[0:64] + (res[64:128] + res[128:192])
    for q in range(4):
        sums_ref[q] = sums[:, 128 * q : 128 * q + 128]


def project_kernel(x_ref, basis_ref, out_ref):
    total = (x_ref[0] + x_ref[1]) + (x_ref[2] + x_ref[3])
    out_ref[...] = KERNEL_SCALE * jnp.dot(
        basis_ref[...], total, precision=lax.Precision.HIGHEST, preferred_element_type=jnp.float32
    )


def call(kernel, outs, ins, scratch=(), smem_first=False):
    vmem = pl.BlockSpec(memory_space=pltpu.VMEM)
    specs = [vmem] * len(ins)
    if smem_first:
        specs[0] = pl.BlockSpec(memory_space=pltpu.SMEM)
    return pl.pallas_call(
        kernel,
        out_shape=[jax.ShapeDtypeStruct(s, jnp.float32) for s in outs],
        in_specs=specs,
        out_specs=[vmem] * len(outs),
        scratch_shapes=[pltpu.VMEM(s, t) for s, t in scratch],
        compiler_params=pltpu.CompilerParams(vmem_limit_bytes=28 * 1024 * 1024),
    )(*ins)


def raw_tiles(x):
    lead = int(np.prod(x.shape[:-2]))
    return x.reshape(lead, 2, 2, 128).transpose(0, 2, 1, 3).reshape(lead * 4, 128)


def from_tiles(x):
    return x.reshape(64, 2, 2, 128).transpose(0, 2, 1, 3).reshape(64, 2, 256)


def on_device(initial_field, adjoint_source, moduli, node_mass, block_owner, spline_basis):
    count = lax.axis_size("dom")
    to_right = [(i, i + 1) for i in range(count - 1)]
    to_left = [(b, a) for a, b in to_right]
    table = jnp.asarray(GRADIENT_TABLE)
    tablet = jnp.asarray(np.ascontiguousarray(GRADIENT_TABLE.T))
    sub = lax.axis_index("sub").astype(jnp.int32).reshape(1)
    u2d, w2d, m2d, mass2d = map(raw_tiles, (initial_field, adjoint_source, moduli, node_mass))
    owner = raw_tiles(block_owner[None])
    u, w, mass = (x.reshape(32, 8, 128) for x in (u2d, w2d, mass2d))
    mod = m2d.reshape(1, 96, 8, 128)
    tile = (64, 8, 128)
    one, two = (1,) + tile, (2,) + tile

    (edges,) = call(edge_kernel, [(2, 64, 128)], [u2d, w2d, m2d, mass2d])
    edges = lax.all_gather(edges, "sub")
    u0, f0 = call(first_kernel, [one, one], [u, w, mod])
    left, right, zo = call(
        send_kernel,
        [(MSG, 8, 128), (MSG, 8, 128), (2, 64, 128)],
        [sub, u, w, mod[0], mass, f0, edges, table, tablet],
        smem_first=True,
    )
    from_right = lax.ppermute(left, "dom", to_left)
    from_left = lax.ppermute(right, "dom", to_right)
    f32 = jnp.float32
    bl, br, mm, inv, u1, v1, f1, u2, v2, f2, smod, sinv, sstate = call(
        middle_kernel,
        [
            (MSG_B, 8, 128), (MSG_B, 8, 128), (2, 96, 8, 128), two, two, two, two,
            tile, tile, tile, (192, 128), (64, 128), (3, 64, 128),
        ],
        [mod, mass, u0, f0, zo, from_right, from_left, table, tablet],
        [(two, f32)] * 3 + [((64, 128), f32)],
    )
    from_right = lax.ppermute(bl, "dom", to_left)
    from_left = lax.ppermute(br, "dom", to_right)
    out_u, out_w, sums = call(
        last_kernel,
        [(32, 8, 128), (32, 8, 128), (4, 64, 128)],
        [
            from_right, from_left, mm, inv, u0, u1, v1, f1, u2, v2, f2, smod, sinv, sstate,
            owner, table, tablet,
        ],
        [(two, f32)] * 3
        + [((64, 128), f32), (one, f32), ((512, 128), f32), ((512, 512), jnp.bfloat16)],
    )
    sums = lax.all_to_all(sums, "sub", 0, 0)
    (kernel,) = call(project_kernel, [(64, 128)], [sums, spline_basis.T])
    return from_tiles(out_u), from_tiles(out_w), kernel


def solution(mesh):
    in_specs = (
        P(None, "dom", "sub"),
        P(None, "dom", "sub"),
        P(None, None, "dom", "sub"),
        P(None, "dom", "sub"),
        P("dom", "sub"),
        P(),
    )
    out_specs = (P(None, "dom", "sub"), P(None, "dom", "sub"), P(None, ("dom", "sub")))
    return jax.shard_map(
        on_device, mesh=mesh, in_specs=in_specs, out_specs=out_specs, check_vma=False
    )
```

```python
import jax
import jax.numpy as jnp
import numpy as np
from jax import lax
from jax.experimental import pallas as pl
from jax.experimental.pallas import tpu as pltpu
from jax.sharding import PartitionSpec as P

STEPS = 4
TIME_STEP = 0.1
KERNEL_SCALE = 0.05
PUSH = TIME_STEP * TIME_STEP

DERIVATIVE = np.array(
    [
        [-3.0, 4.04508497187474, -1.54508497187474, 0.5],
        [-0.80901699437495, 0.0, 1.11803398874989, -0.30901699437495],
        [0.30901699437495, -1.11803398874989, 0.0, 0.80901699437495],
        [-0.5, 1.54508497187474, -4.04508497187474, 3.0],
    ]
)
HALF_AMB = float((DERIVATIVE[0, 1] - DERIVATIVE[0, 2]) / 2)
HALF_CME = float((DERIVATIVE[1, 0] - DERIVATIVE[1, 3]) / 2)
HALF_D = float(DERIVATIVE[1, 2] / 2)

FAR, MFAR, MSG = 96, 104, 112
ZST, SFAR, SMFAR, MSG_S = 0, 8, 10, 12
MSG_B = 20
FIRST_LIMIT = 62


def strip_coefficients():
    tiles = []
    for d in (DERIVATIVE, DERIVATIVE.T):
        for out in range(2):
            for term in range(4):
                col = np.zeros(8)
                for s in range(8):
                    j = 2 * out + s // 4
                    half = s // 4 if term % 2 == 0 else 1 - s // 4
                    col[s] = d[j, 2 * (term // 2) + half]
                tiles.append(col)
        for delta in range(-3, 4):
            col = np.zeros(8)
            for s in range(8):
                k = s % 4
                if 0 <= k + delta < 4:
                    col[s] = d[k, k + delta]
            tiles.append(col)
    return np.broadcast_to(np.array(tiles, np.float32)[:, :, None], (30, 8, 128))


COEFFICIENTS = np.ascontiguousarray(strip_coefficients())


def sub_iota():
    return lax.broadcasted_iota(jnp.int32, (8, 128), 0)


def lane_iota(rows=8):
    return lax.broadcasted_iota(jnp.int32, (rows, 128), 1)


def rs(x, shift):
    return pltpu.roll(x, shift, 0)


def rl(x, shift):
    return pltpu.roll(x, shift, 1)


def masks():
    s = sub_iota()
    lane = lane_iota()
    return dict(
        even=(s % 2) == 0,
        lo=s < 4,
        ct0=((s // 2) % 2) == 0,
        first=lane == 0,
        last=lane == 127,
    )


def d_line(x0, x1, x2, x3):
    p, m, q, n = x0 + x3, x0 - x3, x1 + x2, x1 - x2
    r = q - p
    s1 = -1.75 * m + HALF_AMB * n
    s2 = HALF_CME * m - HALF_D * n
    r1, r2 = 1.25 * r, HALF_D * r
    return s1 + r1, s2 + r2, s2 - r2, s1 - r1


def dt_line(x0, x1, x2, x3):
    p, m, q, n = x0 + x3, x0 - x3, x1 + x2, x1 - x2
    t = 1.25 * m + HALF_D * n
    q1 = HALF_CME * q - 1.75 * p
    q2 = HALF_AMB * p - HALF_D * q
    return q1 - t, t + q2, t - q2, -(q1 + t)


def line_nodes(direction, a, b):
    if direction == 0:
        return [16 * i + 4 * a + b for i in range(4)]
    if direction == 1:
        return [16 * a + 4 * j + b for j in range(4)]
    return [16 * a + 4 * b + k for k in range(4)]


def expanded(x, upper, mk):
    r = rs(x, 4)
    return jnp.where(mk["lo"], r, x) if upper else jnp.where(mk["lo"], x, r)


def forces(u, f, mod, mk, planes=(0, 1, 2, 3), hook=None):
    for direction in (2, 1, 0):
        for a in range(4):
            if direction and a not in planes:
                continue
            for b in range(4):
                nodes = line_nodes(direction, a, b)
                g = d_line(*[u(n) for n in nodes])
                if hook is not None:
                    for n, gn in zip(nodes, g):
                        hook(direction, n, gn)
                t = []
                for n, gn in zip(nodes, g):
                    at = 64 * direction + n
                    t.append(expanded(mod(at // 2), at % 2, mk) * gn)
                for n, o in zip(nodes, dt_line(*t)):
                    if n // 16 in planes:
                        f(n, o, direction == 2)


def into(ref, h):
    def put(n, value, first):
        ref[h, n] = value if first else ref[h, n] + value

    return put


def far_pack(f, mk):
    left, right = [], []
    for p in range(8):
        left.append(jnp.where(mk["even"], rs(f(2 * p), 7), f(2 * p + 1)))
        right.append(jnp.where(mk["even"], f(48 + 2 * p), rs(f(48 + 2 * p + 1), 1)))
    return left, right


def along_x(f, far, h, i, q, mk):
    even = mk["even"]
    x = f(h, 16 * i + q)
    if i in (1, 2):
        return x
    other = 3 - i
    if h == 0:
        inside, beside = f(0, 16 * other + q), f(1, 16 * other + q)
        if i == 3:
            return x + jnp.where(even, rs(inside, 7), rs(beside, 1))
        return x + jnp.where(even, rs(beside, 7), rs(inside, 1))
    near = f(0, 16 * other + q)
    if i == 3:
        beyond = far[0][far[2] + q // 2]
        beyond = rs(beyond, 7) if q % 2 else beyond
        return x + jnp.where(even, beyond, rs(near, 1))
    beyond = far[1][far[2] + q // 2]
    beyond = beyond if q % 2 else rs(beyond, 1)
    return x + jnp.where(even, rs(near, 7), beyond)


def assembled(f, far, strip, h, i, k, mk):
    vals = [along_x(f, far, h, i, 4 * j + k, mk) for j in range(4)]
    shift = 4 if h else 68

    def inject(row):
        return pltpu.roll(
            jnp.broadcast_to(strip[row : row + 1, :], (8, 128)), shift, 1, stride=8, stride_axis=0
        )

    b, a = vals[0], vals[3]
    up, down = rl(b, 127), rl(a, 1)
    up = jnp.where(mk["last"], jnp.where(mk["ct0"], rs(up, 6), inject(16 * i + k)), up)
    down = jnp.where(mk["first"], jnp.where(mk["ct0"], inject(16 * i + 12 + k), rs(down, 2)), down)
    return [b + down, vals[1], vals[2], a + up]


def update(f, far, strip, h, mk, inv, u, v, put):
    for i in range(4):
        for k in range(4):
            for j, total in enumerate(assembled(f, far, strip, h, i, k, mk)):
                n = 16 * i + 4 * j + k
                vel = -inv(n) * total if v is None else v(n) - inv(n) * total
                put(n, u(n) + vel, vel)


def strip_lines(x, cf, base):
    along_j, along_k = [], []
    for i in range(4):
        a, b = x[2 * i], x[2 * i + 1]
        terms = (a, rs(a, 4), b, rs(b, 4))
        for out in range(2):
            along_j.append(sum(cf[base + 4 * out + t] * terms[t] for t in range(4)))
    for v in range(8):
        along_k.append(
            sum(cf[base + 8 + d] * (rs(x[v], (3 - d) % 8) if d != 3 else x[v]) for d in range(7))
        )
    return along_j, along_k


def strip_forces(us, mods, cf):
    x = [us[8 * v : 8 * v + 8] for v in range(8)]
    gj, gk = strip_lines(x, cf, 0)
    gi = [None] * 8
    for e in range(2):
        for i, g in enumerate(d_line(*[x[2 * m + e] for m in range(4)])):
            gi[2 * i + e] = g
    ti, tj, tk = (
        [mods[64 * d + 8 * v : 64 * d + 8 * v + 8] * g[v] for v in range(8)]
        for d, g in enumerate((gi, gj, gk))
    )
    fj = strip_lines(tj, cf, 15)[0]
    fk = strip_lines(tk, cf, 15)[1]
    f = [fj[v] + fk[v] for v in range(8)]
    for e in range(2):
        for i, o in enumerate(dt_line(*[ti[2 * m + e] for m in range(4)])):
            f[2 * i + e] = f[2 * i + e] + o
    return jnp.concatenate(f, axis=0)


def strip_x(f, far_right, far_left):
    lane = lane_iota(16)
    even, own = ((lane // 8) % 2) == 1, lane < 64
    b, a = f[0:16], f[48:64]
    na = a + jnp.where(even, jnp.where(own, rl(b, 8), rl(far_right, 72)), rl(b, 56))
    nb = b + jnp.where(even, rl(a, 72), jnp.where(own, rl(a, 120), rl(far_left, 56)))
    return jnp.concatenate([nb, f[16:48], na], axis=0)


def strip_y(f):
    low = sub_iota() < 4
    parts = []
    for i in range(4):
        x, y = f[16 * i : 16 * i + 8], f[16 * i + 8 : 16 * i + 16]
        parts.append(x + jnp.where(low, rs(rl(y, 1), 4), 0.0))
        parts.append(y + jnp.where(low, 0.0, rs(rl(x, 127), 4)))
    return jnp.concatenate(parts, axis=0)


def inverse_mass(m):
    return jnp.where(m > 0.5, PUSH / jnp.where(m > 0.5, m, 1.0), 0.0)


def strip_arrays(z1o, z2o, z1s, z2s):
    q = lane_iota(64) // 32

    def four(a, b, c, d):
        return jnp.where(q < 2, jnp.where(q == 0, a, b), jnp.where(q == 2, c, d))

    us = jnp.where(q < 2, z1o, rl(z1s, 64))
    m0 = four(rl(z1o, 64), rl(z1o, 96), z1s, rl(z1s, 32))
    m1 = four(rl(z1o, 32), rl(z1o, 64), rl(z1s, 96), z1s)
    m2 = four(z2o, rl(z2o, 32), rl(z2s, 64), rl(z2s, 96))
    mass = four(rl(z2o, 96), z2o, rl(z2s, 32), rl(z2s, 64))
    return us, jnp.concatenate([m0, m1, m2], axis=0), mass


def state_expand(xu, xw, mk):
    return jnp.where(mk["lo"], xu, rs(xw, 4)), jnp.where(mk["lo"], rs(xu, 4), xw)


def tile(ref, p):
    return ref[8 * p : 8 * p + 8, :]


def first_kernel(
    u_hbm, w_hbm, mod_hbm, mass_hbm, z_ref, state_ref, f_ref, left_ref, right_ref,
    u_ref, w_ref, m_ref, mass_ref, sems,
):
    copies = [
        pltpu.make_async_copy(src, dst, sems.at[i])
        for i, (src, dst) in enumerate(
            ((u_hbm, u_ref), (w_hbm, w_ref), (mod_hbm, m_ref), (mass_hbm, mass_ref))
        )
    ]
    for c in copies:
        c.start()
    for c in copies:
        c.wait()
    mk = masks()
    even = mk["even"]
    lane = lane_iota(64)
    pieces = (
        (w_ref, 0, 0, 0),
        (u_ref, 0, 0, 1),
        (m_ref, 0, 0, 2),
        (m_ref, 256, 0, 3),
        (m_ref, 512, 1, 0),
        (mass_ref, 0, 1, 1),
    )
    z = [jnp.zeros((64, 128), jnp.float32), jnp.zeros((64, 128), jnp.float32)]
    for ref, base, half, slot in pieces:
        for side in range(2):
            for r in range(2):
                rows = ref[pl.ds(base + 2 * (1 - side) + r, 64, stride=4), :]
                dest = slot * 32 + (1 - side) * 16 + (1 - r) * 8 + (3 if side else 1)
                src = 0 if side else 124
                moved = rl(rows, (dest - src) % 128)
                z[half] = jnp.where((lane >= dest) & (lane < dest + 4), moved, z[half])
    z_ref[0] = z[0]
    z_ref[1] = z[1]
    base = 0
    for ref in (u_ref, w_ref, m_ref, mass_ref):
        count = ref.shape[0] // 16
        for p in range(count):
            x, y = tile(ref, 2 * p), tile(ref, 2 * p + 1)
            left_ref[base + p] = jnp.where(even, x, rs(y, 1))
            right_ref[base + p] = jnp.where(even, rs(x, 7), y)
        base += count
    for p in range(32):
        a, b = state_expand(tile(u_ref, p), tile(w_ref, p), mk)
        state_ref[0, 2 * p] = a
        state_ref[0, 2 * p + 1] = b
    forces(lambda n: state_ref[0, n], into(f_ref, 0), lambda p: tile(m_ref, p), mk)
    packs = (
        (FAR, far_pack(lambda n: f_ref[0, n], mk)),
        (MFAR, far_pack(lambda n: expanded(tile(mass_ref, n // 2), n % 2, mk), mk)),
    )
    for at, (left, right) in packs:
        for p in range(8):
            left_ref[at + p] = left[p]
            right_ref[at + p] = right[p]


def strip_kernel(sub_ref, z_ref, cf_ref, left_ref, right_ref, zo_ref):
    sub = sub_ref[0]
    lane = lane_iota(64)
    side0 = ((lane // 16) % 2) == 1
    c = lane % 8
    below, above = jnp.maximum(sub - 1, 0), jnp.minimum(sub + 1, 3)
    zs = []
    for half in range(2):
        own = z_ref[sub, half]
        zl = jnp.where(sub > 0, z_ref[below, half], 0.0)
        zr = jnp.where(sub < 3, z_ref[above, half], 0.0)
        low = jnp.where(c == 0, 0.0, jnp.where(c <= 4, zl, rl(own, 18)))
        high = jnp.where(c <= 2, rl(own, 110), jnp.where(c == 7, 0.0, zr))
        z = jnp.where(side0, low, high)
        zo_ref[half] = z
        zs.append(z)
    zero = jnp.zeros((64, 128), jnp.float32)
    us, mods, mass = strip_arrays(zs[0], zs[1], zero, zero)
    fs = strip_forces(us, mods, cf_ref)
    evg = ((lane // 8) % 2) == 0
    wl = jnp.where(evg, rl(zs[1], 120), zs[0])
    wr = jnp.where(evg, zs[0], rl(zs[1], 8))
    for p in range(8):
        left_ref[ZST + p] = wl[8 * p : 8 * p + 8]
        right_ref[ZST + p] = wr[8 * p : 8 * p + 8]
    for p in range(2):
        left_ref[SFAR + p] = fs[8 * p : 8 * p + 8]
        right_ref[SFAR + p] = fs[48 + 8 * p : 56 + 8 * p]
        left_ref[SMFAR + p] = mass[8 * p : 8 * p + 8]
        right_ref[SMFAR + p] = mass[48 + 8 * p : 56 + 8 * p]


def rows16(ref, at):
    return jnp.concatenate([ref[at], ref[at + 1]], axis=0)


def shadow_kernel(
    mod_ref, mass_ref, mr_ref, ml_ref, order_ref, mm_ref, us_ref, mass2_ref, f_ref
):
    mk = masks()
    even = mk["even"]

    def shadow(p):
        r, l = mr_ref[p], ml_ref[p]
        return jnp.where(even, r, rs(l, 1)), jnp.where(even, rs(r, 7), l)

    for p in range(16):
        su, sw = shadow(p), shadow(16 + p)
        for e in range(2):
            us_ref[0, 4 * p + 2 * e], us_ref[0, 4 * p + 2 * e + 1] = state_expand(su[e], sw[e], mk)
    for p in range(48):
        mm_ref[1, 2 * p], mm_ref[1, 2 * p + 1] = shadow(32 + p)
    for p in range(96):
        mm_ref[0, p] = mod_ref[p]
    for p in range(16):
        sm = shadow(80 + p)
        for e in range(2):
            for o in range(2):
                mass2_ref[1, 4 * p + 2 * e + o] = expanded(sm[e], o, mk)
    for p in range(32):
        for o in range(2):
            mass2_ref[0, 2 * p + o] = expanded(mass_ref[p], o, mk)
    forces(lambda n: us_ref[0, n], into(f_ref, 0), lambda p: mm_ref[1, p], mk)


def middle_kernel(
    mm_ref, mass2_ref, u0_ref, us0_ref, f0_ref, f0s_ref, mr_ref, ml_ref, zo_ref, sr_ref, sl_ref,
    cf_ref,
    bl_ref, br_ref, inv_ref, u1_ref, v1_ref, f1_ref, u2_ref, v2_ref, f2_ref,
    smod_ref, sinv_ref, sstate_ref, sx,
):
    mk = masks()
    wr = jnp.concatenate([sr_ref[ZST + p] for p in range(8)], axis=0)
    wl = jnp.concatenate([sl_ref[ZST + p] for p in range(8)], axis=0)
    evg = ((lane_iota(64) // 8) % 2) == 0
    z1s = jnp.where(evg, wl, wr)
    z2s = jnp.where(evg, rl(wl, 120), rl(wr, 8))
    us, mods, smass = strip_arrays(zo_ref[0], zo_ref[1], z1s, z2s)
    smod_ref[...] = mods
    smass = strip_x(smass, rows16(sr_ref, SMFAR), rows16(sl_ref, SMFAR))
    sx[0] = smass
    sinv = inverse_mass(strip_y(smass))
    sinv_ref[...] = sinv
    for h in range(2):
        for i in range(4):
            for k in range(4):
                line = assembled(
                    lambda hh, n: mass2_ref[hh, n], (mr_ref, ml_ref, MFAR), sx.at[0], h, i, k, mk
                )
                for j, total in enumerate(line):
                    inv_ref[h, 16 * i + 4 * j + k] = inverse_mass(total)
    fs = strip_forces(us, mods, cf_ref)
    fs = strip_x(fs, rows16(sr_ref, SFAR), rows16(sl_ref, SFAR))
    sx[1] = fs
    svel = -sinv * strip_y(fs)
    us = us + svel

    def first_forces(h, n):
        return f0s_ref[0, n] if h else f0_ref[0, n]

    for h in range(2):

        def put(n, disp, vel):
            u1_ref[h, n] = disp
            v1_ref[h, n] = vel

        update(
            first_forces, (mr_ref, ml_ref, FAR), sx.at[1], h, mk, lambda n: inv_ref[h, n],
            lambda n: us0_ref[0, n] if h else u0_ref[0, n], None, put,
        )

    def both(h, carry):
        forces(lambda n: u1_ref[h, n], into(f1_ref, h), lambda p: mm_ref[h, p], mk)
        return carry

    lax.fori_loop(0, 2, both, 0)
    fs = strip_forces(us, mods, cf_ref)
    sstate_ref[0] = us
    sstate_ref[1] = svel
    sstate_ref[2] = fs
    left, right = far_pack(lambda n: f1_ref[0, n], mk)
    for p in range(8):
        bl_ref[p] = left[p]
        br_ref[p] = right[p]
    for p in range(2):
        bl_ref[16 + p] = fs[8 * p : 8 * p + 8]
        br_ref[16 + p] = fs[48 + 8 * p : 56 + 8 * p]
    zero = jnp.zeros((16, 128), jnp.float32)
    fs = strip_x(fs, zero, zero)
    sx[2] = fs
    svel = svel - sinv * strip_y(fs)
    us = us + svel

    def put2(n, disp, vel):
        u2_ref[0, n] = disp
        v2_ref[0, n] = vel

    update(
        lambda h, n: f1_ref[h, n], None, sx.at[2], 0, mk, lambda n: inv_ref[0, n],
        lambda n: u1_ref[0, n], lambda n: v1_ref[0, n], put2,
    )
    forces(lambda n: u2_ref[0, n], into(f2_ref, 0), lambda p: mm_ref[0, p], mk)
    fs = strip_forces(us, mods, cf_ref)
    left, right = far_pack(lambda n: f2_ref[0, n], mk)
    for p in range(8):
        bl_ref[8 + p] = left[p]
        br_ref[8 + p] = right[p]
    for p in range(2):
        bl_ref[18 + p] = fs[8 * p : 8 * p + 8]
        br_ref[18 + p] = fs[48 + 8 * p : 56 + 8 * p]


def density_kernel(mm_ref, u0_ref, u1_ref, u2_ref, owner_ref, d2_ref, x0_ref, x1_ref, hot_ref):
    mk = masks()
    lo = mk["lo"]
    for direction in (2, 1, 0):
        for a in range(4):
            for b in range(4):
                nodes = line_nodes(direction, a, b)
                g0 = d_line(*[u0_ref[0, n] for n in nodes])
                g1 = d_line(*[u1_ref[0, n] for n in nodes])
                g2 = d_line(*[u2_ref[0, n] for n in nodes])
                for e, n in enumerate(nodes):
                    at = 64 * direction + n
                    m = expanded(mm_ref[0, at // 2], at % 2, mk)
                    x0_ref[at] = jnp.where(lo, m * rs(g0[e], 4), 0.0)
                    x1_ref[at] = m * rs(g1[e], 4)
                    t = jnp.where(lo, m * g2[e] * rs(g2[e], 4), 0.0)
                    d2_ref[n] = t if direction == 2 else d2_ref[n] + t
    block = lax.broadcasted_iota(jnp.int32, (512, 128), 0)
    for s in range(4):
        owner = jnp.broadcast_to(owner_ref[s : s + 1, :], (512, 128))
        hot_ref[:, 128 * s : 128 * s + 128] = (
            (block == owner).astype(jnp.float32).astype(jnp.bfloat16)
        )


def three_way(x):
    hi = x.astype(jnp.bfloat16)
    rest = x - hi.astype(jnp.float32)
    mid = rest.astype(jnp.bfloat16)
    return hi, mid, (rest - mid.astype(jnp.float32)).astype(jnp.bfloat16)


def last_kernel(
    br_ref, bl_ref, mm_ref, inv_ref, u1_ref, v1_ref, f1_ref, u2_ref, v2_ref, f2_ref,
    smod_ref, sinv_ref, sstate_ref, d2_ref, x0_ref, x1_ref, hot_ref, cf_ref,
    out_u_ref, out_w_ref, sums_ref,
    u, v, f, sx, dens,
):
    mk = masks()
    lo = mk["lo"]
    mods, sinv = smod_ref[...], sinv_ref[...]
    us, svel, fs = sstate_ref[0], sstate_ref[1], sstate_ref[2]

    def put(h):
        def store(n, disp, vel):
            u[h, n] = disp
            v[h, n] = vel

        return store

    fs = strip_x(fs, rows16(br_ref, 16), rows16(bl_ref, 16))
    sx[0] = fs
    svel = svel - sinv * strip_y(fs)
    us = us + svel
    update(
        lambda h, n: f1_ref[h, n], (br_ref, bl_ref, 0), sx.at[0], 1, mk, lambda n: inv_ref[1, n],
        lambda n: u1_ref[1, n], lambda n: v1_ref[1, n], put(1),
    )
    forces(lambda n: u[1, n], into(f, 1), lambda p: mm_ref[1, p], mk)
    fs = strip_forces(us, mods, cf_ref)
    fs = strip_x(fs, rows16(br_ref, 18), rows16(bl_ref, 18))
    sx[1] = fs
    svel = svel - sinv * strip_y(fs)
    us = us + svel

    def step_two(h, n):
        return f[1, n] if h else f2_ref[0, n]

    far = (br_ref, bl_ref, 8)
    update(
        step_two, far, sx.at[1], 0, mk, lambda n: inv_ref[0, n],
        lambda n: u2_ref[0, n], lambda n: v2_ref[0, n], put(0),
    )
    update(
        step_two, far, sx.at[1], 1, mk, lambda n: inv_ref[1, n],
        lambda n: u[1, n], lambda n: v[1, n], put(1),
    )

    def add_third(direction, n, g):
        at = pl.ds(8 * n, 8)
        before = d2_ref[n] if direction == 2 else dens[at, :]
        dens[at, :] = before + x1_ref[64 * direction + n] * g

    forces(lambda n: u[1, n], into(f, 1), lambda p: mm_ref[1, p], mk, planes=(0, 3))
    forces(lambda n: u[0, n], into(f, 0), lambda p: mm_ref[0, p], mk, hook=add_third)
    fs = strip_forces(us, mods, cf_ref)
    zero = jnp.zeros((16, 128), jnp.float32)
    sx[2] = strip_x(fs, zero, zero)
    update(
        lambda h, n: f[h, n], None, sx.at[2], 0, mk, lambda n: inv_ref[0, n],
        lambda n: u[0, n], lambda n: v[0, n], put(0),
    )
    for direction in (2, 1, 0):
        for a in range(4):
            for b in range(4):
                nodes = line_nodes(direction, a, b)
                for n, g in zip(nodes, d_line(*[u[0, n] for n in nodes])):
                    at = pl.ds(8 * n, 8)
                    dens[at, :] = dens[at, :] + x0_ref[64 * direction + n] * g
    cols = [
        dens[pl.ds(s, 64, stride=8), :] + dens[pl.ds(s + 4, 64, stride=8), :] for s in range(4)
    ]
    split = jnp.concatenate(three_way(jnp.concatenate(cols, axis=1)), axis=0)
    res = lax.dot_general(
        split, hot_ref[...], (((1,), (1,)), ((), ())), preferred_element_type=jnp.float32
    )
    sums = res[0:64] + (res[64:128] + res[128:192])
    for q in range(4):
        sums_ref[q] = sums[:, 128 * q : 128 * q + 128]
    for p in range(32):
        a, b = u[0, 2 * p], u[0, 2 * p + 1]
        out_u_ref[p] = jnp.where(lo, a, rs(b, 4))
        out_w_ref[p] = jnp.where(lo, rs(a, 4), b)


def project_kernel(x_ref, basis_ref, out_ref):
    total = (x_ref[0] + x_ref[1]) + (x_ref[2] + x_ref[3])
    t0, t1, t2 = three_way(total)
    b0, b1, b2 = three_way(basis_ref[...])
    out_ref[...] = KERNEL_SCALE * jnp.dot(
        jnp.concatenate([b0, b1, b0, b1, b0, b2], axis=1),
        jnp.concatenate([t0, t0, t1, t1, t2, t0], axis=0),
        preferred_element_type=jnp.float32,
    )


VMEM = pl.BlockSpec(memory_space=pltpu.VMEM)
SMEM = pl.BlockSpec(memory_space=pltpu.SMEM)
HBM = pl.BlockSpec(memory_space=pltpu.HBM)
F32, BF16 = jnp.float32, jnp.bfloat16


def call(kernel, outs, ins, scratch=(), specs=(), limit=24):
    specs = list(specs) + [VMEM] * (len(ins) - len(specs))
    outs = [o if isinstance(o, jax.ShapeDtypeStruct) else jax.ShapeDtypeStruct(o, F32) for o in outs]
    return pl.pallas_call(
        kernel,
        out_shape=outs,
        in_specs=specs,
        out_specs=[VMEM] * len(outs),
        scratch_shapes=list(scratch),
        compiler_params=pltpu.CompilerParams(vmem_limit_bytes=limit * 1024 * 1024),
    )(*ins)


def raw_tiles(x):
    lead = int(np.prod(x.shape[:-2]))
    return x.reshape(lead, 2, 2, 128).transpose(0, 2, 1, 3).reshape(lead * 4, 128)


def from_tiles(x):
    return x.reshape(64, 2, 2, 128).transpose(0, 2, 1, 3).reshape(64, 2, 256)


def on_device(initial_field, adjoint_source, moduli, node_mass, block_owner, spline_basis):
    count = lax.axis_size("dom")
    to_right = [(i, i + 1) for i in range(count - 1)]
    to_left = [(b, a) for a, b in to_right]
    cf = jnp.asarray(COEFFICIENTS)
    sub = lax.axis_index("sub").astype(jnp.int32).reshape(1)
    u2d, w2d, m2d, mass2d = map(raw_tiles, (initial_field, adjoint_source, moduli, node_mass))
    owner = raw_tiles(block_owner[None])
    mass = mass2d.reshape(32, 8, 128)
    mod = m2d.reshape(96, 8, 128)
    one, two = (1, 64, 8, 128), (2, 64, 8, 128)

    def swap_rows(left, right):
        return lax.ppermute(left, "dom", to_left), lax.ppermute(right, "dom", to_right)

    edges, u0, f0, left, right = call(
        first_kernel,
        [(2, 64, 128), one, one, (MSG, 8, 128), (MSG, 8, 128)],
        [u2d, w2d, m2d, mass2d],
        [pltpu.VMEM((n, 128), F32) for n in (256, 256, 768, 256)] + [pltpu.SemaphoreType.DMA((4,))],
        [HBM] * 4,
        limit=FIRST_LIMIT,
    )
    raw_right, raw_left = swap_rows(left, right)
    edges = lax.all_gather(edges, "sub")
    left, right, zo = call(
        strip_kernel,
        [(MSG_S, 8, 128), (MSG_S, 8, 128), (2, 64, 128)],
        [sub, edges, cf],
        specs=[SMEM],
    )
    strip_right, strip_left = swap_rows(left, right)
    mm, us0, mass2, f0s = call(
        shadow_kernel,
        [(2, 96, 8, 128), one, two, one],
        [mod, mass, raw_right, raw_left, zo],
        specs=[VMEM] * 4 + [pl.BlockSpec(memory_space=pl.ANY)],
    )
    bl, br, inv, u1, v1, f1, u2, v2, f2, smod, sinv, sstate = call(
        middle_kernel,
        [
            (MSG_B, 8, 128), (MSG_B, 8, 128), two, two, two, two, one, one, one,
            (192, 128), (64, 128), (3, 64, 128),
        ],
        [mm, mass2, u0, us0, f0, f0s, raw_right, raw_left, zo, strip_right, strip_left, cf],
        [pltpu.VMEM((3, 64, 128), F32)],
    )
    far_right, far_left = swap_rows(bl, br)
    d2, x0, x1, hot = call(
        density_kernel,
        [(64, 8, 128), (192, 8, 128), (192, 8, 128), jax.ShapeDtypeStruct((512, 512), BF16)],
        [mm, u0, u1, u2, owner],
    )
    out_u, out_w, sums = call(
        last_kernel,
        [(32, 8, 128), (32, 8, 128), (4, 64, 128)],
        [
            far_right, far_left, mm, inv, u1, v1, f1, u2, v2, f2, smod, sinv, sstate,
            d2, x0, x1, hot, cf,
        ],
        [pltpu.VMEM(two, F32)] * 3 + [pltpu.VMEM((3, 64, 128), F32), pltpu.VMEM((512, 128), F32)],
    )
    sums = lax.all_to_all(sums, "sub", 0, 0)
    (kernel,) = call(project_kernel, [(64, 128)], [sums, spline_basis.T])
    return from_tiles(out_u), from_tiles(out_w), kernel


def solution(mesh):
    in_specs = (
        P(None, "dom", "sub"),
        P(None, "dom", "sub"),
        P(None, None, "dom", "sub"),
        P(None, "dom", "sub"),
        P("dom", "sub"),
        P(),
    )
    out_specs = (P(None, "dom", "sub"), P(None, "dom", "sub"), P(None, ("dom", "sub")))
    return jax.shard_map(
        on_device, mesh=mesh, in_specs=in_specs, out_specs=out_specs, check_vma=False
    )
```

```python
import jax
import jax.numpy as jnp
import numpy as np
from jax import lax
from jax.experimental import pallas as pl
from jax.experimental.pallas import tpu as pltpu
from jax.sharding import PartitionSpec as P

STEPS = 4
TIME_STEP = 0.1
KERNEL_SCALE = 0.05
PUSH = TIME_STEP * TIME_STEP

DERIVATIVE = np.array(
    [
        [-3.0, 4.04508497187474, -1.54508497187474, 0.5],
        [-0.80901699437495, 0.0, 1.11803398874989, -0.30901699437495],
        [0.30901699437495, -1.11803398874989, 0.0, 0.80901699437495],
        [-0.5, 1.54508497187474, -4.04508497187474, 3.0],
    ]
)
HALF_AMB = float((DERIVATIVE[0, 1] - DERIVATIVE[0, 2]) / 2)
HALF_CME = float((DERIVATIVE[1, 0] - DERIVATIVE[1, 3]) / 2)
HALF_D = float(DERIVATIVE[1, 2] / 2)

MSG, CONST, STRIP = 38, 16, 32
MSG_B, STRIP_B = 18, 16
FIRST_LIMIT = 62


def strip_coefficients():
    tiles = []
    for d in (DERIVATIVE, DERIVATIVE.T):
        for out in range(2):
            for term in range(4):
                col = np.zeros(8)
                for s in range(8):
                    j = 2 * out + s // 4
                    half = s // 4 if term % 2 == 0 else 1 - s // 4
                    col[s] = d[j, 2 * (term // 2) + half]
                tiles.append(col)
        for delta in range(-3, 4):
            col = np.zeros(8)
            for s in range(8):
                k = s % 4
                if 0 <= k + delta < 4:
                    col[s] = d[k, k + delta]
            tiles.append(col)
    return np.broadcast_to(np.array(tiles, np.float32)[:, :, None], (30, 8, 128))


COEFFICIENTS = np.ascontiguousarray(strip_coefficients())


def sub_iota():
    return lax.broadcasted_iota(jnp.int32, (8, 128), 0)


def lane_iota(rows=8):
    return lax.broadcasted_iota(jnp.int32, (rows, 128), 1)


def rs(x, shift):
    return pltpu.roll(x, shift, 0)


def rl(x, shift):
    return pltpu.roll(x, shift, 1)


def masks():
    s = sub_iota()
    lane = lane_iota()
    return dict(
        even=(s % 2) == 0,
        lo=s < 4,
        ct0=((s // 2) % 2) == 0,
        first=lane == 0,
        last=lane == 127,
    )


def d_line(x0, x1, x2, x3):
    p, m, q, n = x0 + x3, x0 - x3, x1 + x2, x1 - x2
    r = q - p
    s1 = -1.75 * m + HALF_AMB * n
    s2 = HALF_CME * m - HALF_D * n
    r1, r2 = 1.25 * r, HALF_D * r
    return s1 + r1, s2 + r2, s2 - r2, s1 - r1


def dt_line(x0, x1, x2, x3):
    p, m, q, n = x0 + x3, x0 - x3, x1 + x2, x1 - x2
    t = 1.25 * m + HALF_D * n
    q1 = HALF_CME * q - 1.75 * p
    q2 = HALF_AMB * p - HALF_D * q
    return q1 - t, t + q2, t - q2, -(q1 + t)


def line_nodes(direction, a, b):
    if direction == 0:
        return [16 * i + 4 * a + b for i in range(4)]
    if direction == 1:
        return [16 * a + 4 * j + b for j in range(4)]
    return [16 * a + 4 * b + k for k in range(4)]


def expanded(x, upper, mk):
    r = rs(x, 4)
    return jnp.where(mk["lo"], r, x) if upper else jnp.where(mk["lo"], x, r)


def forces(u, f, mod, mk, planes=(0, 1, 2, 3), hook=None):
    for direction in (2, 1, 0):
        for a in range(4):
            if direction and a not in planes:
                continue
            for b in range(4):
                nodes = line_nodes(direction, a, b)
                g = d_line(*[u(n) for n in nodes])
                if hook is not None:
                    for n, gn in zip(nodes, g):
                        hook(direction, n, gn)
                t = []
                for n, gn in zip(nodes, g):
                    at = 64 * direction + n
                    t.append(expanded(mod(at // 2), at % 2, mk) * gn)
                for n, o in zip(nodes, dt_line(*t)):
                    if n // 16 in planes:
                        f(n, o, direction == 2)


def into(ref):
    def put(n, value, first):
        ref[n] = value if first else ref[n] + value

    return put


def face_tile(get, q, mk):
    return jnp.where(mk["even"], get(q), get(48 + q))


def pack_faces(left_ref, right_ref, base, get, mk):
    even = mk["even"]
    for p in range(8):
        x, y = get(2 * p), get(2 * p + 1)
        left_ref[base + p] = jnp.where(even, x, rs(y, 1))
        right_ref[base + p] = jnp.where(even, rs(x, 7), y)


def unpack_face(from_right, from_left, base, q, mk):
    r, l = from_right[base + q // 2], from_left[base + q // 2]
    if q % 2:
        return jnp.where(mk["even"], rs(l, 7), r)
    return jnp.where(mk["even"], l, rs(r, 1))


def face_response(delta, diagonal, mod_j, mod_k):
    out = [diagonal(q) * delta[q] for q in range(16)]
    for mod, lines in (
        (mod_j, [[4 * j + k for j in range(4)] for k in range(4)]),
        (mod_k, [[4 * j + k for k in range(4)] for j in range(4)]),
    ):
        for line in lines:
            t = [mod(q) * g for q, g in zip(line, d_line(*[delta[q] for q in line]))]
            for q, o in zip(line, dt_line(*t)):
                out[q] = out[q] + o
    return out


def along_x(f, beside, i, q, mk):
    even = mk["even"]
    x = f(16 * i + q)
    if i in (1, 2):
        return x
    other = beside(q) if beside is not None else 0.0
    if i == 3:
        return x + jnp.where(even, rs(f(q), 7), other)
    return x + jnp.where(even, other, rs(f(48 + q), 1))


def assembled(f, beside, strip, i, k, mk):
    vals = [along_x(f, beside, i, 4 * j + k, mk) for j in range(4)]

    def inject(row):
        return pltpu.roll(
            jnp.broadcast_to(strip[row : row + 1, :], (8, 128)), 68, 1, stride=8, stride_axis=0
        )

    b, a = vals[0], vals[3]
    up, down = rl(b, 127), rl(a, 1)
    up = jnp.where(mk["last"], jnp.where(mk["ct0"], rs(up, 6), inject(16 * i + k)), up)
    down = jnp.where(mk["first"], jnp.where(mk["ct0"], inject(16 * i + 12 + k), rs(down, 2)), down)
    return [b + down, vals[1], vals[2], a + up]


def assemble(f, beside, strip, mk, put, planes=(0, 1, 2, 3)):
    for i in planes:
        for k in range(4):
            for j, total in enumerate(assembled(f, beside, strip, i, k, mk)):
                put(16 * i + 4 * j + k, total)


def not_shared(n, x, mk):
    if n < 16:
        return jnp.where(mk["even"], 0.0, x)
    if n >= 48:
        return jnp.where(mk["even"], x, 0.0)
    return x


def strip_lines(x, cf, base):
    along_j, along_k = [], []
    for i in range(len(x) // 2):
        a, b = x[2 * i], x[2 * i + 1]
        terms = (a, rs(a, 4), b, rs(b, 4))
        for out in range(2):
            along_j.append(sum(cf[base + 4 * out + t] * terms[t] for t in range(4)))
    for y in x:
        along_k.append(
            sum(cf[base + 8 + d] * (rs(y, (3 - d) % 8) if d != 3 else y) for d in range(7))
        )
    return along_j, along_k


def strip_forces(us, mods, cf):
    x = [us[8 * v : 8 * v + 8] for v in range(8)]
    gj, gk = strip_lines(x, cf, 0)
    gi = [None] * 8
    for e in range(2):
        for i, g in enumerate(d_line(*[x[2 * m + e] for m in range(4)])):
            gi[2 * i + e] = g
    ti, tj, tk = (
        [mods[64 * d + 8 * v : 64 * d + 8 * v + 8] * g[v] for v in range(8)]
        for d, g in enumerate((gi, gj, gk))
    )
    fj = strip_lines(tj, cf, 15)[0]
    fk = strip_lines(tk, cf, 15)[1]
    f = [fj[v] + fk[v] for v in range(8)]
    for e in range(2):
        for i, o in enumerate(dt_line(*[ti[2 * m + e] for m in range(4)])):
            f[2 * i + e] = f[2 * i + e] + o
    return jnp.concatenate(f, axis=0)


def row_zero(rows):
    return ((lane_iota(rows) // 8) % 2) == 1


def strip_faces(f):
    return jnp.where(row_zero(16), f[0:16], f[48:64])


def strip_beside(from_right, from_left, base):
    r = jnp.concatenate([from_right[base], from_right[base + 1]], axis=0)
    l = jnp.concatenate([from_left[base], from_left[base + 1]], axis=0)
    both = jnp.where(row_zero(16), rl(l, 8), rl(r, 120))
    return both, rl(both, 64)


def strip_send(left_ref, right_ref, base, x, y):
    both = jnp.where(lane_iota(16) < 64, x, rl(y, 64))
    for p in range(2):
        left_ref[base + p] = both[8 * p : 8 * p + 8]
        right_ref[base + p] = both[8 * p : 8 * p + 8]


def strip_response(delta, diagonal, mod_j, mod_k, cf):
    x = [delta[0:8], delta[8:16]]
    gj, gk = strip_lines(x, cf, 0)
    fj = strip_lines([mod_j[8 * v : 8 * v + 8] * gj[v] for v in range(2)], cf, 15)[0]
    fk = strip_lines([mod_k[8 * v : 8 * v + 8] * gk[v] for v in range(2)], cf, 15)[1]
    return diagonal * delta + jnp.concatenate([fj[v] + fk[v] for v in range(2)], axis=0)


def strip_x(f, beside):
    zero = row_zero(16)
    b, a = f[0:16], f[48:64]
    na = a + jnp.where(zero, rl(b, 8), beside)
    nb = b + jnp.where(zero, beside, rl(a, 120))
    return jnp.concatenate([nb, f[16:48], na], axis=0)


def strip_y(f):
    low = sub_iota() < 4
    parts = []
    for i in range(4):
        x, y = f[16 * i : 16 * i + 8], f[16 * i + 8 : 16 * i + 16]
        parts.append(x + jnp.where(low, rs(rl(y, 1), 4), 0.0))
        parts.append(y + jnp.where(low, 0.0, rs(rl(x, 127), 4)))
    return jnp.concatenate(parts, axis=0)


def inverse_mass(m):
    return jnp.where(m > 0.5, PUSH / jnp.where(m > 0.5, m, 1.0), 0.0)


def strip_not_shared(x):
    zero = row_zero(16)
    return jnp.concatenate(
        [jnp.where(zero, 0.0, x[0:16]), x[16:48], jnp.where(zero, x[48:64], 0.0)], axis=0
    )


def strip_arrays(z1, z2):
    q = lane_iota(64) // 32

    def two(a, b):
        return jnp.where(q == 0, a, jnp.where(q == 1, b, 0.0))

    us = two(z1, z1)
    m0 = two(rl(z1, 64), rl(z1, 96))
    m1 = two(rl(z1, 32), rl(z1, 64))
    m2 = two(z2, rl(z2, 32))
    mass = two(rl(z2, 96), z2)
    return us, jnp.concatenate([m0, m1, m2], axis=0), mass


def state_expand(xu, xw, mk):
    return jnp.where(mk["lo"], xu, rs(xw, 4)), jnp.where(mk["lo"], rs(xu, 4), xw)


def tile(ref, p):
    return ref[8 * p : 8 * p + 8, :]


def first_kernel(
    u_hbm, w_hbm, mod_hbm, mass_hbm, z_ref, state_ref, f_ref, mass2_ref, const_ref,
    u_ref, w_ref, m_ref, mass_ref, sems,
):
    copies = [
        pltpu.make_async_copy(src, dst, sems.at[i])
        for i, (src, dst) in enumerate(
            ((u_hbm, u_ref), (w_hbm, w_ref), (mod_hbm, m_ref), (mass_hbm, mass_ref))
        )
    ]
    for c in copies:
        c.start()
    for c in copies:
        c.wait()
    mk = masks()
    lane = lane_iota(64)
    pieces = (
        (w_ref, 0, 0, 0),
        (u_ref, 0, 0, 1),
        (m_ref, 0, 0, 2),
        (m_ref, 256, 0, 3),
        (m_ref, 512, 1, 0),
        (mass_ref, 0, 1, 1),
    )
    z = [jnp.zeros((64, 128), jnp.float32), jnp.zeros((64, 128), jnp.float32)]
    for ref, base, half, slot in pieces:
        for side in range(2):
            for r in range(2):
                rows = ref[pl.ds(base + 2 * (1 - side) + r, 64, stride=4), :]
                dest = slot * 32 + (1 - side) * 16 + (1 - r) * 8 + (3 if side else 1)
                src = 0 if side else 124
                moved = rl(rows, (dest - src) % 128)
                z[half] = jnp.where((lane >= dest) & (lane < dest + 4), moved, z[half])
    z_ref[0] = z[0]
    z_ref[1] = z[1]
    for p in range(32):
        a, b = state_expand(tile(u_ref, p), tile(w_ref, p), mk)
        state_ref[2 * p] = a
        state_ref[2 * p + 1] = b
        mass2_ref[2 * p] = expanded(tile(mass_ref, p), 0, mk)
        mass2_ref[2 * p + 1] = expanded(tile(mass_ref, p), 1, mk)

    def moduli(direction):
        def get(n):
            at = 64 * direction + n
            return expanded(tile(m_ref, at // 2), at % 2, mk)

        return get

    for q in range(16):
        mi = [moduli(0)(16 * i + q) for i in range(4)]
        diagonal = [sum(float(DERIVATIVE[i, e] ** 2) * mi[i] for i in range(4)) for e in (0, 3)]
        diagonal = jnp.where(mk["even"], diagonal[0], diagonal[1])
        own_mass = face_tile(lambda n: mass2_ref[n], q, mk)
        const_ref[q] = jnp.where(mk["lo"], own_mass, diagonal)
        const_ref[16 + q] = jnp.where(
            mk["lo"], face_tile(moduli(1), q, mk), face_tile(moduli(2), q, mk)
        )
    forces(lambda n: state_ref[n], into(f_ref), lambda p: tile(m_ref, p), mk)


def open_kernel(
    sub_ref, z_ref, u0_ref, f0_ref, mass2_ref, const_ref, mod_ref, cf_ref,
    left_ref, right_ref, u1_ref, v1_ref, inv_ref, strip_ref, smod_ref,
    f, sx,
):
    mk = masks()
    sub = sub_ref[0]
    lane = lane_iota(64)
    side0 = ((lane // 16) % 2) == 1
    c = lane % 8
    below, above = jnp.maximum(sub - 1, 0), jnp.minimum(sub + 1, 3)
    zs = []
    for half in range(2):
        own = z_ref[sub, half]
        zl = jnp.where(sub > 0, z_ref[below, half], 0.0)
        zr = jnp.where(sub < 3, z_ref[above, half], 0.0)
        low = jnp.where(c == 0, 0.0, jnp.where(c <= 4, zl, rl(own, 18)))
        high = jnp.where(c <= 2, rl(own, 110), jnp.where(c == 7, 0.0, zr))
        zs.append(jnp.where(side0, low, high))
    us, mods, smass = strip_arrays(zs[0], zs[1])
    fs = strip_forces(us, mods, cf_ref)
    smod_ref[...] = mods
    strip_ref[0] = us
    strip_ref[1] = fs
    strip_ref[2] = smass
    zero = row_zero(16)
    diagonal = [
        sum(float(DERIVATIVE[i, e] ** 2) * mods[16 * i : 16 * i + 16] for i in range(4))
        for e in (0, 3)
    ]
    strip_send(
        left_ref, right_ref, STRIP + 2, strip_faces(smass), jnp.where(zero, *diagonal)
    )
    strip_send(
        left_ref, right_ref, STRIP + 4, strip_faces(mods[64:128]), strip_faces(mods[128:192])
    )
    sm = strip_x(smass, 0.0)
    sx[0] = sm
    fx = strip_x(fs, 0.0)
    sx[1] = fx
    sinv = strip_not_shared(inverse_mass(strip_y(sm)))
    partial = strip_forces(us - sinv * strip_y(fx), mods, cf_ref)
    strip_send(left_ref, right_ref, STRIP, strip_faces(fs), strip_faces(partial))

    def put_mass(n, total):
        inv_ref[n] = not_shared(n, inverse_mass(total), mk)

    assemble(lambda n: mass2_ref[n], None, sx.at[0], mk, put_mass)

    def put(n, total):
        vel = -inv_ref[n] * total
        v1_ref[n] = vel
        u1_ref[n] = u0_ref[n] + vel

    assemble(lambda n: f0_ref[n], None, sx.at[1], mk, put)
    forces(lambda n: u1_ref[n], into(f), lambda p: mod_ref[p], mk, planes=(0, 3))
    pack_faces(left_ref, right_ref, 0, lambda q: face_tile(lambda n: f0_ref[n], q, mk), mk)
    pack_faces(left_ref, right_ref, 8, lambda q: face_tile(lambda n: f[n], q, mk), mk)
    pack_faces(left_ref, right_ref, CONST, lambda q: const_ref[q], mk)
    pack_faces(left_ref, right_ref, CONST + 8, lambda q: const_ref[16 + q], mk)


def middle_kernel(
    mr_ref, ml_ref, u0_ref, f0_ref, mass2_ref, u1p_ref, v1p_ref, invp_ref, strip_ref, smod_ref,
    mod_ref, cf_ref,
    bl_ref, br_ref, inv_ref, u1_ref, u2_ref, v2_ref, f2_ref, u3_ref, v3_ref, resp_ref,
    sresp_ref, sstate_ref,
    v1, f, sx, beside,
):
    mk = masks()
    lo = mk["lo"]
    us, fs, smass = strip_ref[0], strip_ref[1], strip_ref[2]
    mods = smod_ref[...]
    sf0, sp1 = strip_beside(mr_ref, ml_ref, STRIP)
    smn, sresp0 = strip_beside(mr_ref, ml_ref, STRIP + 2)
    sresp1, sresp2 = strip_beside(mr_ref, ml_ref, STRIP + 4)
    sresp_ref[0] = sresp0
    sresp_ref[1] = sresp1
    sresp_ref[2] = sresp2
    for q in range(16):
        x = unpack_face(mr_ref, ml_ref, CONST, q, mk)
        r = rs(x, 4)
        beside[q] = jnp.where(lo, x, r)
        resp_ref[0, q] = jnp.where(lo, r, x)
        x = unpack_face(mr_ref, ml_ref, CONST + 8, q, mk)
        r = rs(x, 4)
        resp_ref[1, q] = jnp.where(lo, x, r)
        resp_ref[2, q] = jnp.where(lo, r, x)
    responses = [lambda q, d=d: resp_ref[d, q] for d in range(3)]
    sm = strip_x(smass, smn)
    sx[0] = sm
    sinv = inverse_mass(strip_y(sm))
    for n in range(16, 48):
        inv_ref[n] = invp_ref[n]
        u1_ref[n] = u1p_ref[n]
        v1[n] = v1p_ref[n]

    def put_mass(n, total):
        inv_ref[n] = inverse_mass(total)

    assemble(lambda n: mass2_ref[n], lambda q: beside[q], sx.at[0], mk, put_mass, (0, 3))
    fs = strip_x(fs, sf0)
    sx[1] = fs
    svel = -sinv * strip_y(fs)
    us = us + svel

    def put0(n, total):
        vel = -inv_ref[n] * total
        v1[n] = vel
        u1_ref[n] = u0_ref[n] + vel

    assemble(
        lambda n: f0_ref[n], lambda q: unpack_face(mr_ref, ml_ref, 0, q, mk), sx.at[1], mk, put0,
        (0, 3),
    )
    forces(lambda n: u1_ref[n], into(f), lambda p: mod_ref[p], mk)
    delta = [face_tile(lambda n: v1[n], q, mk) for q in range(16)]
    for q, x in enumerate(face_response(delta, *responses)):
        beside[q] = unpack_face(mr_ref, ml_ref, 8, q, mk) + x
    sbeside = sp1 + strip_response(strip_faces(svel), sresp0, sresp1, sresp2, cf_ref)
    fs = strip_x(strip_forces(us, mods, cf_ref), sbeside)
    sx[2] = fs
    svel = svel - sinv * strip_y(fs)
    us = us + svel

    def put1(n, total):
        vel = v1[n] - inv_ref[n] * total
        v2_ref[n] = vel
        u2_ref[n] = u1_ref[n] + vel

    assemble(lambda n: f[n], lambda q: beside[q], sx.at[2], mk, put1)
    forces(lambda n: u2_ref[n], into(f2_ref), lambda p: mod_ref[p], mk)
    fs = strip_forces(us, mods, cf_ref)
    sstate_ref[0] = us
    sstate_ref[1] = svel
    sstate_ref[2] = fs
    sstate_ref[3] = sinv
    fx = strip_x(fs, 0.0)
    sx[3] = fx
    partial = strip_forces(
        us + (svel - strip_not_shared(sinv) * strip_y(fx)), mods, cf_ref
    )

    def put2(n, total):
        vel = v2_ref[n] - not_shared(n, inv_ref[n], mk) * total
        v3_ref[n] = vel
        u3_ref[n] = u2_ref[n] + vel

    assemble(lambda n: f2_ref[n], None, sx.at[3], mk, put2)
    forces(lambda n: u3_ref[n], into(f), lambda p: mod_ref[p], mk, planes=(0, 3))
    pack_faces(bl_ref, br_ref, 0, lambda q: face_tile(lambda n: f2_ref[n], q, mk), mk)
    pack_faces(bl_ref, br_ref, 8, lambda q: face_tile(lambda n: f[n], q, mk), mk)
    strip_send(bl_ref, br_ref, STRIP_B, strip_faces(fs), strip_faces(partial))


def density_kernel(mod_ref, u0_ref, u1_ref, u2_ref, owner_ref, d2_ref, x0_ref, x1_ref, hot_ref):
    mk = masks()
    lo = mk["lo"]
    for direction in (2, 1, 0):
        for a in range(4):
            for b in range(4):
                nodes = line_nodes(direction, a, b)
                g0 = d_line(*[u0_ref[n] for n in nodes])
                g1 = d_line(*[u1_ref[n] for n in nodes])
                g2 = d_line(*[u2_ref[n] for n in nodes])
                for e, n in enumerate(nodes):
                    at = 64 * direction + n
                    m = expanded(mod_ref[at // 2], at % 2, mk)
                    x0_ref[at] = jnp.where(lo, m * rs(g0[e], 4), 0.0)
                    x1_ref[at] = m * rs(g1[e], 4)
                    t = jnp.where(lo, m * g2[e] * rs(g2[e], 4), 0.0)
                    d2_ref[n] = t if direction == 2 else d2_ref[n] + t
    block = lax.broadcasted_iota(jnp.int32, (512, 128), 0)
    for s in range(4):
        owner = jnp.broadcast_to(owner_ref[s : s + 1, :], (512, 128))
        hot_ref[:, 128 * s : 128 * s + 128] = (
            (block == owner).astype(jnp.float32).astype(jnp.bfloat16)
        )


def three_way(x):
    hi = x.astype(jnp.bfloat16)
    rest = x - hi.astype(jnp.float32)
    mid = rest.astype(jnp.bfloat16)
    return hi, mid, (rest - mid.astype(jnp.float32)).astype(jnp.bfloat16)


def last_kernel(
    br_ref, bl_ref, mod_ref, inv_ref, u2_ref, v2_ref, f2_ref, u3p_ref, v3p_ref, resp_ref,
    sresp_ref, sstate_ref, smod_ref, d2_ref, x0_ref, x1_ref, hot_ref, cf_ref,
    out_u_ref, out_w_ref, sums_ref,
    u, v, f, sx, beside, dens,
):
    mk = masks()
    lo = mk["lo"]
    mods = smod_ref[...]
    us, svel, fs, sinv = sstate_ref[0], sstate_ref[1], sstate_ref[2], sstate_ref[3]
    sf2, sp3 = strip_beside(br_ref, bl_ref, STRIP_B)
    fs = strip_x(fs, sf2)
    sx[0] = fs
    spush = -sinv * strip_y(fs)
    us = us + (svel + spush)
    for n in range(16, 48):
        u[n] = u3p_ref[n]
        v[n] = v3p_ref[n]

    def put2(n, total):
        vel = v2_ref[n] - inv_ref[n] * total
        v[n] = vel
        u[n] = u2_ref[n] + vel

    assemble(
        lambda n: f2_ref[n], lambda q: unpack_face(br_ref, bl_ref, 0, q, mk), sx.at[0], mk, put2,
        (0, 3),
    )

    def add_third(direction, n, g):
        at = pl.ds(8 * n, 8)
        before = d2_ref[n] if direction == 2 else dens[at, :]
        dens[at, :] = before + x1_ref[64 * direction + n] * g

    forces(lambda n: u[n], into(f), lambda p: mod_ref[p], mk, hook=add_third)
    delta = [face_tile(lambda n: v[n] - v2_ref[n], q, mk) for q in range(16)]
    for q, x in enumerate(face_response(delta, *[lambda q, d=d: resp_ref[d, q] for d in range(3)])):
        beside[q] = unpack_face(br_ref, bl_ref, 8, q, mk) + x
    sbeside = sp3 + strip_response(
        strip_faces(spush), sresp_ref[0], sresp_ref[1], sresp_ref[2], cf_ref
    )
    sx[1] = strip_x(strip_forces(us, mods, cf_ref), sbeside)

    def put3(n, total):
        u[n] = u[n] + (v[n] - inv_ref[n] * total)

    assemble(lambda n: f[n], lambda q: beside[q], sx.at[1], mk, put3)
    for direction in (2, 1, 0):
        for a in range(4):
            for b in range(4):
                nodes = line_nodes(direction, a, b)
                for n, g in zip(nodes, d_line(*[u[n] for n in nodes])):
                    at = pl.ds(8 * n, 8)
                    dens[at, :] = dens[at, :] + x0_ref[64 * direction + n] * g
    cols = [
        dens[pl.ds(s, 64, stride=8), :] + dens[pl.ds(s + 4, 64, stride=8), :] for s in range(4)
    ]
    split = jnp.concatenate(three_way(jnp.concatenate(cols, axis=1)), axis=0)
    res = lax.dot_general(
        split, hot_ref[...], (((1,), (1,)), ((), ())), preferred_element_type=jnp.float32
    )
    sums = res[0:64] + (res[64:128] + res[128:192])
    for q in range(4):
        sums_ref[q] = sums[:, 128 * q : 128 * q + 128]
    for p in range(32):
        a, b = u[2 * p], u[2 * p + 1]
        out_u_ref[p] = jnp.where(lo, a, rs(b, 4))
        out_w_ref[p] = jnp.where(lo, rs(a, 4), b)


def project_kernel(x_ref, basis_ref, out_ref):
    total = (x_ref[0] + x_ref[1]) + (x_ref[2] + x_ref[3])
    t0, t1, t2 = three_way(total)
    b0, b1, b2 = three_way(basis_ref[...])
    out_ref[...] = KERNEL_SCALE * jnp.dot(
        jnp.concatenate([b0, b1, b0, b1, b0, b2], axis=1),
        jnp.concatenate([t0, t0, t1, t1, t2, t0], axis=0),
        preferred_element_type=jnp.float32,
    )


VMEM = pl.BlockSpec(memory_space=pltpu.VMEM)
SMEM = pl.BlockSpec(memory_space=pltpu.SMEM)
HBM = pl.BlockSpec(memory_space=pltpu.HBM)
F32, BF16 = jnp.float32, jnp.bfloat16


def call(kernel, outs, ins, scratch=(), specs=(), limit=24):
    specs = list(specs) + [VMEM] * (len(ins) - len(specs))
    outs = [o if isinstance(o, jax.ShapeDtypeStruct) else jax.ShapeDtypeStruct(o, F32) for o in outs]
    return pl.pallas_call(
        kernel,
        out_shape=outs,
        in_specs=specs,
        out_specs=[VMEM] * len(outs),
        scratch_shapes=list(scratch),
        compiler_params=pltpu.CompilerParams(vmem_limit_bytes=limit * 1024 * 1024),
    )(*ins)


def raw_tiles(x):
    lead = int(np.prod(x.shape[:-2]))
    return x.reshape(lead, 2, 2, 128).transpose(0, 2, 1, 3).reshape(lead * 4, 128)


def from_tiles(x):
    return x.reshape(64, 2, 2, 128).transpose(0, 2, 1, 3).reshape(64, 2, 256)


def on_device(initial_field, adjoint_source, moduli, node_mass, block_owner, spline_basis):
    count = lax.axis_size("dom")
    to_right = [(i, i + 1) for i in range(count - 1)]
    to_left = [(b, a) for a, b in to_right]
    cf = jnp.asarray(COEFFICIENTS)
    sub = lax.axis_index("sub").astype(jnp.int32).reshape(1)
    u2d, w2d, m2d, mass2d = map(raw_tiles, (initial_field, adjoint_source, moduli, node_mass))
    owner = raw_tiles(block_owner[None])
    mod = m2d.reshape(96, 8, 128)
    full, face, strip = (64, 8, 128), (16, 8, 128), (64, 128)

    def swap_rows(left, right):
        return lax.ppermute(left, "dom", to_left), lax.ppermute(right, "dom", to_right)

    edges, u0, f0, mass2, const = call(
        first_kernel,
        [(2, 64, 128), full, full, full, (32, 8, 128)],
        [u2d, w2d, m2d, mass2d],
        [pltpu.VMEM((n, 128), F32) for n in (256, 256, 768, 256)] + [pltpu.SemaphoreType.DMA((4,))],
        [HBM] * 4,
        limit=FIRST_LIMIT,
    )
    edges = lax.all_gather(edges, "sub")
    left, right, u1p, v1p, invp, strips, smod = call(
        open_kernel,
        [(MSG, 8, 128), (MSG, 8, 128), full, full, full, (3, 64, 128), (192, 128)],
        [sub, edges, u0, f0, mass2, const, mod, cf],
        [pltpu.VMEM(full, F32), pltpu.VMEM((2, 64, 128), F32)],
        specs=[SMEM],
    )
    from_right, from_left = swap_rows(left, right)
    left, right, inv, u1, u2, v2, f2, u3p, v3p, resp, sresp, sstate = call(
        middle_kernel,
        [
            (MSG_B, 8, 128), (MSG_B, 8, 128), full, full, full, full, full, full, full,
            (3, 16, 8, 128), (3, 16, 128), (4, 64, 128),
        ],
        [from_right, from_left, u0, f0, mass2, u1p, v1p, invp, strips, smod, mod, cf],
        [pltpu.VMEM(full, F32)] * 2 + [pltpu.VMEM((4, 64, 128), F32), pltpu.VMEM(face, F32)],
    )
    from_right, from_left = swap_rows(left, right)
    d2, x0, x1, hot = call(
        density_kernel,
        [full, (192, 8, 128), (192, 8, 128), jax.ShapeDtypeStruct((512, 512), BF16)],
        [mod, u0, u1, u2, owner],
    )
    out_u, out_w, sums = call(
        last_kernel,
        [(32, 8, 128), (32, 8, 128), (4, 64, 128)],
        [
            from_right, from_left, mod, inv, u2, v2, f2, u3p, v3p, resp, sresp, sstate, smod,
            d2, x0, x1, hot, cf,
        ],
        [pltpu.VMEM(full, F32)] * 3
        + [pltpu.VMEM((2, 64, 128), F32), pltpu.VMEM(face, F32), pltpu.VMEM((512, 128), F32)],
    )
    sums = lax.all_to_all(sums, "sub", 0, 0)
    (kernel,) = call(project_kernel, [(64, 128)], [sums, spline_basis.T])
    return from_tiles(out_u), from_tiles(out_w), kernel


def solution(mesh):
    in_specs = (
        P(None, "dom", "sub"),
        P(None, "dom", "sub"),
        P(None, None, "dom", "sub"),
        P(None, "dom", "sub"),
        P("dom", "sub"),
        P(),
    )
    out_specs = (P(None, "dom", "sub"), P(None, "dom", "sub"), P(None, ("dom", "sub")))
    return jax.shard_map(
        on_device, mesh=mesh, in_specs=in_specs, out_specs=out_specs, check_vma=False
    )
```

```python
import jax
import jax.numpy as jnp
import numpy as np
from jax import lax
from jax.experimental import pallas as pl
from jax.experimental.pallas import tpu as pltpu
from jax.sharding import PartitionSpec as P

STEPS = 4
TIME_STEP = 0.1
KERNEL_SCALE = 0.05
PUSH = TIME_STEP * TIME_STEP

DERIVATIVE = np.array(
    [
        [-3.0, 4.04508497187474, -1.54508497187474, 0.5],
        [-0.80901699437495, 0.0, 1.11803398874989, -0.30901699437495],
        [0.30901699437495, -1.11803398874989, 0.0, 0.80901699437495],
        [-0.5, 1.54508497187474, -4.04508497187474, 3.0],
    ]
)
HALF_AMB = float((DERIVATIVE[0, 1] - DERIVATIVE[0, 2]) / 2)
HALF_CME = float((DERIVATIVE[1, 0] - DERIVATIVE[1, 3]) / 2)
HALF_D = float(DERIVATIVE[1, 2] / 2)

MSG, CONST, STRIP = 38, 16, 32
MSG_B, STRIP_B = 18, 16
FIRST_LIMIT = 54
U0, OWNER, WEIGHTS, BASE = 0, 64, 65, 95
F0, MASS, FACES, HEAD = 0, 64, 128, 160


def strip_coefficients():
    tiles = []
    for d in (DERIVATIVE, DERIVATIVE.T):
        for out in range(2):
            for term in range(4):
                col = np.zeros(8)
                for s in range(8):
                    j = 2 * out + s // 4
                    half = s // 4 if term % 2 == 0 else 1 - s // 4
                    col[s] = d[j, 2 * (term // 2) + half]
                tiles.append(col)
        for delta in range(-3, 4):
            col = np.zeros(8)
            for s in range(8):
                k = s % 4
                if 0 <= k + delta < 4:
                    col[s] = d[k, k + delta]
            tiles.append(col)
    return np.broadcast_to(np.array(tiles, np.float32)[:, :, None], (30, 8, 128))


COEFFICIENTS = np.ascontiguousarray(strip_coefficients())


def sub_iota():
    return lax.broadcasted_iota(jnp.int32, (8, 128), 0)


def lane_iota(rows=8):
    return lax.broadcasted_iota(jnp.int32, (rows, 128), 1)


def rs(x, shift):
    return pltpu.roll(x, shift, 0)


def rl(x, shift):
    return pltpu.roll(x, shift, 1)


def masks():
    s = sub_iota()
    lane = lane_iota()
    return dict(
        even=(s % 2) == 0,
        lo=s < 4,
        ct0=((s // 2) % 2) == 0,
        first=lane == 0,
        last=lane == 127,
    )


def d_line(x0, x1, x2, x3):
    p, m, q, n = x0 + x3, x0 - x3, x1 + x2, x1 - x2
    r = q - p
    s1 = -1.75 * m + HALF_AMB * n
    s2 = HALF_CME * m - HALF_D * n
    r1, r2 = 1.25 * r, HALF_D * r
    return s1 + r1, s2 + r2, s2 - r2, s1 - r1


def dt_line(x0, x1, x2, x3):
    p, m, q, n = x0 + x3, x0 - x3, x1 + x2, x1 - x2
    t = 1.25 * m + HALF_D * n
    q1 = HALF_CME * q - 1.75 * p
    q2 = HALF_AMB * p - HALF_D * q
    return q1 - t, t + q2, t - q2, -(q1 + t)


def line_nodes(direction, a, b):
    if direction == 0:
        return [16 * i + 4 * a + b for i in range(4)]
    if direction == 1:
        return [16 * a + 4 * j + b for j in range(4)]
    return [16 * a + 4 * b + k for k in range(4)]


def expanded(x, upper, mk):
    r = rs(x, 4)
    return jnp.where(mk["lo"], r, x) if upper else jnp.where(mk["lo"], x, r)


def forces(u, f, mod, mk, planes=(0, 1, 2, 3), hook=None):
    for direction in (2, 1, 0):
        for a in range(4):
            if direction and a not in planes:
                continue
            for b in range(4):
                nodes = line_nodes(direction, a, b)
                g = d_line(*[u(n) for n in nodes])
                if hook is not None:
                    for n, gn in zip(nodes, g):
                        hook(direction, n, gn)
                t = []
                for n, gn in zip(nodes, g):
                    at = 64 * direction + n
                    t.append(expanded(mod(at // 2), at % 2, mk) * gn)
                for n, o in zip(nodes, dt_line(*t)):
                    if n // 16 in planes:
                        f(n, o, direction == 2)


def into(ref):
    def put(n, value, first):
        ref[n] = value if first else ref[n] + value

    return put


def face_tile(get, q, mk):
    return jnp.where(mk["even"], get(q), get(48 + q))


def pack_faces(left_ref, right_ref, base, get, mk):
    even = mk["even"]
    for p in range(8):
        x, y = get(2 * p), get(2 * p + 1)
        left_ref[base + p] = jnp.where(even, x, rs(y, 1))
        right_ref[base + p] = jnp.where(even, rs(x, 7), y)


def unpack_face(from_right, from_left, base, q, mk):
    r, l = from_right[base + q // 2], from_left[base + q // 2]
    if q % 2:
        return jnp.where(mk["even"], rs(l, 7), r)
    return jnp.where(mk["even"], l, rs(r, 1))


def face_response(delta, diagonal, mod_j, mod_k):
    out = [diagonal(q) * delta[q] for q in range(16)]
    for mod, lines in (
        (mod_j, [[4 * j + k for j in range(4)] for k in range(4)]),
        (mod_k, [[4 * j + k for k in range(4)] for j in range(4)]),
    ):
        for line in lines:
            t = [mod(q) * g for q, g in zip(line, d_line(*[delta[q] for q in line]))]
            for q, o in zip(line, dt_line(*t)):
                out[q] = out[q] + o
    return out


def along_x(f, beside, i, q, mk):
    even = mk["even"]
    x = f(16 * i + q)
    if i in (1, 2):
        return x
    other = beside(q) if beside is not None else 0.0
    if i == 3:
        return x + jnp.where(even, rs(f(q), 7), other)
    return x + jnp.where(even, other, rs(f(48 + q), 1))


def assembled(f, beside, strip, i, k, mk):
    vals = [along_x(f, beside, i, 4 * j + k, mk) for j in range(4)]

    def inject(row):
        return pltpu.roll(
            jnp.broadcast_to(strip[row : row + 1, :], (8, 128)), 68, 1, stride=8, stride_axis=0
        )

    b, a = vals[0], vals[3]
    up, down = rl(b, 127), rl(a, 1)
    up = jnp.where(mk["last"], jnp.where(mk["ct0"], rs(up, 6), inject(16 * i + k)), up)
    down = jnp.where(mk["first"], jnp.where(mk["ct0"], inject(16 * i + 12 + k), rs(down, 2)), down)
    return [b + down, vals[1], vals[2], a + up]


def assemble(f, beside, strip, mk, put, planes=(0, 1, 2, 3)):
    for i in planes:
        for k in range(4):
            for j, total in enumerate(assembled(f, beside, strip, i, k, mk)):
                put(16 * i + 4 * j + k, total)


def not_shared(n, x, mk):
    if n < 16:
        return jnp.where(mk["even"], 0.0, x)
    if n >= 48:
        return jnp.where(mk["even"], x, 0.0)
    return x


def strip_lines(x, cf, base):
    along_j, along_k = [], []
    for i in range(len(x) // 2):
        a, b = x[2 * i], x[2 * i + 1]
        terms = (a, rs(a, 4), b, rs(b, 4))
        for out in range(2):
            along_j.append(sum(cf[base + 4 * out + t] * terms[t] for t in range(4)))
    for y in x:
        along_k.append(
            sum(cf[base + 8 + d] * (rs(y, (3 - d) % 8) if d != 3 else y) for d in range(7))
        )
    return along_j, along_k


def strip_forces(us, mods, cf):
    x = [us[8 * v : 8 * v + 8] for v in range(8)]
    gj, gk = strip_lines(x, cf, 0)
    gi = [None] * 8
    for e in range(2):
        for i, g in enumerate(d_line(*[x[2 * m + e] for m in range(4)])):
            gi[2 * i + e] = g
    ti, tj, tk = (
        [mods[64 * d + 8 * v : 64 * d + 8 * v + 8] * g[v] for v in range(8)]
        for d, g in enumerate((gi, gj, gk))
    )
    fj = strip_lines(tj, cf, 15)[0]
    fk = strip_lines(tk, cf, 15)[1]
    f = [fj[v] + fk[v] for v in range(8)]
    for e in range(2):
        for i, o in enumerate(dt_line(*[ti[2 * m + e] for m in range(4)])):
            f[2 * i + e] = f[2 * i + e] + o
    return jnp.concatenate(f, axis=0)


def row_zero(rows):
    return ((lane_iota(rows) // 8) % 2) == 1


def strip_faces(f):
    return jnp.where(row_zero(16), f[0:16], f[48:64])


def strip_beside(from_right, from_left, base):
    r = jnp.concatenate([from_right[base], from_right[base + 1]], axis=0)
    l = jnp.concatenate([from_left[base], from_left[base + 1]], axis=0)
    both = jnp.where(row_zero(16), rl(l, 8), rl(r, 120))
    return both, rl(both, 64)


def strip_send(left_ref, right_ref, base, x, y):
    both = jnp.where(lane_iota(16) < 64, x, rl(y, 64))
    for p in range(2):
        left_ref[base + p] = both[8 * p : 8 * p + 8]
        right_ref[base + p] = both[8 * p : 8 * p + 8]


def strip_response(delta, diagonal, mod_j, mod_k, cf):
    x = [delta[0:8], delta[8:16]]
    gj, gk = strip_lines(x, cf, 0)
    fj = strip_lines([mod_j[8 * v : 8 * v + 8] * gj[v] for v in range(2)], cf, 15)[0]
    fk = strip_lines([mod_k[8 * v : 8 * v + 8] * gk[v] for v in range(2)], cf, 15)[1]
    return diagonal * delta + jnp.concatenate([fj[v] + fk[v] for v in range(2)], axis=0)


def strip_x(f, beside):
    zero = row_zero(16)
    b, a = f[0:16], f[48:64]
    na = a + jnp.where(zero, rl(b, 8), beside)
    nb = b + jnp.where(zero, beside, rl(a, 120))
    return jnp.concatenate([nb, f[16:48], na], axis=0)


def strip_y(f):
    low = sub_iota() < 4
    parts = []
    for i in range(4):
        x, y = f[16 * i : 16 * i + 8], f[16 * i + 8 : 16 * i + 16]
        parts.append(x + jnp.where(low, rs(rl(y, 1), 4), 0.0))
        parts.append(y + jnp.where(low, 0.0, rs(rl(x, 127), 4)))
    return jnp.concatenate(parts, axis=0)


def inverse_mass(m):
    return jnp.where(m > 0.5, PUSH / jnp.where(m > 0.5, m, 1.0), 0.0)


def strip_not_shared(x):
    zero = row_zero(16)
    return jnp.concatenate(
        [jnp.where(zero, 0.0, x[0:16]), x[16:48], jnp.where(zero, x[48:64], 0.0)], axis=0
    )


def strip_arrays(z1, z2):
    q = lane_iota(64) // 32

    def two(a, b):
        return jnp.where(q == 0, a, jnp.where(q == 1, b, 0.0))

    us = two(z1, z1)
    m0 = two(rl(z1, 64), rl(z1, 96))
    m1 = two(rl(z1, 32), rl(z1, 64))
    m2 = two(z2, rl(z2, 32))
    mass = two(rl(z2, 96), z2)
    return us, jnp.concatenate([m0, m1, m2], axis=0), mass


def state_expand(xu, xw, mk):
    return jnp.where(mk["lo"], xu, rs(xw, 4)), jnp.where(mk["lo"], rs(xu, 4), xw)


def tile(ref, p):
    return ref[8 * p : 8 * p + 8, :]


def first_kernel(
    u_hbm, w_hbm, mod_hbm, mass_hbm, owner_hbm, cf_hbm, z_ref, base_ref, head_ref,
    u_ref, w_ref, m_ref, mass_ref, owner_ref, cf_ref, sems,
):
    state_ref, f_ref = base_ref.at[U0:OWNER], head_ref.at[F0:MASS]
    mass2_ref, const_ref = head_ref.at[MASS:FACES], head_ref.at[FACES:HEAD]
    copies = [
        pltpu.make_async_copy(src, dst, sems.at[i])
        for i, (src, dst) in enumerate(
            (
                (u_hbm, u_ref), (w_hbm, w_ref), (mod_hbm, m_ref), (mass_hbm, mass_ref),
                (owner_hbm, owner_ref), (cf_hbm, cf_ref),
            )
        )
    ]
    for c in copies:
        c.start()
    for c in copies:
        c.wait()
    mk = masks()
    lane = lane_iota(64)
    pieces = (
        (w_ref, 0, 0, 0),
        (u_ref, 0, 0, 1),
        (m_ref, 0, 0, 2),
        (m_ref, 256, 0, 3),
        (m_ref, 512, 1, 0),
        (mass_ref, 0, 1, 1),
    )
    z = [jnp.zeros((64, 128), jnp.float32), jnp.zeros((64, 128), jnp.float32)]
    for ref, base, half, slot in pieces:
        for side in range(2):
            for r in range(2):
                rows = ref[pl.ds(base + 2 * (1 - side) + r, 64, stride=4), :]
                dest = slot * 32 + (1 - side) * 16 + (1 - r) * 8 + (3 if side else 1)
                src = 0 if side else 124
                moved = rl(rows, (dest - src) % 128)
                z[half] = jnp.where((lane >= dest) & (lane < dest + 4), moved, z[half])
    z_ref[0] = z[0]
    z_ref[1] = z[1]
    for p in range(32):
        a, b = state_expand(tile(u_ref, p), tile(w_ref, p), mk)
        state_ref[2 * p] = a
        state_ref[2 * p + 1] = b
        mass2_ref[2 * p] = expanded(tile(mass_ref, p), 0, mk)
        mass2_ref[2 * p + 1] = expanded(tile(mass_ref, p), 1, mk)

    def moduli(direction):
        def get(n):
            at = 64 * direction + n
            return expanded(tile(m_ref, at // 2), at % 2, mk)

        return get

    for q in range(16):
        mi = [moduli(0)(16 * i + q) for i in range(4)]
        diagonal = [sum(float(DERIVATIVE[i, e] ** 2) * mi[i] for i in range(4)) for e in (0, 3)]
        diagonal = jnp.where(mk["even"], diagonal[0], diagonal[1])
        own_mass = face_tile(lambda n: mass2_ref[n], q, mk)
        const_ref[q] = jnp.where(mk["lo"], own_mass, diagonal)
        const_ref[16 + q] = jnp.where(
            mk["lo"], face_tile(moduli(1), q, mk), face_tile(moduli(2), q, mk)
        )
    forces(lambda n: state_ref[n], into(f_ref), lambda p: tile(m_ref, p), mk)
    owner = owner_ref[...].astype(jnp.float32)
    base_ref[OWNER] = jnp.concatenate([owner, owner], axis=0)
    for t in range(WEIGHTS, BASE):
        base_ref[t] = cf_ref[t - WEIGHTS]


def open_kernel(
    sub_ref, z_ref, base_ref, head_ref, mod_ref,
    left_ref, right_ref, u1_ref, v1_ref, inv_ref, strip_ref, smod_ref,
    f, sx,
):
    u0_ref, f0_ref = base_ref.at[U0:OWNER], head_ref.at[F0:MASS]
    mass2_ref, const_ref = head_ref.at[MASS:FACES], head_ref.at[FACES:HEAD]
    cf_ref = base_ref.at[WEIGHTS:BASE]
    mk = masks()
    sub = sub_ref[0]
    lane = lane_iota(64)
    side0 = ((lane // 16) % 2) == 1
    c = lane % 8
    below, above = jnp.maximum(sub - 1, 0), jnp.minimum(sub + 1, 3)
    zs = []
    for half in range(2):
        own = z_ref[sub, half]
        zl = jnp.where(sub > 0, z_ref[below, half], 0.0)
        zr = jnp.where(sub < 3, z_ref[above, half], 0.0)
        low = jnp.where(c == 0, 0.0, jnp.where(c <= 4, zl, rl(own, 18)))
        high = jnp.where(c <= 2, rl(own, 110), jnp.where(c == 7, 0.0, zr))
        zs.append(jnp.where(side0, low, high))
    us, mods, smass = strip_arrays(zs[0], zs[1])
    fs = strip_forces(us, mods, cf_ref)
    smod_ref[...] = mods
    strip_ref[0] = us
    strip_ref[1] = fs
    strip_ref[2] = smass
    zero = row_zero(16)
    diagonal = [
        sum(float(DERIVATIVE[i, e] ** 2) * mods[16 * i : 16 * i + 16] for i in range(4))
        for e in (0, 3)
    ]
    strip_send(
        left_ref, right_ref, STRIP + 2, strip_faces(smass), jnp.where(zero, *diagonal)
    )
    strip_send(
        left_ref, right_ref, STRIP + 4, strip_faces(mods[64:128]), strip_faces(mods[128:192])
    )
    sm = strip_x(smass, 0.0)
    sx[0] = sm
    fx = strip_x(fs, 0.0)
    sx[1] = fx
    sinv = strip_not_shared(inverse_mass(strip_y(sm)))
    partial = strip_forces(us - sinv * strip_y(fx), mods, cf_ref)
    strip_send(left_ref, right_ref, STRIP, strip_faces(fs), strip_faces(partial))

    def put_mass(n, total):
        inv_ref[n] = not_shared(n, inverse_mass(total), mk)

    assemble(lambda n: mass2_ref[n], None, sx.at[0], mk, put_mass)

    def put(n, total):
        vel = -inv_ref[n] * total
        v1_ref[n] = vel
        u1_ref[n] = u0_ref[n] + vel

    assemble(lambda n: f0_ref[n], None, sx.at[1], mk, put)
    forces(lambda n: u1_ref[n], into(f), lambda p: mod_ref[p], mk, planes=(0, 3))
    pack_faces(left_ref, right_ref, 0, lambda q: face_tile(lambda n: f0_ref[n], q, mk), mk)
    pack_faces(left_ref, right_ref, 8, lambda q: face_tile(lambda n: f[n], q, mk), mk)
    pack_faces(left_ref, right_ref, CONST, lambda q: const_ref[q], mk)
    pack_faces(left_ref, right_ref, CONST + 8, lambda q: const_ref[16 + q], mk)


def middle_kernel(
    mr_ref, ml_ref, base_ref, head_ref, u1p_ref, v1p_ref, invp_ref, strip_ref, smod_ref,
    mod_ref,
    bl_ref, br_ref, inv_ref, u1_ref, u2_ref, v2_ref, f2_ref, u3_ref, v3_ref, resp_ref,
    sresp_ref, sstate_ref,
    v1, f, sx, beside,
):
    u0_ref, f0_ref = base_ref.at[U0:OWNER], head_ref.at[F0:MASS]
    mass2_ref, cf_ref = head_ref.at[MASS:FACES], base_ref.at[WEIGHTS:BASE]
    mk = masks()
    lo = mk["lo"]
    us, fs, smass = strip_ref[0], strip_ref[1], strip_ref[2]
    mods = smod_ref[...]
    sf0, sp1 = strip_beside(mr_ref, ml_ref, STRIP)
    smn, sresp0 = strip_beside(mr_ref, ml_ref, STRIP + 2)
    sresp1, sresp2 = strip_beside(mr_ref, ml_ref, STRIP + 4)
    sresp_ref[0] = sresp0
    sresp_ref[1] = sresp1
    sresp_ref[2] = sresp2
    for q in range(16):
        x = unpack_face(mr_ref, ml_ref, CONST, q, mk)
        r = rs(x, 4)
        beside[q] = jnp.where(lo, x, r)
        resp_ref[0, q] = jnp.where(lo, r, x)
        x = unpack_face(mr_ref, ml_ref, CONST + 8, q, mk)
        r = rs(x, 4)
        resp_ref[1, q] = jnp.where(lo, x, r)
        resp_ref[2, q] = jnp.where(lo, r, x)
    responses = [lambda q, d=d: resp_ref[d, q] for d in range(3)]
    sm = strip_x(smass, smn)
    sx[0] = sm
    sinv = inverse_mass(strip_y(sm))
    for n in range(16, 48):
        inv_ref[n] = invp_ref[n]
        u1_ref[n] = u1p_ref[n]
        v1[n] = v1p_ref[n]

    def put_mass(n, total):
        inv_ref[n] = inverse_mass(total)

    assemble(lambda n: mass2_ref[n], lambda q: beside[q], sx.at[0], mk, put_mass, (0, 3))
    fs = strip_x(fs, sf0)
    sx[1] = fs
    svel = -sinv * strip_y(fs)
    us = us + svel

    def put0(n, total):
        vel = -inv_ref[n] * total
        v1[n] = vel
        u1_ref[n] = u0_ref[n] + vel

    assemble(
        lambda n: f0_ref[n], lambda q: unpack_face(mr_ref, ml_ref, 0, q, mk), sx.at[1], mk, put0,
        (0, 3),
    )
    forces(lambda n: u1_ref[n], into(f), lambda p: mod_ref[p], mk)
    delta = [face_tile(lambda n: v1[n], q, mk) for q in range(16)]
    for q, x in enumerate(face_response(delta, *responses)):
        beside[q] = unpack_face(mr_ref, ml_ref, 8, q, mk) + x
    sbeside = sp1 + strip_response(strip_faces(svel), sresp0, sresp1, sresp2, cf_ref)
    fs = strip_x(strip_forces(us, mods, cf_ref), sbeside)
    sx[2] = fs
    svel = svel - sinv * strip_y(fs)
    us = us + svel

    def put1(n, total):
        vel = v1[n] - inv_ref[n] * total
        v2_ref[n] = vel
        u2_ref[n] = u1_ref[n] + vel

    assemble(lambda n: f[n], lambda q: beside[q], sx.at[2], mk, put1)
    forces(lambda n: u2_ref[n], into(f2_ref), lambda p: mod_ref[p], mk)
    fs = strip_forces(us, mods, cf_ref)
    sstate_ref[0] = us
    sstate_ref[1] = svel
    sstate_ref[2] = fs
    sstate_ref[3] = sinv
    fx = strip_x(fs, 0.0)
    sx[3] = fx
    partial = strip_forces(
        us + (svel - strip_not_shared(sinv) * strip_y(fx)), mods, cf_ref
    )

    def put2(n, total):
        vel = v2_ref[n] - not_shared(n, inv_ref[n], mk) * total
        v3_ref[n] = vel
        u3_ref[n] = u2_ref[n] + vel

    assemble(lambda n: f2_ref[n], None, sx.at[3], mk, put2)
    forces(lambda n: u3_ref[n], into(f), lambda p: mod_ref[p], mk, planes=(0, 3))
    pack_faces(bl_ref, br_ref, 0, lambda q: face_tile(lambda n: f2_ref[n], q, mk), mk)
    pack_faces(bl_ref, br_ref, 8, lambda q: face_tile(lambda n: f[n], q, mk), mk)
    strip_send(bl_ref, br_ref, STRIP_B, strip_faces(fs), strip_faces(partial))


def three_way(x):
    hi = x.astype(jnp.bfloat16)
    rest = x - hi.astype(jnp.float32)
    mid = rest.astype(jnp.bfloat16)
    return hi, mid, (rest - mid.astype(jnp.float32)).astype(jnp.bfloat16)


def density_kernel(
    mod_ref, base_ref, u1_ref, u2_ref, basis_ref, d2_ref, x0_ref, x1_ref, hot_ref, stack_ref
):
    mk = masks()
    lo = mk["lo"]
    for direction in (2, 1, 0):
        for a in range(4):
            for b in range(4):
                nodes = line_nodes(direction, a, b)
                g0 = d_line(*[base_ref[U0 + n] for n in nodes])
                g1 = d_line(*[u1_ref[n] for n in nodes])
                g2 = d_line(*[u2_ref[n] for n in nodes])
                for e, n in enumerate(nodes):
                    at = 64 * direction + n
                    m = expanded(mod_ref[at // 2], at % 2, mk)
                    x0_ref[at] = jnp.where(lo, m * rs(g0[e], 4), 0.0)
                    x1_ref[at] = m * rs(g1[e], 4)
                    t = jnp.where(lo, m * g2[e] * rs(g2[e], 4), 0.0)
                    d2_ref[n] = t if direction == 2 else d2_ref[n] + t
    block = lax.broadcasted_iota(jnp.int32, (512, 128), 0).astype(jnp.float32)
    for s in range(4):
        owner = jnp.broadcast_to(base_ref[OWNER][s : s + 1, :], (512, 128))
        hot_ref[:, 128 * s : 128 * s + 128] = (
            (block == owner).astype(jnp.float32).astype(jnp.bfloat16)
        )
    b0, b1, b2 = three_way(basis_ref[...])
    stack_ref[...] = jnp.concatenate([b0, b1, b0, b1, b0, b2], axis=1)


def last_kernel(
    br_ref, bl_ref, mod_ref, inv_ref, u2_ref, v2_ref, f2_ref, u3p_ref, v3p_ref, resp_ref,
    sresp_ref, sstate_ref, smod_ref, d2_ref, x0_ref, x1_ref, hot_ref, base_ref,
    out_u_ref, out_w_ref, sums_ref,
    u, v, f, sx, beside, dens,
):
    cf_ref = base_ref.at[WEIGHTS:BASE]
    mk = masks()
    lo = mk["lo"]
    mods = smod_ref[...]
    us, svel, fs, sinv = sstate_ref[0], sstate_ref[1], sstate_ref[2], sstate_ref[3]
    sf2, sp3 = strip_beside(br_ref, bl_ref, STRIP_B)
    fs = strip_x(fs, sf2)
    sx[0] = fs
    spush = -sinv * strip_y(fs)
    us = us + (svel + spush)
    for n in range(16, 48):
        u[n] = u3p_ref[n]
        v[n] = v3p_ref[n]

    def put2(n, total):
        vel = v2_ref[n] - inv_ref[n] * total
        v[n] = vel
        u[n] = u2_ref[n] + vel

    assemble(
        lambda n: f2_ref[n], lambda q: unpack_face(br_ref, bl_ref, 0, q, mk), sx.at[0], mk, put2,
        (0, 3),
    )

    def add_third(direction, n, g):
        at = pl.ds(8 * n, 8)
        before = d2_ref[n] if direction == 2 else dens[at, :]
        dens[at, :] = before + x1_ref[64 * direction + n] * g

    forces(lambda n: u[n], into(f), lambda p: mod_ref[p], mk, hook=add_third)
    delta = [face_tile(lambda n: v[n] - v2_ref[n], q, mk) for q in range(16)]
    for q, x in enumerate(face_response(delta, *[lambda q, d=d: resp_ref[d, q] for d in range(3)])):
        beside[q] = unpack_face(br_ref, bl_ref, 8, q, mk) + x
    sbeside = sp3 + strip_response(
        strip_faces(spush), sresp_ref[0], sresp_ref[1], sresp_ref[2], cf_ref
    )
    sx[1] = strip_x(strip_forces(us, mods, cf_ref), sbeside)

    def put3(n, total):
        u[n] = u[n] + (v[n] - inv_ref[n] * total)

    assemble(lambda n: f[n], lambda q: beside[q], sx.at[1], mk, put3)
    for direction in (2, 1, 0):
        for a in range(4):
            for b in range(4):
                nodes = line_nodes(direction, a, b)
                for n, g in zip(nodes, d_line(*[u[n] for n in nodes])):
                    at = pl.ds(8 * n, 8)
                    dens[at, :] = dens[at, :] + x0_ref[64 * direction + n] * g
    cols = [
        dens[pl.ds(s, 64, stride=8), :] + dens[pl.ds(s + 4, 64, stride=8), :] for s in range(4)
    ]
    split = jnp.concatenate(three_way(jnp.concatenate(cols, axis=1)), axis=0)
    res = lax.dot_general(
        split, hot_ref[...], (((1,), (1,)), ((), ())), preferred_element_type=jnp.float32
    )
    sums = res[0:64] + (res[64:128] + res[128:192])
    for q in range(4):
        sums_ref[q] = sums[:, 128 * q : 128 * q + 128]
    for p in range(32):
        a, b = u[2 * p], u[2 * p + 1]
        out_u_ref[p] = jnp.where(lo, a, rs(b, 4))
        out_w_ref[p] = jnp.where(lo, rs(a, 4), b)


def project_kernel(sub_ref, x_ref, stack_ref, out_ref):
    sub = sub_ref[0]
    total = (x_ref[0, sub] + x_ref[1, sub]) + (x_ref[2, sub] + x_ref[3, sub])
    t0, t1, t2 = three_way(total)
    out_ref[...] = KERNEL_SCALE * jnp.dot(
        stack_ref[...], jnp.concatenate([t0, t0, t1, t1, t2, t0], axis=0),
        preferred_element_type=jnp.float32,
    )


VMEM = pl.BlockSpec(memory_space=pltpu.VMEM)
SMEM = pl.BlockSpec(memory_space=pltpu.SMEM)
HBM = pl.BlockSpec(memory_space=pltpu.HBM)
F32, BF16 = jnp.float32, jnp.bfloat16


def call(kernel, outs, ins, scratch=(), specs=(), limit=24, space=None):
    specs = list(specs) + [VMEM] * (len(ins) - len(specs))
    outs = [o if isinstance(o, jax.ShapeDtypeStruct) else jax.ShapeDtypeStruct(o, F32) for o in outs]
    if space is not None:
        outs = [space(o.shape, o.dtype) for o in outs]
    return pl.pallas_call(
        kernel,
        out_shape=outs,
        in_specs=specs,
        out_specs=[VMEM] * len(outs),
        scratch_shapes=list(scratch),
        compiler_params=pltpu.CompilerParams(vmem_limit_bytes=limit * 1024 * 1024),
    )(*ins)


def raw_tiles(x):
    lead = int(np.prod(x.shape[:-2]))
    return x.reshape(lead, 2, 2, 128).transpose(0, 2, 1, 3).reshape(lead * 4, 128)


def from_tiles(x):
    return x.reshape(64, 2, 2, 128).transpose(0, 2, 1, 3).reshape(64, 2, 256)


def on_device(initial_field, adjoint_source, moduli, node_mass, block_owner, spline_basis):
    count = lax.axis_size("dom")
    to_right = [(i, i + 1) for i in range(count - 1)]
    to_left = [(b, a) for a, b in to_right]
    cf = jnp.asarray(COEFFICIENTS)
    sub = lax.axis_index("sub").astype(jnp.int32).reshape(1)
    u2d, w2d, m2d, mass2d = map(raw_tiles, (initial_field, adjoint_source, moduli, node_mass))
    owner = raw_tiles(block_owner[None])
    mod = m2d.reshape(96, 8, 128)
    full, face = (64, 8, 128), (16, 8, 128)

    def swap_rows(left, right):
        return lax.ppermute(left, "dom", to_left), lax.ppermute(right, "dom", to_right)

    edges, base, head = call(
        first_kernel,
        [(2, 64, 128), (BASE, 8, 128), (HEAD, 8, 128)],
        [u2d, w2d, m2d, mass2d, owner, cf],
        [pltpu.VMEM((n, 128), F32) for n in (256, 256, 768, 256)]
        + [pltpu.VMEM((4, 128), jnp.int32), pltpu.VMEM((BASE - WEIGHTS, 8, 128), F32)]
        + [pltpu.SemaphoreType.DMA((6,))],
        [HBM] * 6,
        limit=FIRST_LIMIT,
        space=pltpu.VMEM,
    )
    edges = lax.all_gather(edges, "sub")
    left, right, u1p, v1p, invp, strips, smod = call(
        open_kernel,
        [(MSG, 8, 128), (MSG, 8, 128), full, full, full, (3, 64, 128), (192, 128)],
        [sub, edges, base, head, mod],
        [pltpu.VMEM(full, F32), pltpu.VMEM((2, 64, 128), F32)],
        specs=[SMEM],
        space=pltpu.VMEM,
    )
    from_right, from_left = swap_rows(left, right)
    left, right, inv, u1, u2, v2, f2, u3p, v3p, resp, sresp, sstate = call(
        middle_kernel,
        [
            (MSG_B, 8, 128), (MSG_B, 8, 128), full, full, full, full, full, full, full,
            (3, 16, 8, 128), (3, 16, 128), (4, 64, 128),
        ],
        [from_right, from_left, base, head, u1p, v1p, invp, strips, smod, mod],
        [pltpu.VMEM(full, F32)] * 2 + [pltpu.VMEM((4, 64, 128), F32), pltpu.VMEM(face, F32)],
        space=pltpu.VMEM,
    )
    from_right, from_left = swap_rows(left, right)
    wide = jax.ShapeDtypeStruct((512, 512), BF16)
    d2, x0, x1, hot, stack = call(
        density_kernel,
        [full, (192, 8, 128), (192, 8, 128), wide, jax.ShapeDtypeStruct((64, 384), BF16)],
        [mod, base, u1, u2, spline_basis.T],
        space=pltpu.VMEM,
    )
    out_u, out_w, sums = call(
        last_kernel,
        [(32, 8, 128), (32, 8, 128), (4, 64, 128)],
        [
            from_right, from_left, mod, inv, u2, v2, f2, u3p, v3p, resp, sresp, sstate, smod,
            d2, x0, x1, hot, base,
        ],
        [pltpu.VMEM(full, F32)] * 3
        + [pltpu.VMEM((2, 64, 128), F32), pltpu.VMEM(face, F32), pltpu.VMEM((512, 128), F32)],
    )
    sums = lax.all_gather(sums, "sub")
    (kernel,) = call(project_kernel, [(64, 128)], [sub, sums, stack], specs=[SMEM])
    return from_tiles(out_u), from_tiles(out_w), kernel


def solution(mesh):
    in_specs = (
        P(None, "dom", "sub"),
        P(None, "dom", "sub"),
        P(None, None, "dom", "sub"),
        P(None, "dom", "sub"),
        P("dom", "sub"),
        P(),
    )
    out_specs = (P(None, "dom", "sub"), P(None, "dom", "sub"), P(None, ("dom", "sub")))
    return jax.shard_map(
        on_device, mesh=mesh, in_specs=in_specs, out_specs=out_specs, check_vma=False
    )
```

```python
import jax
import jax.numpy as jnp
import numpy as np
from jax import lax
from jax.experimental import pallas as pl
from jax.experimental.pallas import tpu as pltpu
from jax.sharding import PartitionSpec as P

STEPS = 4
TIME_STEP = 0.1
KERNEL_SCALE = 0.05
PUSH = TIME_STEP * TIME_STEP

DERIVATIVE = np.array(
    [
        [-3.0, 4.04508497187474, -1.54508497187474, 0.5],
        [-0.80901699437495, 0.0, 1.11803398874989, -0.30901699437495],
        [0.30901699437495, -1.11803398874989, 0.0, 0.80901699437495],
        [-0.5, 1.54508497187474, -4.04508497187474, 3.0],
    ]
)
HALF_AMB = float((DERIVATIVE[0, 1] - DERIVATIVE[0, 2]) / 2)
HALF_CME = float((DERIVATIVE[1, 0] - DERIVATIVE[1, 3]) / 2)
HALF_D = float(DERIVATIVE[1, 2] / 2)

MSG, CONST, STRIP = 38, 16, 32
MSG_B, STRIP_B = 18, 16
FIRST_LIMIT = 54
U0, OWNER, WEIGHTS, BASE = 0, 64, 65, 95
F0, MASS, FACES, HEAD = 0, 64, 128, 160


def strip_coefficients():
    tiles = []
    for d in (DERIVATIVE, DERIVATIVE.T):
        for out in range(2):
            for term in range(4):
                col = np.zeros(8)
                for s in range(8):
                    j = 2 * out + s // 4
                    half = s // 4 if term % 2 == 0 else 1 - s // 4
                    col[s] = d[j, 2 * (term // 2) + half]
                tiles.append(col)
        for delta in range(-3, 4):
            col = np.zeros(8)
            for s in range(8):
                k = s % 4
                if 0 <= k + delta < 4:
                    col[s] = d[k, k + delta]
            tiles.append(col)
    return np.broadcast_to(np.array(tiles, np.float32)[:, :, None], (30, 8, 128))


COEFFICIENTS = np.ascontiguousarray(strip_coefficients())


def sub_iota():
    return lax.broadcasted_iota(jnp.int32, (8, 128), 0)


def lane_iota(rows=8):
    return lax.broadcasted_iota(jnp.int32, (rows, 128), 1)


def rs(x, shift):
    return pltpu.roll(x, shift, 0)


def rl(x, shift):
    return pltpu.roll(x, shift, 1)


def masks():
    s = sub_iota()
    lane = lane_iota()
    return dict(
        even=(s % 2) == 0,
        lo=s < 4,
        ct0=((s // 2) % 2) == 0,
        first=lane == 0,
        last=lane == 127,
    )


def d_line(x0, x1, x2, x3):
    p, m, q, n = x0 + x3, x0 - x3, x1 + x2, x1 - x2
    r = q - p
    s1 = -1.75 * m + HALF_AMB * n
    s2 = HALF_CME * m - HALF_D * n
    r1, r2 = 1.25 * r, HALF_D * r
    return s1 + r1, s2 + r2, s2 - r2, s1 - r1


def dt_line(x0, x1, x2, x3):
    p, m, q, n = x0 + x3, x0 - x3, x1 + x2, x1 - x2
    t = 1.25 * m + HALF_D * n
    q1 = HALF_CME * q - 1.75 * p
    q2 = HALF_AMB * p - HALF_D * q
    return q1 - t, t + q2, t - q2, -(q1 + t)


def line_nodes(direction, a, b):
    if direction == 0:
        return [16 * i + 4 * a + b for i in range(4)]
    if direction == 1:
        return [16 * a + 4 * j + b for j in range(4)]
    return [16 * a + 4 * b + k for k in range(4)]


def expanded(x, upper, mk):
    r = rs(x, 4)
    return jnp.where(mk["lo"], r, x) if upper else jnp.where(mk["lo"], x, r)


def forces(u, f, mod, mk, planes=(0, 1, 2, 3), hook=None):
    for direction in (2, 1, 0):
        for a in range(4):
            if direction and a not in planes:
                continue
            for b in range(4):
                nodes = line_nodes(direction, a, b)
                g = d_line(*[u(n) for n in nodes])
                if hook is not None:
                    for n, gn in zip(nodes, g):
                        hook(direction, n, gn)
                t = []
                for n, gn in zip(nodes, g):
                    at = 64 * direction + n
                    t.append(expanded(mod(at // 2), at % 2, mk) * gn)
                for n, o in zip(nodes, dt_line(*t)):
                    if n // 16 in planes:
                        f(n, o, direction == 2)


def into(ref):
    def put(n, value, first):
        ref[n] = value if first else ref[n] + value

    return put


def face_tile(get, q, mk):
    return jnp.where(mk["even"], get(q), get(48 + q))


class Send:
    def __init__(self, far_ref, near_ref, odd):
        self.far, self.near, self.odd = far_ref, near_ref, odd

    def put(self, at, left, right):
        self.far[at] = jnp.where(self.odd, right, left)
        self.near[at] = jnp.where(self.odd, left, right)


class Receive:
    def __init__(self, odd_ref, even_ref, odd):
        self.odd_ref, self.even_ref, self.odd = odd_ref, even_ref, odd

    def __getitem__(self, at):
        return jnp.where(self.odd, self.odd_ref[at], self.even_ref[at])


def pack_faces(send, base, get, mk):
    even = mk["even"]
    for p in range(8):
        x, y = get(2 * p), get(2 * p + 1)
        send.put(base + p, jnp.where(even, x, rs(y, 1)), jnp.where(even, rs(x, 7), y))


def unpack_face(from_right, from_left, base, q, mk):
    r, l = from_right[base + q // 2], from_left[base + q // 2]
    if q % 2:
        return jnp.where(mk["even"], rs(l, 7), r)
    return jnp.where(mk["even"], l, rs(r, 1))


def face_response(delta, diagonal, mod_j, mod_k):
    out = [diagonal(q) * delta[q] for q in range(16)]
    for mod, lines in (
        (mod_j, [[4 * j + k for j in range(4)] for k in range(4)]),
        (mod_k, [[4 * j + k for k in range(4)] for j in range(4)]),
    ):
        for line in lines:
            t = [mod(q) * g for q, g in zip(line, d_line(*[delta[q] for q in line]))]
            for q, o in zip(line, dt_line(*t)):
                out[q] = out[q] + o
    return out


def along_x(f, beside, i, q, mk):
    even = mk["even"]
    x = f(16 * i + q)
    if i in (1, 2):
        return x
    other = beside(q) if beside is not None else 0.0
    if i == 3:
        return x + jnp.where(even, rs(f(q), 7), other)
    return x + jnp.where(even, other, rs(f(48 + q), 1))


def assembled(f, beside, strip, i, k, mk):
    vals = [along_x(f, beside, i, 4 * j + k, mk) for j in range(4)]

    def inject(row):
        return pltpu.roll(
            jnp.broadcast_to(strip[row : row + 1, :], (8, 128)), 68, 1, stride=8, stride_axis=0
        )

    b, a = vals[0], vals[3]
    up, down = rl(b, 127), rl(a, 1)
    up = jnp.where(mk["last"], jnp.where(mk["ct0"], rs(up, 6), inject(16 * i + k)), up)
    down = jnp.where(mk["first"], jnp.where(mk["ct0"], inject(16 * i + 12 + k), rs(down, 2)), down)
    return [b + down, vals[1], vals[2], a + up]


def assemble(f, beside, strip, mk, put, planes=(0, 1, 2, 3)):
    for i in planes:
        for k in range(4):
            for j, total in enumerate(assembled(f, beside, strip, i, k, mk)):
                put(16 * i + 4 * j + k, total)


def not_shared(n, x, mk):
    if n < 16:
        return jnp.where(mk["even"], 0.0, x)
    if n >= 48:
        return jnp.where(mk["even"], x, 0.0)
    return x


def strip_lines(x, cf, base):
    along_j, along_k = [], []
    for i in range(len(x) // 2):
        a, b = x[2 * i], x[2 * i + 1]
        terms = (a, rs(a, 4), b, rs(b, 4))
        for out in range(2):
            along_j.append(sum(cf[base + 4 * out + t] * terms[t] for t in range(4)))
    for y in x:
        along_k.append(
            sum(cf[base + 8 + d] * (rs(y, (3 - d) % 8) if d != 3 else y) for d in range(7))
        )
    return along_j, along_k


def strip_forces(us, mods, cf):
    x = [us[8 * v : 8 * v + 8] for v in range(8)]
    gj, gk = strip_lines(x, cf, 0)
    gi = [None] * 8
    for e in range(2):
        for i, g in enumerate(d_line(*[x[2 * m + e] for m in range(4)])):
            gi[2 * i + e] = g
    ti, tj, tk = (
        [mods[64 * d + 8 * v : 64 * d + 8 * v + 8] * g[v] for v in range(8)]
        for d, g in enumerate((gi, gj, gk))
    )
    fj = strip_lines(tj, cf, 15)[0]
    fk = strip_lines(tk, cf, 15)[1]
    f = [fj[v] + fk[v] for v in range(8)]
    for e in range(2):
        for i, o in enumerate(dt_line(*[ti[2 * m + e] for m in range(4)])):
            f[2 * i + e] = f[2 * i + e] + o
    return jnp.concatenate(f, axis=0)


def row_zero(rows):
    return ((lane_iota(rows) // 8) % 2) == 1


def strip_faces(f):
    return jnp.where(row_zero(16), f[0:16], f[48:64])


def strip_beside(from_right, from_left, base):
    r = jnp.concatenate([from_right[base], from_right[base + 1]], axis=0)
    l = jnp.concatenate([from_left[base], from_left[base + 1]], axis=0)
    both = jnp.where(row_zero(16), rl(l, 8), rl(r, 120))
    return both, rl(both, 64)


def strip_send(send, base, x, y):
    both = jnp.where(lane_iota(16) < 64, x, rl(y, 64))
    for p in range(2):
        send.put(base + p, both[8 * p : 8 * p + 8], both[8 * p : 8 * p + 8])


def strip_response(delta, diagonal, mod_j, mod_k, cf):
    x = [delta[0:8], delta[8:16]]
    gj, gk = strip_lines(x, cf, 0)
    fj = strip_lines([mod_j[8 * v : 8 * v + 8] * gj[v] for v in range(2)], cf, 15)[0]
    fk = strip_lines([mod_k[8 * v : 8 * v + 8] * gk[v] for v in range(2)], cf, 15)[1]
    return diagonal * delta + jnp.concatenate([fj[v] + fk[v] for v in range(2)], axis=0)


def strip_x(f, beside):
    zero = row_zero(16)
    b, a = f[0:16], f[48:64]
    na = a + jnp.where(zero, rl(b, 8), beside)
    nb = b + jnp.where(zero, beside, rl(a, 120))
    return jnp.concatenate([nb, f[16:48], na], axis=0)


def strip_y(f):
    low = sub_iota() < 4
    parts = []
    for i in range(4):
        x, y = f[16 * i : 16 * i + 8], f[16 * i + 8 : 16 * i + 16]
        parts.append(x + jnp.where(low, rs(rl(y, 1), 4), 0.0))
        parts.append(y + jnp.where(low, 0.0, rs(rl(x, 127), 4)))
    return jnp.concatenate(parts, axis=0)


def inverse_mass(m):
    return jnp.where(m > 0.5, PUSH / jnp.where(m > 0.5, m, 1.0), 0.0)


def strip_not_shared(x):
    zero = row_zero(16)
    return jnp.concatenate(
        [jnp.where(zero, 0.0, x[0:16]), x[16:48], jnp.where(zero, x[48:64], 0.0)], axis=0
    )


def strip_arrays(z1, z2):
    q = lane_iota(64) // 32

    def two(a, b):
        return jnp.where(q == 0, a, jnp.where(q == 1, b, 0.0))

    us = two(z1, z1)
    m0 = two(rl(z1, 64), rl(z1, 96))
    m1 = two(rl(z1, 32), rl(z1, 64))
    m2 = two(z2, rl(z2, 32))
    mass = two(rl(z2, 96), z2)
    return us, jnp.concatenate([m0, m1, m2], axis=0), mass


def state_expand(xu, xw, mk):
    return jnp.where(mk["lo"], xu, rs(xw, 4)), jnp.where(mk["lo"], rs(xu, 4), xw)


def tile(ref, p):
    return ref[8 * p : 8 * p + 8, :]


def first_kernel(
    u_hbm, w_hbm, mod_hbm, mass_hbm, owner_hbm, cf_hbm, z_ref, base_ref, head_ref,
    u_ref, w_ref, m_ref, mass_ref, owner_ref, cf_ref, sems,
):
    state_ref, f_ref = base_ref.at[U0:OWNER], head_ref.at[F0:MASS]
    mass2_ref, const_ref = head_ref.at[MASS:FACES], head_ref.at[FACES:HEAD]
    copies = [
        pltpu.make_async_copy(src, dst, sems.at[i])
        for i, (src, dst) in enumerate(
            (
                (u_hbm, u_ref), (w_hbm, w_ref), (mod_hbm, m_ref), (mass_hbm, mass_ref),
                (owner_hbm, owner_ref), (cf_hbm, cf_ref),
            )
        )
    ]
    for c in copies:
        c.start()
    for c in copies:
        c.wait()
    mk = masks()
    lane = lane_iota(64)
    pieces = (
        (w_ref, 0, 0, 0),
        (u_ref, 0, 0, 1),
        (m_ref, 0, 0, 2),
        (m_ref, 256, 0, 3),
        (m_ref, 512, 1, 0),
        (mass_ref, 0, 1, 1),
    )
    z = [jnp.zeros((64, 128), jnp.float32), jnp.zeros((64, 128), jnp.float32)]
    for ref, base, half, slot in pieces:
        for side in range(2):
            for r in range(2):
                rows = ref[pl.ds(base + 2 * (1 - side) + r, 64, stride=4), :]
                dest = slot * 32 + (1 - side) * 16 + (1 - r) * 8 + (3 if side else 1)
                src = 0 if side else 124
                moved = rl(rows, (dest - src) % 128)
                z[half] = jnp.where((lane >= dest) & (lane < dest + 4), moved, z[half])
    z_ref[0] = z[0]
    z_ref[1] = z[1]
    for p in range(32):
        a, b = state_expand(tile(u_ref, p), tile(w_ref, p), mk)
        state_ref[2 * p] = a
        state_ref[2 * p + 1] = b
        mass2_ref[2 * p] = expanded(tile(mass_ref, p), 0, mk)
        mass2_ref[2 * p + 1] = expanded(tile(mass_ref, p), 1, mk)

    def moduli(direction):
        def get(n):
            at = 64 * direction + n
            return expanded(tile(m_ref, at // 2), at % 2, mk)

        return get

    for q in range(16):
        mi = [moduli(0)(16 * i + q) for i in range(4)]
        diagonal = [sum(float(DERIVATIVE[i, e] ** 2) * mi[i] for i in range(4)) for e in (0, 3)]
        diagonal = jnp.where(mk["even"], diagonal[0], diagonal[1])
        own_mass = face_tile(lambda n: mass2_ref[n], q, mk)
        const_ref[q] = jnp.where(mk["lo"], own_mass, diagonal)
        const_ref[16 + q] = jnp.where(
            mk["lo"], face_tile(moduli(1), q, mk), face_tile(moduli(2), q, mk)
        )
    forces(lambda n: state_ref[n], into(f_ref), lambda p: tile(m_ref, p), mk)
    owner = owner_ref[...].astype(jnp.float32)
    base_ref[OWNER] = jnp.concatenate([owner, owner], axis=0)
    for t in range(WEIGHTS, BASE):
        base_ref[t] = cf_ref[t - WEIGHTS]


def open_kernel(
    place_ref, z_ref, base_ref, head_ref, mod_ref,
    far_ref, near_ref, u1_ref, v1_ref, inv_ref, strip_ref, smod_ref,
    f, sx,
):
    u0_ref, f0_ref = base_ref.at[U0:OWNER], head_ref.at[F0:MASS]
    mass2_ref, const_ref = head_ref.at[MASS:FACES], head_ref.at[FACES:HEAD]
    cf_ref = base_ref.at[WEIGHTS:BASE]
    mk = masks()
    sub = place_ref[0]
    send = Send(far_ref, near_ref, place_ref[1] == 1)
    lane = lane_iota(64)
    side0 = ((lane // 16) % 2) == 1
    c = lane % 8
    below, above = jnp.maximum(sub - 1, 0), jnp.minimum(sub + 1, 3)
    zs = []
    for half in range(2):
        own = z_ref[sub, half]
        zl = jnp.where(sub > 0, z_ref[below, half], 0.0)
        zr = jnp.where(sub < 3, z_ref[above, half], 0.0)
        low = jnp.where(c == 0, 0.0, jnp.where(c <= 4, zl, rl(own, 18)))
        high = jnp.where(c <= 2, rl(own, 110), jnp.where(c == 7, 0.0, zr))
        zs.append(jnp.where(side0, low, high))
    us, mods, smass = strip_arrays(zs[0], zs[1])
    fs = strip_forces(us, mods, cf_ref)
    smod_ref[...] = mods
    strip_ref[0] = us
    strip_ref[1] = fs
    strip_ref[2] = smass
    zero = row_zero(16)
    diagonal = [
        sum(float(DERIVATIVE[i, e] ** 2) * mods[16 * i : 16 * i + 16] for i in range(4))
        for e in (0, 3)
    ]
    strip_send(
        send, STRIP + 2, strip_faces(smass), jnp.where(zero, *diagonal)
    )
    strip_send(
        send, STRIP + 4, strip_faces(mods[64:128]), strip_faces(mods[128:192])
    )
    sm = strip_x(smass, 0.0)
    sx[0] = sm
    fx = strip_x(fs, 0.0)
    sx[1] = fx
    sinv = strip_not_shared(inverse_mass(strip_y(sm)))
    partial = strip_forces(us - sinv * strip_y(fx), mods, cf_ref)
    strip_send(send, STRIP, strip_faces(fs), strip_faces(partial))

    def put_mass(n, total):
        inv_ref[n] = not_shared(n, inverse_mass(total), mk)

    assemble(lambda n: mass2_ref[n], None, sx.at[0], mk, put_mass)

    def put(n, total):
        vel = -inv_ref[n] * total
        v1_ref[n] = vel
        u1_ref[n] = u0_ref[n] + vel

    assemble(lambda n: f0_ref[n], None, sx.at[1], mk, put)
    forces(lambda n: u1_ref[n], into(f), lambda p: mod_ref[p], mk, planes=(0, 3))
    pack_faces(send, 0, lambda q: face_tile(lambda n: f0_ref[n], q, mk), mk)
    pack_faces(send, 8, lambda q: face_tile(lambda n: f[n], q, mk), mk)
    pack_faces(send, CONST, lambda q: const_ref[q], mk)
    pack_faces(send, CONST + 8, lambda q: const_ref[16 + q], mk)


def rim(n):
    return n if n < 16 else n - 32


def middle_kernel(
    place_ref, far_in, near_in, base_ref, head_ref, u1p_ref, v1p_ref, invp_ref, strip_ref, smod_ref,
    mod_ref,
    far_ref, near_ref, inv_ref, u1_ref, u2_ref, rims_ref, inner_ref, resp_ref, sresp_ref, sstate_ref,
    v1, f, v2_ref, f2_ref, u3_ref, sx, beside,
):
    u0_ref, f0_ref = base_ref.at[U0:OWNER], head_ref.at[F0:MASS]
    mass2_ref, cf_ref = head_ref.at[MASS:FACES], base_ref.at[WEIGHTS:BASE]
    mk = masks()
    odd = place_ref[1] == 1
    mr_ref, ml_ref = Receive(far_in, near_in, odd), Receive(near_in, far_in, odd)
    send = Send(far_ref, near_ref, odd)
    lo = mk["lo"]
    us, fs, smass = strip_ref[0], strip_ref[1], strip_ref[2]
    mods = smod_ref[...]
    sf0, sp1 = strip_beside(mr_ref, ml_ref, STRIP)
    smn, sresp0 = strip_beside(mr_ref, ml_ref, STRIP + 2)
    sresp1, sresp2 = strip_beside(mr_ref, ml_ref, STRIP + 4)
    sresp_ref[0] = sresp0
    sresp_ref[1] = sresp1
    sresp_ref[2] = sresp2
    for q in range(16):
        x = unpack_face(mr_ref, ml_ref, CONST, q, mk)
        r = rs(x, 4)
        beside[q] = jnp.where(lo, x, r)
        resp_ref[0, q] = jnp.where(lo, r, x)
        x = unpack_face(mr_ref, ml_ref, CONST + 8, q, mk)
        r = rs(x, 4)
        resp_ref[1, q] = jnp.where(lo, x, r)
        resp_ref[2, q] = jnp.where(lo, r, x)
    responses = [lambda q, d=d: resp_ref[d, q] for d in range(3)]
    sm = strip_x(smass, smn)
    sx[0] = sm
    sinv = inverse_mass(strip_y(sm))
    for n in range(16, 48):
        inv_ref[n] = invp_ref[n]
        u1_ref[n] = u1p_ref[n]
        v1[n] = v1p_ref[n]

    def put_mass(n, total):
        inv_ref[n] = inverse_mass(total)

    assemble(lambda n: mass2_ref[n], lambda q: beside[q], sx.at[0], mk, put_mass, (0, 3))
    fs = strip_x(fs, sf0)
    sx[1] = fs
    svel = -sinv * strip_y(fs)
    us = us + svel

    def put0(n, total):
        vel = -inv_ref[n] * total
        v1[n] = vel
        u1_ref[n] = u0_ref[n] + vel

    assemble(
        lambda n: f0_ref[n], lambda q: unpack_face(mr_ref, ml_ref, 0, q, mk), sx.at[1], mk, put0,
        (0, 3),
    )
    forces(lambda n: u1_ref[n], into(f), lambda p: mod_ref[p], mk)
    delta = [face_tile(lambda n: v1[n], q, mk) for q in range(16)]
    for q, x in enumerate(face_response(delta, *responses)):
        beside[q] = unpack_face(mr_ref, ml_ref, 8, q, mk) + x
    sbeside = sp1 + strip_response(strip_faces(svel), sresp0, sresp1, sresp2, cf_ref)
    fs = strip_x(strip_forces(us, mods, cf_ref), sbeside)
    sx[2] = fs
    svel = svel - sinv * strip_y(fs)
    us = us + svel

    def put1(n, total):
        vel = v1[n] - inv_ref[n] * total
        v2_ref[n] = vel
        u2_ref[n] = u1_ref[n] + vel

    assemble(lambda n: f[n], lambda q: beside[q], sx.at[2], mk, put1)
    forces(lambda n: u2_ref[n], into(f2_ref), lambda p: mod_ref[p], mk)
    fs = strip_forces(us, mods, cf_ref)
    sstate_ref[0] = us
    sstate_ref[1] = svel
    sstate_ref[2] = fs
    sstate_ref[3] = sinv
    fx = strip_x(fs, 0.0)
    sx[3] = fx
    partial = strip_forces(
        us + (svel - strip_not_shared(sinv) * strip_y(fx)), mods, cf_ref
    )

    def put2(n, total):
        vel = v2_ref[n] - not_shared(n, inv_ref[n], mk) * total
        u3_ref[n] = u2_ref[n] + vel
        if 16 <= n < 48:
            inner_ref[0, n - 16] = u3_ref[n]
            inner_ref[1, n - 16] = vel

    assemble(lambda n: f2_ref[n], None, sx.at[3], mk, put2)
    for n in list(range(16)) + list(range(48, 64)):
        rims_ref[0, rim(n)] = v2_ref[n]
        rims_ref[1, rim(n)] = f2_ref[n]
    forces(lambda n: u3_ref[n], into(f), lambda p: mod_ref[p], mk, planes=(0, 3))
    pack_faces(send, 0, lambda q: face_tile(lambda n: f2_ref[n], q, mk), mk)
    pack_faces(send, 8, lambda q: face_tile(lambda n: f[n], q, mk), mk)
    strip_send(send, STRIP_B, strip_faces(fs), strip_faces(partial))


def three_way(x):
    hi = x.astype(jnp.bfloat16)
    rest = x - hi.astype(jnp.float32)
    mid = rest.astype(jnp.bfloat16)
    return hi, mid, (rest - mid.astype(jnp.float32)).astype(jnp.bfloat16)


def density_kernel(
    mod_ref, base_ref, u1_ref, u2_ref, basis_ref, d2_ref, x0_ref, x1_ref, hot_ref, stack_ref
):
    mk = masks()
    lo = mk["lo"]
    for direction in (2, 1, 0):
        for a in range(4):
            for b in range(4):
                nodes = line_nodes(direction, a, b)
                g0 = d_line(*[base_ref[U0 + n] for n in nodes])
                g1 = d_line(*[u1_ref[n] for n in nodes])
                g2 = d_line(*[u2_ref[n] for n in nodes])
                for e, n in enumerate(nodes):
                    at = 64 * direction + n
                    m = expanded(mod_ref[at // 2], at % 2, mk)
                    x0_ref[at] = jnp.where(lo, m * rs(g0[e], 4), 0.0)
                    x1_ref[at] = m * rs(g1[e], 4)
                    t = jnp.where(lo, m * g2[e] * rs(g2[e], 4), 0.0)
                    d2_ref[n] = t if direction == 2 else d2_ref[n] + t
    block = lax.broadcasted_iota(jnp.int32, (512, 128), 0).astype(jnp.float32)
    for s in range(4):
        owner = jnp.broadcast_to(base_ref[OWNER][s : s + 1, :], (512, 128))
        hot_ref[:, 128 * s : 128 * s + 128] = (
            (block == owner).astype(jnp.float32).astype(jnp.bfloat16)
        )
    b0, b1, b2 = three_way(basis_ref[...])
    stack_ref[...] = jnp.concatenate([b0, b1, b0, b1, b0, b2], axis=1)


def last_kernel(
    place_ref, far_in, near_in, mod_ref, inv_ref, u2_ref, rims_ref, inner_ref, resp_ref,
    sresp_ref, sstate_ref, smod_ref, d2_ref, x0_ref, x1_ref, hot_ref, base_ref,
    out_u_ref, out_w_ref, sums_ref,
    u, v, f, sx, beside, dens,
):
    cf_ref = base_ref.at[WEIGHTS:BASE]
    mk = masks()
    odd = place_ref[1] == 1
    br_ref, bl_ref = Receive(far_in, near_in, odd), Receive(near_in, far_in, odd)
    lo = mk["lo"]
    mods = smod_ref[...]
    us, svel, fs, sinv = sstate_ref[0], sstate_ref[1], sstate_ref[2], sstate_ref[3]
    sf2, sp3 = strip_beside(br_ref, bl_ref, STRIP_B)
    fs = strip_x(fs, sf2)
    sx[0] = fs
    spush = -sinv * strip_y(fs)
    us = us + (svel + spush)
    for n in range(16, 48):
        u[n] = inner_ref[0, n - 16]
        v[n] = inner_ref[1, n - 16]

    def put2(n, total):
        vel = rims_ref[0, rim(n)] - inv_ref[n] * total
        v[n] = vel
        u[n] = u2_ref[n] + vel

    assemble(
        lambda n: rims_ref[1, rim(n)], lambda q: unpack_face(br_ref, bl_ref, 0, q, mk), sx.at[0],
        mk, put2, (0, 3),
    )

    def add_third(direction, n, g):
        at = pl.ds(8 * n, 8)
        before = d2_ref[n] if direction == 2 else dens[at, :]
        dens[at, :] = before + x1_ref[64 * direction + n] * g

    forces(lambda n: u[n], into(f), lambda p: mod_ref[p], mk, hook=add_third)
    delta = [face_tile(lambda n: v[n] - rims_ref[0, rim(n)], q, mk) for q in range(16)]
    for q, x in enumerate(face_response(delta, *[lambda q, d=d: resp_ref[d, q] for d in range(3)])):
        beside[q] = unpack_face(br_ref, bl_ref, 8, q, mk) + x
    sbeside = sp3 + strip_response(
        strip_faces(spush), sresp_ref[0], sresp_ref[1], sresp_ref[2], cf_ref
    )
    sx[1] = strip_x(strip_forces(us, mods, cf_ref), sbeside)

    def put3(n, total):
        u[n] = u[n] + (v[n] - inv_ref[n] * total)

    assemble(lambda n: f[n], lambda q: beside[q], sx.at[1], mk, put3)
    for direction in (2, 1, 0):
        for a in range(4):
            for b in range(4):
                nodes = line_nodes(direction, a, b)
                for n, g in zip(nodes, d_line(*[u[n] for n in nodes])):
                    at = pl.ds(8 * n, 8)
                    dens[at, :] = dens[at, :] + x0_ref[64 * direction + n] * g
    cols = [
        dens[pl.ds(s, 64, stride=8), :] + dens[pl.ds(s + 4, 64, stride=8), :] for s in range(4)
    ]
    split = jnp.concatenate(three_way(jnp.concatenate(cols, axis=1)), axis=0)
    res = lax.dot_general(
        split, hot_ref[...], (((1,), (1,)), ((), ())), preferred_element_type=jnp.float32
    )
    sums = res[0:64] + (res[64:128] + res[128:192])
    for q in range(4):
        sums_ref[q] = sums[:, 128 * q : 128 * q + 128]
    for p in range(32):
        a, b = u[2 * p], u[2 * p + 1]
        out_u_ref[p] = jnp.where(lo, a, rs(b, 4))
        out_w_ref[p] = jnp.where(lo, rs(a, 4), b)


def project_kernel(place_ref, x_ref, stack_ref, out_ref):
    sub = place_ref[0]
    total = (x_ref[0, sub] + x_ref[1, sub]) + (x_ref[2, sub] + x_ref[3, sub])
    t0, t1, t2 = three_way(total)
    out_ref[...] = KERNEL_SCALE * jnp.dot(
        stack_ref[...], jnp.concatenate([t0, t0, t1, t1, t2, t0], axis=0),
        preferred_element_type=jnp.float32,
    )


VMEM = pl.BlockSpec(memory_space=pltpu.VMEM)
SMEM = pl.BlockSpec(memory_space=pltpu.SMEM)
HBM = pl.BlockSpec(memory_space=pltpu.HBM)
F32, BF16 = jnp.float32, jnp.bfloat16


def call(kernel, outs, ins, scratch=(), specs=(), limit=24, space=None):
    specs = list(specs) + [VMEM] * (len(ins) - len(specs))
    outs = [o if isinstance(o, jax.ShapeDtypeStruct) else jax.ShapeDtypeStruct(o, F32) for o in outs]
    if space is not None:
        outs = [space(o.shape, o.dtype) for o in outs]
    return pl.pallas_call(
        kernel,
        out_shape=outs,
        in_specs=specs,
        out_specs=[VMEM] * len(outs),
        scratch_shapes=list(scratch),
        compiler_params=pltpu.CompilerParams(vmem_limit_bytes=limit * 1024 * 1024),
    )(*ins)


def raw_tiles(x):
    lead = int(np.prod(x.shape[:-2]))
    return x.reshape(lead, 2, 2, 128).transpose(0, 2, 1, 3).reshape(lead * 4, 128)


def from_tiles(x):
    return x.reshape(64, 2, 2, 128).transpose(0, 2, 1, 3).reshape(64, 2, 256)


def on_device(initial_field, adjoint_source, moduli, node_mass, block_owner, spline_basis):
    count = lax.axis_size("dom")
    near_pairs = [(i, i ^ 1) for i in range(count)]
    far_pairs = [(i, ((i + 1) ^ 1) - 1) for i in range(1, count - 1)]
    cf = jnp.asarray(COEFFICIENTS)
    place = jnp.stack([lax.axis_index("sub"), lax.axis_index("dom") & 1]).astype(jnp.int32)
    u2d, w2d, m2d, mass2d = map(raw_tiles, (initial_field, adjoint_source, moduli, node_mass))
    owner = raw_tiles(block_owner[None])
    mod = m2d.reshape(96, 8, 128)
    full, face = (64, 8, 128), (16, 8, 128)

    def swap_rows(far, near):
        return lax.ppermute(far, "dom", far_pairs), lax.ppermute(near, "dom", near_pairs)

    edges, base, head = call(
        first_kernel,
        [(2, 64, 128), (BASE, 8, 128), (HEAD, 8, 128)],
        [u2d, w2d, m2d, mass2d, owner, cf],
        [pltpu.VMEM((n, 128), F32) for n in (256, 256, 768, 256)]
        + [pltpu.VMEM((4, 128), jnp.int32), pltpu.VMEM((BASE - WEIGHTS, 8, 128), F32)]
        + [pltpu.SemaphoreType.DMA((6,))],
        [HBM] * 6,
        limit=FIRST_LIMIT,
        space=pltpu.VMEM,
    )
    edges = lax.all_gather(edges, "sub")
    far, near, u1p, v1p, invp, strips, smod = call(
        open_kernel,
        [(MSG, 8, 128), (MSG, 8, 128), full, full, full, (3, 64, 128), (192, 128)],
        [place, edges, base, head, mod],
        [pltpu.VMEM(full, F32), pltpu.VMEM((2, 64, 128), F32)],
        specs=[SMEM],
        space=pltpu.VMEM,
    )
    far, near = swap_rows(far, near)
    far, near, inv, u1, u2, rims, inner, resp, sresp, sstate = call(
        middle_kernel,
        [
            (MSG_B, 8, 128), (MSG_B, 8, 128), full, full, full, (2, 32, 8, 128),
            (2, 32, 8, 128), (3, 16, 8, 128), (3, 16, 128), (4, 64, 128),
        ],
        [place, far, near, base, head, u1p, v1p, invp, strips, smod, mod],
        [pltpu.VMEM(full, F32)] * 5 + [pltpu.VMEM((4, 64, 128), F32), pltpu.VMEM(face, F32)],
        specs=[SMEM],
        space=pltpu.VMEM,
    )
    far, near = swap_rows(far, near)
    wide = jax.ShapeDtypeStruct((512, 512), BF16)
    d2, x0, x1, hot, stack = call(
        density_kernel,
        [full, (192, 8, 128), (192, 8, 128), wide, jax.ShapeDtypeStruct((64, 384), BF16)],
        [mod, base, u1, u2, spline_basis.T],
        space=pltpu.VMEM,
    )
    out_u, out_w, sums = call(
        last_kernel,
        [(32, 8, 128), (32, 8, 128), (4, 64, 128)],
        [
            place, far, near, mod, inv, u2, rims, inner, resp, sresp, sstate, smod,
            d2, x0, x1, hot, base,
        ],
        [pltpu.VMEM(full, F32)] * 3
        + [pltpu.VMEM((2, 64, 128), F32), pltpu.VMEM(face, F32), pltpu.VMEM((512, 128), F32)],
        specs=[SMEM],
    )
    sums = lax.all_gather(sums, "sub")
    (kernel,) = call(project_kernel, [(64, 128)], [place, sums, stack], specs=[SMEM])
    return from_tiles(out_u), from_tiles(out_w), kernel


def solution(mesh):
    in_specs = (
        P(None, "dom", "sub"),
        P(None, "dom", "sub"),
        P(None, None, "dom", "sub"),
        P(None, "dom", "sub"),
        P("dom", "sub"),
        P(),
    )
    out_specs = (P(None, "dom", "sub"), P(None, "dom", "sub"), P(None, ("dom", "sub")))
    return jax.shard_map(
        on_device, mesh=mesh, in_specs=in_specs, out_specs=out_specs, check_vma=False
    )
```

```python
import jax
import jax.numpy as jnp
import numpy as np
from jax import lax
from jax.experimental import pallas as pl
from jax.experimental.pallas import tpu as pltpu
from jax.sharding import PartitionSpec as P

STEPS = 4
TIME_STEP = 0.1
KERNEL_SCALE = 0.05
PUSH = TIME_STEP * TIME_STEP

DERIVATIVE = np.array(
    [
        [-3.0, 4.04508497187474, -1.54508497187474, 0.5],
        [-0.80901699437495, 0.0, 1.11803398874989, -0.30901699437495],
        [0.30901699437495, -1.11803398874989, 0.0, 0.80901699437495],
        [-0.5, 1.54508497187474, -4.04508497187474, 3.0],
    ]
)
HALF_AMB = float((DERIVATIVE[0, 1] - DERIVATIVE[0, 2]) / 2)
HALF_CME = float((DERIVATIVE[1, 0] - DERIVATIVE[1, 3]) / 2)
HALF_D = float(DERIVATIVE[1, 2] / 2)

MSG, CONST, STRIP = 38, 16, 32
MSG_B, STRIP_B = 18, 16
FIRST_LIMIT = 54
U0, OWNER, WEIGHTS, BASE = 0, 64, 65, 95
F0, MASS, FACES, HEAD = 0, 64, 128, 160


def strip_coefficients():
    tiles = []
    for d in (DERIVATIVE, DERIVATIVE.T):
        for out in range(2):
            for term in range(4):
                col = np.zeros(8)
                for s in range(8):
                    j = 2 * out + s // 4
                    half = s // 4 if term % 2 == 0 else 1 - s // 4
                    col[s] = d[j, 2 * (term // 2) + half]
                tiles.append(col)
        for delta in range(-3, 4):
            col = np.zeros(8)
            for s in range(8):
                k = s % 4
                if 0 <= k + delta < 4:
                    col[s] = d[k, k + delta]
            tiles.append(col)
    return np.broadcast_to(np.array(tiles, np.float32)[:, :, None], (30, 8, 128))


COEFFICIENTS = np.ascontiguousarray(strip_coefficients())


def sub_iota():
    return lax.broadcasted_iota(jnp.int32, (8, 128), 0)


def lane_iota(rows=8):
    return lax.broadcasted_iota(jnp.int32, (rows, 128), 1)


def rs(x, shift):
    return pltpu.roll(x, shift, 0)


def rl(x, shift):
    return pltpu.roll(x, shift, 1)


def masks():
    s = sub_iota()
    lane = lane_iota()
    return dict(
        even=(s % 2) == 0,
        lo=s < 4,
        ct0=((s // 2) % 2) == 0,
        first=lane == 0,
        last=lane == 127,
    )


def d_line(x0, x1, x2, x3):
    p, m, q, n = x0 + x3, x0 - x3, x1 + x2, x1 - x2
    r = q - p
    s1 = -1.75 * m + HALF_AMB * n
    s2 = HALF_CME * m - HALF_D * n
    r1, r2 = 1.25 * r, HALF_D * r
    return s1 + r1, s2 + r2, s2 - r2, s1 - r1


def dt_line(x0, x1, x2, x3):
    p, m, q, n = x0 + x3, x0 - x3, x1 + x2, x1 - x2
    t = 1.25 * m + HALF_D * n
    q1 = HALF_CME * q - 1.75 * p
    q2 = HALF_AMB * p - HALF_D * q
    return q1 - t, t + q2, t - q2, -(q1 + t)


def line_nodes(direction, a, b):
    if direction == 0:
        return [16 * i + 4 * a + b for i in range(4)]
    if direction == 1:
        return [16 * a + 4 * j + b for j in range(4)]
    return [16 * a + 4 * b + k for k in range(4)]


def expanded(x, upper, mk):
    r = rs(x, 4)
    return jnp.where(mk["lo"], r, x) if upper else jnp.where(mk["lo"], x, r)


def forces(u, f, mod, mk, planes=(0, 1, 2, 3), hook=None):
    for direction in (2, 1, 0):
        for a in range(4):
            if direction and a not in planes:
                continue
            for b in range(4):
                nodes = line_nodes(direction, a, b)
                g = d_line(*[u(n) for n in nodes])
                if hook is not None:
                    for n, gn in zip(nodes, g):
                        hook(direction, n, gn)
                t = []
                for n, gn in zip(nodes, g):
                    at = 64 * direction + n
                    t.append(expanded(mod(at // 2), at % 2, mk) * gn)
                for n, o in zip(nodes, dt_line(*t)):
                    if n // 16 in planes:
                        f(n, o, direction == 2)


def into(ref):
    def put(n, value, first):
        ref[n] = value if first else ref[n] + value

    return put


def face_tile(get, q, mk):
    return jnp.where(mk["even"], get(q), get(48 + q))


class Send:
    def __init__(self, far_ref, near_ref, odd):
        self.far, self.near, self.odd = far_ref, near_ref, odd

    def put(self, at, left, right):
        self.far[at] = jnp.where(self.odd, right, left)
        self.near[at] = jnp.where(self.odd, left, right)


class Receive:
    def __init__(self, odd_ref, even_ref, odd):
        self.odd_ref, self.even_ref, self.odd = odd_ref, even_ref, odd

    def __getitem__(self, at):
        return jnp.where(self.odd, self.odd_ref[at], self.even_ref[at])


def pack_faces(send, base, get, mk):
    even = mk["even"]
    for p in range(8):
        x, y = get(2 * p), get(2 * p + 1)
        send.put(base + p, jnp.where(even, x, rs(y, 1)), jnp.where(even, rs(x, 7), y))


def unpack_face(from_right, from_left, base, q, mk):
    r, l = from_right[base + q // 2], from_left[base + q // 2]
    if q % 2:
        return jnp.where(mk["even"], rs(l, 7), r)
    return jnp.where(mk["even"], l, rs(r, 1))


def face_response(delta, diagonal, mod_j, mod_k):
    out = [diagonal(q) * delta[q] for q in range(16)]
    for mod, lines in (
        (mod_j, [[4 * j + k for j in range(4)] for k in range(4)]),
        (mod_k, [[4 * j + k for k in range(4)] for j in range(4)]),
    ):
        for line in lines:
            t = [mod(q) * g for q, g in zip(line, d_line(*[delta[q] for q in line]))]
            for q, o in zip(line, dt_line(*t)):
                out[q] = out[q] + o
    return out


def along_x(f, beside, i, q, mk):
    even = mk["even"]
    x = f(16 * i + q)
    if i in (1, 2):
        return x
    other = beside(q) if beside is not None else 0.0
    if i == 3:
        return x + jnp.where(even, rs(f(q), 7), other)
    return x + jnp.where(even, other, rs(f(48 + q), 1))


def assembled(f, beside, strip, i, k, mk):
    vals = [along_x(f, beside, i, 4 * j + k, mk) for j in range(4)]

    def inject(row):
        return pltpu.roll(
            jnp.broadcast_to(strip[row : row + 1, :], (8, 128)), 68, 1, stride=8, stride_axis=0
        )

    b, a = vals[0], vals[3]
    up, down = rl(b, 127), rl(a, 1)
    up = jnp.where(mk["last"], jnp.where(mk["ct0"], rs(up, 6), inject(16 * i + k)), up)
    down = jnp.where(mk["first"], jnp.where(mk["ct0"], inject(16 * i + 12 + k), rs(down, 2)), down)
    return [b + down, vals[1], vals[2], a + up]


def assemble(f, beside, strip, mk, put, planes=(0, 1, 2, 3)):
    for i in planes:
        for k in range(4):
            for j, total in enumerate(assembled(f, beside, strip, i, k, mk)):
                put(16 * i + 4 * j + k, total)


def not_shared(n, x, mk):
    if n < 16:
        return jnp.where(mk["even"], 0.0, x)
    if n >= 48:
        return jnp.where(mk["even"], x, 0.0)
    return x


def strip_lines(x, cf, base):
    along_j, along_k = [], []
    for i in range(len(x) // 2):
        a, b = x[2 * i], x[2 * i + 1]
        terms = (a, rs(a, 4), b, rs(b, 4))
        for out in range(2):
            along_j.append(sum(cf[base + 4 * out + t] * terms[t] for t in range(4)))
    for y in x:
        along_k.append(
            sum(cf[base + 8 + d] * (rs(y, (3 - d) % 8) if d != 3 else y) for d in range(7))
        )
    return along_j, along_k


def strip_forces(us, mods, cf):
    x = [us[8 * v : 8 * v + 8] for v in range(8)]
    gj, gk = strip_lines(x, cf, 0)
    gi = [None] * 8
    for e in range(2):
        for i, g in enumerate(d_line(*[x[2 * m + e] for m in range(4)])):
            gi[2 * i + e] = g
    ti, tj, tk = (
        [mods[64 * d + 8 * v : 64 * d + 8 * v + 8] * g[v] for v in range(8)]
        for d, g in enumerate((gi, gj, gk))
    )
    fj = strip_lines(tj, cf, 15)[0]
    fk = strip_lines(tk, cf, 15)[1]
    f = [fj[v] + fk[v] for v in range(8)]
    for e in range(2):
        for i, o in enumerate(dt_line(*[ti[2 * m + e] for m in range(4)])):
            f[2 * i + e] = f[2 * i + e] + o
    return jnp.concatenate(f, axis=0)


def row_zero(rows):
    return ((lane_iota(rows) // 8) % 2) == 1


def strip_faces(f):
    return jnp.where(row_zero(16), f[0:16], f[48:64])


def strip_beside(from_right, from_left, base):
    r = jnp.concatenate([from_right[base], from_right[base + 1]], axis=0)
    l = jnp.concatenate([from_left[base], from_left[base + 1]], axis=0)
    both = jnp.where(row_zero(16), rl(l, 8), rl(r, 120))
    return both, rl(both, 64)


def strip_send(send, base, x, y):
    both = jnp.where(lane_iota(16) < 64, x, rl(y, 64))
    for p in range(2):
        send.put(base + p, both[8 * p : 8 * p + 8], both[8 * p : 8 * p + 8])


def strip_response(delta, diagonal, mod_j, mod_k, cf):
    x = [delta[0:8], delta[8:16]]
    gj, gk = strip_lines(x, cf, 0)
    fj = strip_lines([mod_j[8 * v : 8 * v + 8] * gj[v] for v in range(2)], cf, 15)[0]
    fk = strip_lines([mod_k[8 * v : 8 * v + 8] * gk[v] for v in range(2)], cf, 15)[1]
    return diagonal * delta + jnp.concatenate([fj[v] + fk[v] for v in range(2)], axis=0)


def strip_x(f, beside):
    zero = row_zero(16)
    b, a = f[0:16], f[48:64]
    na = a + jnp.where(zero, rl(b, 8), beside)
    nb = b + jnp.where(zero, beside, rl(a, 120))
    return jnp.concatenate([nb, f[16:48], na], axis=0)


def strip_y(f):
    low = sub_iota() < 4
    parts = []
    for i in range(4):
        x, y = f[16 * i : 16 * i + 8], f[16 * i + 8 : 16 * i + 16]
        parts.append(x + jnp.where(low, rs(rl(y, 1), 4), 0.0))
        parts.append(y + jnp.where(low, 0.0, rs(rl(x, 127), 4)))
    return jnp.concatenate(parts, axis=0)


def inverse_mass(m):
    return jnp.where(m > 0.5, PUSH / jnp.where(m > 0.5, m, 1.0), 0.0)


def strip_not_shared(x):
    zero = row_zero(16)
    return jnp.concatenate(
        [jnp.where(zero, 0.0, x[0:16]), x[16:48], jnp.where(zero, x[48:64], 0.0)], axis=0
    )


def strip_arrays(z1, z2):
    q = lane_iota(64) // 32

    def two(a, b):
        return jnp.where(q == 0, a, jnp.where(q == 1, b, 0.0))

    us = two(z1, z1)
    m0 = two(rl(z1, 64), rl(z1, 96))
    m1 = two(rl(z1, 32), rl(z1, 64))
    m2 = two(z2, rl(z2, 32))
    mass = two(rl(z2, 96), z2)
    return us, jnp.concatenate([m0, m1, m2], axis=0), mass


def state_expand(xu, xw, mk):
    return jnp.where(mk["lo"], xu, rs(xw, 4)), jnp.where(mk["lo"], rs(xu, 4), xw)


def tile(ref, p):
    return ref[8 * p : 8 * p + 8, :]


def first_kernel(
    u_hbm, w_hbm, mod_hbm, mass_hbm, owner_hbm, cf_hbm, z_ref, base_ref, head_ref,
    u_ref, w_ref, m_ref, mass_ref, owner_ref, cf_ref, sems,
):
    state_ref, f_ref = base_ref.at[U0:OWNER], head_ref.at[F0:MASS]
    mass2_ref, const_ref = head_ref.at[MASS:FACES], head_ref.at[FACES:HEAD]
    copies = [
        pltpu.make_async_copy(src, dst, sems.at[i])
        for i, (src, dst) in enumerate(
            (
                (u_hbm, u_ref), (w_hbm, w_ref), (mod_hbm, m_ref), (mass_hbm, mass_ref),
                (owner_hbm, owner_ref), (cf_hbm, cf_ref),
            )
        )
    ]
    for c in copies:
        c.start()
    mk = masks()
    lane = lane_iota(64)
    pieces = (
        (w_ref, 0, 0, 0),
        (u_ref, 0, 0, 1),
        (m_ref, 0, 0, 2),
        (m_ref, 256, 0, 3),
        (m_ref, 512, 1, 0),
        (mass_ref, 0, 1, 1),
    )
    z = [jnp.zeros((64, 128), jnp.float32), jnp.zeros((64, 128), jnp.float32)]
    for step, (ref, base, half, slot) in enumerate(pieces):
        for arrival in ((1,), (0,), (2,), (), (), (3,))[step]:
            copies[arrival].wait()
        for side in range(2):
            for r in range(2):
                rows = ref[pl.ds(base + 2 * (1 - side) + r, 64, stride=4), :]
                dest = slot * 32 + (1 - side) * 16 + (1 - r) * 8 + (3 if side else 1)
                src = 0 if side else 124
                moved = rl(rows, (dest - src) % 128)
                z[half] = jnp.where((lane >= dest) & (lane < dest + 4), moved, z[half])
    z_ref[0] = z[0]
    z_ref[1] = z[1]
    for p in range(32):
        a, b = state_expand(tile(u_ref, p), tile(w_ref, p), mk)
        state_ref[2 * p] = a
        state_ref[2 * p + 1] = b
        mass2_ref[2 * p] = expanded(tile(mass_ref, p), 0, mk)
        mass2_ref[2 * p + 1] = expanded(tile(mass_ref, p), 1, mk)

    def moduli(direction):
        def get(n):
            at = 64 * direction + n
            return expanded(tile(m_ref, at // 2), at % 2, mk)

        return get

    for q in range(16):
        mi = [moduli(0)(16 * i + q) for i in range(4)]
        diagonal = [sum(float(DERIVATIVE[i, e] ** 2) * mi[i] for i in range(4)) for e in (0, 3)]
        diagonal = jnp.where(mk["even"], diagonal[0], diagonal[1])
        own_mass = face_tile(lambda n: mass2_ref[n], q, mk)
        const_ref[q] = jnp.where(mk["lo"], own_mass, diagonal)
        const_ref[16 + q] = jnp.where(
            mk["lo"], face_tile(moduli(1), q, mk), face_tile(moduli(2), q, mk)
        )
    forces(lambda n: state_ref[n], into(f_ref), lambda p: tile(m_ref, p), mk)
    copies[4].wait()
    copies[5].wait()
    owner = owner_ref[...].astype(jnp.float32)
    base_ref[OWNER] = jnp.concatenate([owner, owner], axis=0)
    for t in range(WEIGHTS, BASE):
        base_ref[t] = cf_ref[t - WEIGHTS]


def open_kernel(
    odd_ref, sub_ref, z_ref, base_ref, head_ref, mod_ref,
    far_ref, near_ref, u1_ref, v1_ref, inv_ref, strip_ref, smod_ref,
    f, sx,
):
    u0_ref, f0_ref = base_ref.at[U0:OWNER], head_ref.at[F0:MASS]
    mass2_ref, const_ref = head_ref.at[MASS:FACES], head_ref.at[FACES:HEAD]
    cf_ref = base_ref.at[WEIGHTS:BASE]
    mk = masks()
    sub = sub_ref[0]
    send = Send(far_ref, near_ref, odd_ref[0] == 1)
    lane = lane_iota(64)
    side0 = ((lane // 16) % 2) == 1
    c = lane % 8
    below, above = jnp.maximum(sub - 1, 0), jnp.minimum(sub + 1, 3)
    zs = []
    for half in range(2):
        own = z_ref[sub, half]
        zl = jnp.where(sub > 0, z_ref[below, half], 0.0)
        zr = jnp.where(sub < 3, z_ref[above, half], 0.0)
        low = jnp.where(c == 0, 0.0, jnp.where(c <= 4, zl, rl(own, 18)))
        high = jnp.where(c <= 2, rl(own, 110), jnp.where(c == 7, 0.0, zr))
        zs.append(jnp.where(side0, low, high))
    us, mods, smass = strip_arrays(zs[0], zs[1])
    fs = strip_forces(us, mods, cf_ref)
    smod_ref[...] = mods
    strip_ref[0] = us
    strip_ref[1] = fs
    strip_ref[2] = smass
    zero = row_zero(16)
    diagonal = [
        sum(float(DERIVATIVE[i, e] ** 2) * mods[16 * i : 16 * i + 16] for i in range(4))
        for e in (0, 3)
    ]
    strip_send(
        send, STRIP + 2, strip_faces(smass), jnp.where(zero, *diagonal)
    )
    strip_send(
        send, STRIP + 4, strip_faces(mods[64:128]), strip_faces(mods[128:192])
    )
    sm = strip_x(smass, 0.0)
    sx[0] = sm
    fx = strip_x(fs, 0.0)
    sx[1] = fx
    sinv = strip_not_shared(inverse_mass(strip_y(sm)))
    partial = strip_forces(us - sinv * strip_y(fx), mods, cf_ref)
    strip_send(send, STRIP, strip_faces(fs), strip_faces(partial))

    def put_mass(n, total):
        inv_ref[n] = not_shared(n, inverse_mass(total), mk)

    assemble(lambda n: mass2_ref[n], None, sx.at[0], mk, put_mass)

    def put(n, total):
        vel = -inv_ref[n] * total
        v1_ref[n] = vel
        u1_ref[n] = u0_ref[n] + vel

    assemble(lambda n: f0_ref[n], None, sx.at[1], mk, put)
    forces(lambda n: u1_ref[n], into(f), lambda p: mod_ref[p], mk, planes=(0, 3))
    pack_faces(send, 0, lambda q: face_tile(lambda n: f0_ref[n], q, mk), mk)
    pack_faces(send, 8, lambda q: face_tile(lambda n: f[n], q, mk), mk)
    pack_faces(send, CONST, lambda q: const_ref[q], mk)
    pack_faces(send, CONST + 8, lambda q: const_ref[16 + q], mk)


def rim(n):
    return n if n < 16 else n - 32


def middle_kernel(
    odd_ref, far_in, near_in, base_ref, head_ref, u1p_ref, v1p_ref, invp_ref, strip_ref, smod_ref,
    mod_ref,
    far_ref, near_ref, inv_ref, u1_ref, u2_ref, rims_ref, inner_ref, resp_ref, sresp_ref, sstate_ref,
    v1, f, v2_ref, f2_ref, u3_ref, sx, beside,
):
    u0_ref, f0_ref = base_ref.at[U0:OWNER], head_ref.at[F0:MASS]
    mass2_ref, cf_ref = head_ref.at[MASS:FACES], base_ref.at[WEIGHTS:BASE]
    mk = masks()
    odd = odd_ref[0] == 1
    mr_ref, ml_ref = Receive(far_in, near_in, odd), Receive(near_in, far_in, odd)
    send = Send(far_ref, near_ref, odd)
    lo = mk["lo"]
    us, fs, smass = strip_ref[0], strip_ref[1], strip_ref[2]
    mods = smod_ref[...]
    sf0, sp1 = strip_beside(mr_ref, ml_ref, STRIP)
    smn, sresp0 = strip_beside(mr_ref, ml_ref, STRIP + 2)
    sresp1, sresp2 = strip_beside(mr_ref, ml_ref, STRIP + 4)
    sresp_ref[0] = sresp0
    sresp_ref[1] = sresp1
    sresp_ref[2] = sresp2
    for q in range(16):
        x = unpack_face(mr_ref, ml_ref, CONST, q, mk)
        r = rs(x, 4)
        beside[q] = jnp.where(lo, x, r)
        resp_ref[0, q] = jnp.where(lo, r, x)
        x = unpack_face(mr_ref, ml_ref, CONST + 8, q, mk)
        r = rs(x, 4)
        resp_ref[1, q] = jnp.where(lo, x, r)
        resp_ref[2, q] = jnp.where(lo, r, x)
    responses = [lambda q, d=d: resp_ref[d, q] for d in range(3)]
    sm = strip_x(smass, smn)
    sx[0] = sm
    sinv = inverse_mass(strip_y(sm))
    for n in range(16, 48):
        inv_ref[n] = invp_ref[n]
        u1_ref[n] = u1p_ref[n]
        v1[n] = v1p_ref[n]

    def put_mass(n, total):
        inv_ref[n] = inverse_mass(total)

    assemble(lambda n: mass2_ref[n], lambda q: beside[q], sx.at[0], mk, put_mass, (0, 3))
    fs = strip_x(fs, sf0)
    sx[1] = fs
    svel = -sinv * strip_y(fs)
    us = us + svel

    def put0(n, total):
        vel = -inv_ref[n] * total
        v1[n] = vel
        u1_ref[n] = u0_ref[n] + vel

    assemble(
        lambda n: f0_ref[n], lambda q: unpack_face(mr_ref, ml_ref, 0, q, mk), sx.at[1], mk, put0,
        (0, 3),
    )
    forces(lambda n: u1_ref[n], into(f), lambda p: mod_ref[p], mk)
    delta = [face_tile(lambda n: v1[n], q, mk) for q in range(16)]
    for q, x in enumerate(face_response(delta, *responses)):
        beside[q] = unpack_face(mr_ref, ml_ref, 8, q, mk) + x
    sbeside = sp1 + strip_response(strip_faces(svel), sresp0, sresp1, sresp2, cf_ref)
    fs = strip_x(strip_forces(us, mods, cf_ref), sbeside)
    sx[2] = fs
    svel = svel - sinv * strip_y(fs)
    us = us + svel

    def put1(n, total):
        vel = v1[n] - inv_ref[n] * total
        v2_ref[n] = vel
        u2_ref[n] = u1_ref[n] + vel

    assemble(lambda n: f[n], lambda q: beside[q], sx.at[2], mk, put1)
    forces(lambda n: u2_ref[n], into(f2_ref), lambda p: mod_ref[p], mk)
    fs = strip_forces(us, mods, cf_ref)
    sstate_ref[0] = us
    sstate_ref[1] = svel
    sstate_ref[2] = fs
    sstate_ref[3] = sinv
    fx = strip_x(fs, 0.0)
    sx[3] = fx
    partial = strip_forces(
        us + (svel - strip_not_shared(sinv) * strip_y(fx)), mods, cf_ref
    )

    def put2(n, total):
        vel = v2_ref[n] - not_shared(n, inv_ref[n], mk) * total
        u3_ref[n] = u2_ref[n] + vel
        if 16 <= n < 48:
            inner_ref[0, n - 16] = u3_ref[n]
            inner_ref[1, n - 16] = vel

    assemble(lambda n: f2_ref[n], None, sx.at[3], mk, put2)
    for n in list(range(16)) + list(range(48, 64)):
        rims_ref[0, rim(n)] = v2_ref[n]
        rims_ref[1, rim(n)] = f2_ref[n]
    forces(lambda n: u3_ref[n], into(f), lambda p: mod_ref[p], mk, planes=(0, 3))
    pack_faces(send, 0, lambda q: face_tile(lambda n: f2_ref[n], q, mk), mk)
    pack_faces(send, 8, lambda q: face_tile(lambda n: f[n], q, mk), mk)
    strip_send(send, STRIP_B, strip_faces(fs), strip_faces(partial))


def three_way(x):
    hi = x.astype(jnp.bfloat16)
    rest = x - hi.astype(jnp.float32)
    mid = rest.astype(jnp.bfloat16)
    return hi, mid, (rest - mid.astype(jnp.float32)).astype(jnp.bfloat16)


def density_kernel(
    mod_ref, base_ref, u1_ref, u2_ref, basis_ref, d2_ref, x0_ref, x1_ref, hot_ref, stack_ref
):
    mk = masks()
    lo = mk["lo"]
    for direction in (2, 1, 0):
        for a in range(4):
            for b in range(4):
                nodes = line_nodes(direction, a, b)
                g0 = d_line(*[base_ref[U0 + n] for n in nodes])
                g1 = d_line(*[u1_ref[n] for n in nodes])
                g2 = d_line(*[u2_ref[n] for n in nodes])
                for e, n in enumerate(nodes):
                    at = 64 * direction + n
                    m = expanded(mod_ref[at // 2], at % 2, mk)
                    x0_ref[at] = jnp.where(lo, m * rs(g0[e], 4), 0.0)
                    x1_ref[at] = m * rs(g1[e], 4)
                    t = jnp.where(lo, m * g2[e] * rs(g2[e], 4), 0.0)
                    d2_ref[n] = t if direction == 2 else d2_ref[n] + t
    block = lax.broadcasted_iota(jnp.int32, (512, 128), 0).astype(jnp.float32)
    for s in range(4):
        owner = jnp.broadcast_to(base_ref[OWNER][s : s + 1, :], (512, 128))
        hot_ref[:, 128 * s : 128 * s + 128] = (
            (block == owner).astype(jnp.float32).astype(jnp.bfloat16)
        )
    b0, b1, b2 = three_way(basis_ref[...])
    stack_ref[...] = jnp.concatenate([b0, b1, b0, b1, b0, b2], axis=1)


def last_kernel(
    odd_ref, far_in, near_in, mod_ref, inv_ref, u2_ref, rims_ref, inner_ref, resp_ref,
    sresp_ref, sstate_ref, smod_ref, d2_ref, x0_ref, x1_ref, hot_ref, base_ref,
    out_u_ref, out_w_ref, sums_ref,
    u, v, f, sx, beside, dens,
):
    cf_ref = base_ref.at[WEIGHTS:BASE]
    mk = masks()
    odd = odd_ref[0] == 1
    br_ref, bl_ref = Receive(far_in, near_in, odd), Receive(near_in, far_in, odd)
    lo = mk["lo"]
    mods = smod_ref[...]
    us, svel, fs, sinv = sstate_ref[0], sstate_ref[1], sstate_ref[2], sstate_ref[3]
    sf2, sp3 = strip_beside(br_ref, bl_ref, STRIP_B)
    fs = strip_x(fs, sf2)
    sx[0] = fs
    spush = -sinv * strip_y(fs)
    us = us + (svel + spush)
    for n in range(16, 48):
        u[n] = inner_ref[0, n - 16]
        v[n] = inner_ref[1, n - 16]

    def put2(n, total):
        vel = rims_ref[0, rim(n)] - inv_ref[n] * total
        v[n] = vel
        u[n] = u2_ref[n] + vel

    assemble(
        lambda n: rims_ref[1, rim(n)], lambda q: unpack_face(br_ref, bl_ref, 0, q, mk), sx.at[0],
        mk, put2, (0, 3),
    )

    def add_third(direction, n, g):
        at = pl.ds(8 * n, 8)
        before = d2_ref[n] if direction == 2 else dens[at, :]
        dens[at, :] = before + x1_ref[64 * direction + n] * g

    forces(lambda n: u[n], into(f), lambda p: mod_ref[p], mk, hook=add_third)
    delta = [face_tile(lambda n: v[n] - rims_ref[0, rim(n)], q, mk) for q in range(16)]
    for q, x in enumerate(face_response(delta, *[lambda q, d=d: resp_ref[d, q] for d in range(3)])):
        beside[q] = unpack_face(br_ref, bl_ref, 8, q, mk) + x
    sbeside = sp3 + strip_response(
        strip_faces(spush), sresp_ref[0], sresp_ref[1], sresp_ref[2], cf_ref
    )
    sx[1] = strip_x(strip_forces(us, mods, cf_ref), sbeside)

    def put3(n, total):
        u[n] = u[n] + (v[n] - inv_ref[n] * total)

    assemble(lambda n: f[n], lambda q: beside[q], sx.at[1], mk, put3)
    for direction in (2, 1, 0):
        for a in range(4):
            for b in range(4):
                nodes = line_nodes(direction, a, b)
                for n, g in zip(nodes, d_line(*[u[n] for n in nodes])):
                    at = pl.ds(8 * n, 8)
                    dens[at, :] = dens[at, :] + x0_ref[64 * direction + n] * g
    cols = [
        dens[pl.ds(s, 64, stride=8), :] + dens[pl.ds(s + 4, 64, stride=8), :] for s in range(4)
    ]
    split = jnp.concatenate(three_way(jnp.concatenate(cols, axis=1)), axis=0)
    res = lax.dot_general(
        split, hot_ref[...], (((1,), (1,)), ((), ())), preferred_element_type=jnp.float32
    )
    sums = res[0:64] + (res[64:128] + res[128:192])
    for q in range(4):
        sums_ref[q] = sums[:, 128 * q : 128 * q + 128]
    for p in range(32):
        a, b = u[2 * p], u[2 * p + 1]
        out_u_ref[p] = jnp.where(lo, a, rs(b, 4))
        out_w_ref[p] = jnp.where(lo, rs(a, 4), b)


def project_kernel(sub_ref, x_ref, stack_ref, out_ref):
    sub = sub_ref[0]
    total = (x_ref[0, sub] + x_ref[1, sub]) + (x_ref[2, sub] + x_ref[3, sub])
    t0, t1, t2 = three_way(total)
    out_ref[...] = KERNEL_SCALE * jnp.dot(
        stack_ref[...], jnp.concatenate([t0, t0, t1, t1, t2, t0], axis=0),
        preferred_element_type=jnp.float32,
    )


VMEM = pl.BlockSpec(memory_space=pltpu.VMEM)
SMEM = pl.BlockSpec(memory_space=pltpu.SMEM)
HBM = pl.BlockSpec(memory_space=pltpu.HBM)
F32, BF16 = jnp.float32, jnp.bfloat16


def call(kernel, outs, ins, scratch=(), specs=(), limit=24, space=None):
    specs = list(specs) + [VMEM] * (len(ins) - len(specs))
    outs = [o if isinstance(o, jax.ShapeDtypeStruct) else jax.ShapeDtypeStruct(o, F32) for o in outs]
    if space is not None:
        outs = [space(o.shape, o.dtype) for o in outs]
    return pl.pallas_call(
        kernel,
        out_shape=outs,
        in_specs=specs,
        out_specs=[VMEM] * len(outs),
        scratch_shapes=list(scratch),
        compiler_params=pltpu.CompilerParams(vmem_limit_bytes=limit * 1024 * 1024),
    )(*ins)


def raw_tiles(x):
    lead = int(np.prod(x.shape[:-2]))
    return x.reshape(lead, 2, 2, 128).transpose(0, 2, 1, 3).reshape(lead * 4, 128)


def from_tiles(x):
    return x.reshape(64, 2, 2, 128).transpose(0, 2, 1, 3).reshape(64, 2, 256)


def on_device(initial_field, adjoint_source, moduli, node_mass, block_owner, spline_basis):
    count = lax.axis_size("dom")
    near_pairs = [(i, i ^ 1) for i in range(count)]
    far_pairs = [(i, ((i + 1) ^ 1) - 1) for i in range(1, count - 1)]
    cf = jnp.asarray(COEFFICIENTS)
    sub = lax.axis_index("sub").astype(jnp.int32).reshape(1)
    odd = (lax.axis_index("dom") & 1).astype(jnp.int32).reshape(1)
    u2d, w2d, m2d, mass2d = map(raw_tiles, (initial_field, adjoint_source, moduli, node_mass))
    owner = raw_tiles(block_owner[None])
    mod = m2d.reshape(96, 8, 128)
    full, face = (64, 8, 128), (16, 8, 128)

    def swap_rows(far, near):
        return lax.ppermute(far, "dom", far_pairs), lax.ppermute(near, "dom", near_pairs)

    edges, base, head = call(
        first_kernel,
        [(2, 64, 128), (BASE, 8, 128), (HEAD, 8, 128)],
        [u2d, w2d, m2d, mass2d, owner, cf],
        [pltpu.VMEM((n, 128), F32) for n in (256, 256, 768, 256)]
        + [pltpu.VMEM((4, 128), jnp.int32), pltpu.VMEM((BASE - WEIGHTS, 8, 128), F32)]
        + [pltpu.SemaphoreType.DMA((6,))],
        [HBM] * 6,
        limit=FIRST_LIMIT,
        space=pltpu.VMEM,
    )
    edges = lax.all_gather(edges, "sub")
    far, near, u1p, v1p, invp, strips, smod = call(
        open_kernel,
        [(MSG, 8, 128), (MSG, 8, 128), full, full, full, (3, 64, 128), (192, 128)],
        [odd, sub, edges, base, head, mod],
        [pltpu.VMEM(full, F32), pltpu.VMEM((2, 64, 128), F32)],
        specs=[SMEM, SMEM],
        space=pltpu.VMEM,
    )
    far, near = swap_rows(far, near)
    far, near, inv, u1, u2, rims, inner, resp, sresp, sstate = call(
        middle_kernel,
        [
            (MSG_B, 8, 128), (MSG_B, 8, 128), full, full, full, (2, 32, 8, 128),
            (2, 32, 8, 128), (3, 16, 8, 128), (3, 16, 128), (4, 64, 128),
        ],
        [odd, far, near, base, head, u1p, v1p, invp, strips, smod, mod],
        [pltpu.VMEM(full, F32)] * 5 + [pltpu.VMEM((4, 64, 128), F32), pltpu.VMEM(face, F32)],
        specs=[SMEM],
        space=pltpu.VMEM,
    )
    far, near = swap_rows(far, near)
    wide = jax.ShapeDtypeStruct((512, 512), BF16)
    d2, x0, x1, hot, stack = call(
        density_kernel,
        [full, (192, 8, 128), (192, 8, 128), wide, jax.ShapeDtypeStruct((64, 384), BF16)],
        [mod, base, u1, u2, spline_basis.T],
        space=pltpu.VMEM,
    )
    out_u, out_w, sums = call(
        last_kernel,
        [(32, 8, 128), (32, 8, 128), (4, 64, 128)],
        [
            odd, far, near, mod, inv, u2, rims, inner, resp, sresp, sstate, smod,
            d2, x0, x1, hot, base,
        ],
        [pltpu.VMEM(full, F32)] * 3
        + [pltpu.VMEM((2, 64, 128), F32), pltpu.VMEM(face, F32), pltpu.VMEM((512, 128), F32)],
        specs=[SMEM],
    )
    sums = lax.all_gather(sums, "sub")
    (kernel,) = call(project_kernel, [(64, 128)], [sub, sums, stack], specs=[SMEM])
    return from_tiles(out_u), from_tiles(out_w), kernel


def solution(mesh):
    in_specs = (
        P(None, "dom", "sub"),
        P(None, "dom", "sub"),
        P(None, None, "dom", "sub"),
        P(None, "dom", "sub"),
        P("dom", "sub"),
        P(),
    )
    out_specs = (P(None, "dom", "sub"), P(None, "dom", "sub"), P(None, ("dom", "sub")))
    return jax.shard_map(
        on_device, mesh=mesh, in_specs=in_specs, out_specs=out_specs, check_vma=False
    )
```

```python
import jax
import jax.numpy as jnp
import numpy as np
from jax import lax
from jax.experimental import pallas as pl
from jax.experimental.pallas import tpu as pltpu
from jax.sharding import PartitionSpec as P

STEPS = 4
TIME_STEP = 0.1
KERNEL_SCALE = 0.05
PUSH = TIME_STEP * TIME_STEP

DERIVATIVE = np.array(
    [
        [-3.0, 4.04508497187474, -1.54508497187474, 0.5],
        [-0.80901699437495, 0.0, 1.11803398874989, -0.30901699437495],
        [0.30901699437495, -1.11803398874989, 0.0, 0.80901699437495],
        [-0.5, 1.54508497187474, -4.04508497187474, 3.0],
    ]
)
HALF_AMB = float((DERIVATIVE[0, 1] - DERIVATIVE[0, 2]) / 2)
HALF_CME = float((DERIVATIVE[1, 0] - DERIVATIVE[1, 3]) / 2)
HALF_D = float(DERIVATIVE[1, 2] / 2)

MSG, CONST, STRIP = 38, 16, 32
MSG_B, STRIP_B = 18, 16
FIRST_LIMIT = 54
U0, OWNER, WEIGHTS, BASE = 0, 64, 65, 95
F0, MASS, FACES, HEAD = 0, 64, 128, 160


def strip_coefficients():
    tiles = []
    for d in (DERIVATIVE, DERIVATIVE.T):
        for out in range(2):
            for term in range(4):
                col = np.zeros(8)
                for s in range(8):
                    j = 2 * out + s // 4
                    half = s // 4 if term % 2 == 0 else 1 - s // 4
                    col[s] = d[j, 2 * (term // 2) + half]
                tiles.append(col)
        for delta in range(-3, 4):
            col = np.zeros(8)
            for s in range(8):
                k = s % 4
                if 0 <= k + delta < 4:
                    col[s] = d[k, k + delta]
            tiles.append(col)
    return np.broadcast_to(np.array(tiles, np.float32)[:, :, None], (30, 8, 128))


COEFFICIENTS = np.ascontiguousarray(strip_coefficients())


def sub_iota():
    return lax.broadcasted_iota(jnp.int32, (8, 128), 0)


def lane_iota(rows=8):
    return lax.broadcasted_iota(jnp.int32, (rows, 128), 1)


def rs(x, shift):
    return pltpu.roll(x, shift, 0)


def rl(x, shift):
    return pltpu.roll(x, shift, 1)


def masks():
    s = sub_iota()
    lane = lane_iota()
    return dict(
        even=(s % 2) == 0,
        lo=s < 4,
        ct0=((s // 2) % 2) == 0,
        first=lane == 0,
        last=lane == 127,
    )


def d_line(x0, x1, x2, x3):
    p, m, q, n = x0 + x3, x0 - x3, x1 + x2, x1 - x2
    r = q - p
    s1 = -1.75 * m + HALF_AMB * n
    s2 = HALF_CME * m - HALF_D * n
    r1, r2 = 1.25 * r, HALF_D * r
    return s1 + r1, s2 + r2, s2 - r2, s1 - r1


def dt_line(x0, x1, x2, x3):
    p, m, q, n = x0 + x3, x0 - x3, x1 + x2, x1 - x2
    t = 1.25 * m + HALF_D * n
    q1 = HALF_CME * q - 1.75 * p
    q2 = HALF_AMB * p - HALF_D * q
    return q1 - t, t + q2, t - q2, -(q1 + t)


def line_nodes(direction, a, b):
    if direction == 0:
        return [16 * i + 4 * a + b for i in range(4)]
    if direction == 1:
        return [16 * a + 4 * j + b for j in range(4)]
    return [16 * a + 4 * b + k for k in range(4)]


def expanded(x, upper, mk):
    r = rs(x, 4)
    return jnp.where(mk["lo"], r, x) if upper else jnp.where(mk["lo"], x, r)


def forces(u, f, mod, mk, planes=(0, 1, 2, 3), hook=None):
    for direction in (2, 1, 0):
        for a in range(4):
            if direction and a not in planes:
                continue
            for b in range(4):
                nodes = line_nodes(direction, a, b)
                g = d_line(*[u(n) for n in nodes])
                if hook is not None:
                    for n, gn in zip(nodes, g):
                        hook(direction, n, gn)
                t = []
                for n, gn in zip(nodes, g):
                    at = 64 * direction + n
                    t.append(expanded(mod(at // 2), at % 2, mk) * gn)
                for n, o in zip(nodes, dt_line(*t)):
                    if n // 16 in planes:
                        f(n, o, direction == 2)


def into(ref):
    def put(n, value, first):
        ref[n] = value if first else ref[n] + value

    return put


def face_tile(get, q, mk):
    return jnp.where(mk["even"], get(q), get(48 + q))


class Send:
    def __init__(self, far_ref, near_ref, odd):
        self.far, self.near, self.odd = far_ref, near_ref, odd

    def put(self, at, left, right):
        self.far[at] = jnp.where(self.odd, right, left)
        self.near[at] = jnp.where(self.odd, left, right)


class Receive:
    def __init__(self, odd_ref, even_ref, odd):
        self.odd_ref, self.even_ref, self.odd = odd_ref, even_ref, odd

    def __getitem__(self, at):
        return jnp.where(self.odd, self.odd_ref[at], self.even_ref[at])


def pack_faces(send, base, get, mk):
    even = mk["even"]
    for p in range(8):
        x, y = get(2 * p), get(2 * p + 1)
        send.put(base + p, jnp.where(even, x, rs(y, 1)), jnp.where(even, rs(x, 7), y))


def unpack_face(from_right, from_left, base, q, mk):
    r, l = from_right[base + q // 2], from_left[base + q // 2]
    if q % 2:
        return jnp.where(mk["even"], rs(l, 7), r)
    return jnp.where(mk["even"], l, rs(r, 1))


def face_response(delta, diagonal, mod_j, mod_k):
    out = [diagonal(q) * delta[q] for q in range(16)]
    for mod, lines in (
        (mod_j, [[4 * j + k for j in range(4)] for k in range(4)]),
        (mod_k, [[4 * j + k for k in range(4)] for j in range(4)]),
    ):
        for line in lines:
            t = [mod(q) * g for q, g in zip(line, d_line(*[delta[q] for q in line]))]
            for q, o in zip(line, dt_line(*t)):
                out[q] = out[q] + o
    return out


def along_x(f, beside, i, q, mk):
    even = mk["even"]
    x = f(16 * i + q)
    if i in (1, 2):
        return x
    other = beside(q) if beside is not None else 0.0
    if i == 3:
        return x + jnp.where(even, rs(f(q), 7), other)
    return x + jnp.where(even, other, rs(f(48 + q), 1))


def assembled(f, beside, strip, i, k, mk):
    vals = [along_x(f, beside, i, 4 * j + k, mk) for j in range(4)]

    def inject(row):
        return pltpu.roll(
            jnp.broadcast_to(strip[row : row + 1, :], (8, 128)), 68, 1, stride=8, stride_axis=0
        )

    b, a = vals[0], vals[3]
    up, down = rl(b, 127), rl(a, 1)
    up = jnp.where(mk["last"], jnp.where(mk["ct0"], rs(up, 6), inject(16 * i + k)), up)
    down = jnp.where(mk["first"], jnp.where(mk["ct0"], inject(16 * i + 12 + k), rs(down, 2)), down)
    return [b + down, vals[1], vals[2], a + up]


def assemble(f, beside, strip, mk, put, planes=(0, 1, 2, 3)):
    for i in planes:
        for k in range(4):
            for j, total in enumerate(assembled(f, beside, strip, i, k, mk)):
                put(16 * i + 4 * j + k, total)


def not_shared(n, x, mk):
    if n < 16:
        return jnp.where(mk["even"], 0.0, x)
    if n >= 48:
        return jnp.where(mk["even"], x, 0.0)
    return x


def strip_lines(x, cf, base):
    along_j, along_k = [], []
    for i in range(len(x) // 2):
        a, b = x[2 * i], x[2 * i + 1]
        terms = (a, rs(a, 4), b, rs(b, 4))
        for out in range(2):
            along_j.append(sum(cf[base + 4 * out + t] * terms[t] for t in range(4)))
    for y in x:
        along_k.append(
            sum(cf[base + 8 + d] * (rs(y, (3 - d) % 8) if d != 3 else y) for d in range(7))
        )
    return along_j, along_k


def strip_forces(us, mods, cf):
    x = [us[8 * v : 8 * v + 8] for v in range(8)]
    gj, gk = strip_lines(x, cf, 0)
    gi = [None] * 8
    for e in range(2):
        for i, g in enumerate(d_line(*[x[2 * m + e] for m in range(4)])):
            gi[2 * i + e] = g
    ti, tj, tk = (
        [mods[64 * d + 8 * v : 64 * d + 8 * v + 8] * g[v] for v in range(8)]
        for d, g in enumerate((gi, gj, gk))
    )
    fj = strip_lines(tj, cf, 15)[0]
    fk = strip_lines(tk, cf, 15)[1]
    f = [fj[v] + fk[v] for v in range(8)]
    for e in range(2):
        for i, o in enumerate(dt_line(*[ti[2 * m + e] for m in range(4)])):
            f[2 * i + e] = f[2 * i + e] + o
    return jnp.concatenate(f, axis=0)


def row_zero(rows):
    return ((lane_iota(rows) // 8) % 2) == 1


def strip_faces(f):
    return jnp.where(row_zero(16), f[0:16], f[48:64])


def strip_beside(from_right, from_left, base):
    r = jnp.concatenate([from_right[base], from_right[base + 1]], axis=0)
    l = jnp.concatenate([from_left[base], from_left[base + 1]], axis=0)
    both = jnp.where(row_zero(16), rl(l, 8), rl(r, 120))
    return both, rl(both, 64)


def strip_send(send, base, x, y):
    both = jnp.where(lane_iota(16) < 64, x, rl(y, 64))
    for p in range(2):
        send.put(base + p, both[8 * p : 8 * p + 8], both[8 * p : 8 * p + 8])


def strip_response(delta, diagonal, mod_j, mod_k, cf):
    x = [delta[0:8], delta[8:16]]
    gj, gk = strip_lines(x, cf, 0)
    fj = strip_lines([mod_j[8 * v : 8 * v + 8] * gj[v] for v in range(2)], cf, 15)[0]
    fk = strip_lines([mod_k[8 * v : 8 * v + 8] * gk[v] for v in range(2)], cf, 15)[1]
    return diagonal * delta + jnp.concatenate([fj[v] + fk[v] for v in range(2)], axis=0)


def strip_x(f, beside):
    zero = row_zero(16)
    b, a = f[0:16], f[48:64]
    na = a + jnp.where(zero, rl(b, 8), beside)
    nb = b + jnp.where(zero, beside, rl(a, 120))
    return jnp.concatenate([nb, f[16:48], na], axis=0)


def strip_y(f):
    low = sub_iota() < 4
    parts = []
    for i in range(4):
        x, y = f[16 * i : 16 * i + 8], f[16 * i + 8 : 16 * i + 16]
        parts.append(x + jnp.where(low, rs(rl(y, 1), 4), 0.0))
        parts.append(y + jnp.where(low, 0.0, rs(rl(x, 127), 4)))
    return jnp.concatenate(parts, axis=0)


def inverse_mass(m):
    return jnp.where(m > 0.5, PUSH / jnp.where(m > 0.5, m, 1.0), 0.0)


def strip_not_shared(x):
    zero = row_zero(16)
    return jnp.concatenate(
        [jnp.where(zero, 0.0, x[0:16]), x[16:48], jnp.where(zero, x[48:64], 0.0)], axis=0
    )


def strip_arrays(z1, z2):
    q = lane_iota(64) // 32

    def two(a, b):
        return jnp.where(q == 0, a, jnp.where(q == 1, b, 0.0))

    us = two(z1, z1)
    m0 = two(rl(z1, 64), rl(z1, 96))
    m1 = two(rl(z1, 32), rl(z1, 64))
    m2 = two(z2, rl(z2, 32))
    mass = two(rl(z2, 96), z2)
    return us, jnp.concatenate([m0, m1, m2], axis=0), mass


def state_expand(xu, xw, mk):
    return jnp.where(mk["lo"], xu, rs(xw, 4)), jnp.where(mk["lo"], rs(xu, 4), xw)


def tile(ref, p):
    return ref[8 * p : 8 * p + 8, :]


def first_kernel(
    u_hbm, w_hbm, mod_hbm, mass_hbm, owner_hbm, cf_hbm, z_ref, base_ref, head_ref,
    u_ref, w_ref, m_ref, mass_ref, owner_ref, cf_ref, sems,
):
    state_ref, f_ref = base_ref.at[U0:OWNER], head_ref.at[F0:MASS]
    mass2_ref, const_ref = head_ref.at[MASS:FACES], head_ref.at[FACES:HEAD]
    copies = [
        pltpu.make_async_copy(src, dst, sems.at[i])
        for i, (src, dst) in enumerate(
            (
                (u_hbm, u_ref), (w_hbm, w_ref), (mod_hbm, m_ref), (mass_hbm, mass_ref),
                (owner_hbm, owner_ref), (cf_hbm, cf_ref),
            )
        )
    ]
    for c in copies:
        c.start()
    mk = masks()
    lane = lane_iota(64)
    pieces = (
        (w_ref, 0, 0, 0),
        (u_ref, 0, 0, 1),
        (m_ref, 0, 0, 2),
        (m_ref, 256, 0, 3),
        (m_ref, 512, 1, 0),
        (mass_ref, 0, 1, 1),
    )
    z = [jnp.zeros((64, 128), jnp.float32), jnp.zeros((64, 128), jnp.float32)]
    for step, (ref, base, half, slot) in enumerate(pieces):
        for arrival in ((1,), (0,), (2,), (), (), (3,))[step]:
            copies[arrival].wait()
        for side in range(2):
            for r in range(2):
                rows = ref[pl.ds(base + 2 * (1 - side) + r, 64, stride=4), :]
                dest = slot * 32 + (1 - side) * 16 + (1 - r) * 8 + (3 if side else 1)
                src = 0 if side else 124
                moved = rl(rows, (dest - src) % 128)
                z[half] = jnp.where((lane >= dest) & (lane < dest + 4), moved, z[half])
    z_ref[0] = z[0]
    z_ref[1] = z[1]
    for p in range(32):
        a, b = state_expand(tile(u_ref, p), tile(w_ref, p), mk)
        state_ref[2 * p] = a
        state_ref[2 * p + 1] = b
        mass2_ref[2 * p] = expanded(tile(mass_ref, p), 0, mk)
        mass2_ref[2 * p + 1] = expanded(tile(mass_ref, p), 1, mk)

    def moduli(direction):
        def get(n):
            at = 64 * direction + n
            return expanded(tile(m_ref, at // 2), at % 2, mk)

        return get

    for q in range(16):
        mi = [moduli(0)(16 * i + q) for i in range(4)]
        diagonal = [sum(float(DERIVATIVE[i, e] ** 2) * mi[i] for i in range(4)) for e in (0, 3)]
        diagonal = jnp.where(mk["even"], diagonal[0], diagonal[1])
        own_mass = face_tile(lambda n: mass2_ref[n], q, mk)
        const_ref[q] = jnp.where(mk["lo"], own_mass, diagonal)
        const_ref[16 + q] = jnp.where(
            mk["lo"], face_tile(moduli(1), q, mk), face_tile(moduli(2), q, mk)
        )
    forces(lambda n: state_ref[n], into(f_ref), lambda p: tile(m_ref, p), mk)
    copies[4].wait()
    copies[5].wait()
    owner = owner_ref[...].astype(jnp.float32)
    base_ref[OWNER] = jnp.concatenate([owner, owner], axis=0)
    for t in range(WEIGHTS, BASE):
        base_ref[t] = cf_ref[t - WEIGHTS]


def open_kernel(
    odd_ref, sub_ref, z_ref, base_ref, head_ref, mod_ref,
    far_ref, near_ref, u1_ref, v1_ref, inv_ref, strip_ref, smod_ref,
    f, sx,
):
    u0_ref, f0_ref = base_ref.at[U0:OWNER], head_ref.at[F0:MASS]
    mass2_ref, const_ref = head_ref.at[MASS:FACES], head_ref.at[FACES:HEAD]
    cf_ref = base_ref.at[WEIGHTS:BASE]
    mk = masks()
    sub = sub_ref[0]
    send = Send(far_ref, near_ref, odd_ref[0] == 1)
    lane = lane_iota(64)
    side0 = ((lane // 16) % 2) == 1
    c = lane % 8
    below, above = jnp.maximum(sub - 1, 0), jnp.minimum(sub + 1, 3)
    zs = []
    for half in range(2):
        own = z_ref[sub, half]
        zl = jnp.where(sub > 0, z_ref[below, half], 0.0)
        zr = jnp.where(sub < 3, z_ref[above, half], 0.0)
        low = jnp.where(c == 0, 0.0, jnp.where(c <= 4, zl, rl(own, 18)))
        high = jnp.where(c <= 2, rl(own, 110), jnp.where(c == 7, 0.0, zr))
        zs.append(jnp.where(side0, low, high))
    us, mods, smass = strip_arrays(zs[0], zs[1])
    fs = strip_forces(us, mods, cf_ref)
    smod_ref[...] = mods
    strip_ref[0] = us
    strip_ref[1] = fs
    strip_ref[2] = smass
    zero = row_zero(16)
    diagonal = [
        sum(float(DERIVATIVE[i, e] ** 2) * mods[16 * i : 16 * i + 16] for i in range(4))
        for e in (0, 3)
    ]
    strip_send(
        send, STRIP + 2, strip_faces(smass), jnp.where(zero, *diagonal)
    )
    strip_send(
        send, STRIP + 4, strip_faces(mods[64:128]), strip_faces(mods[128:192])
    )
    sm = strip_x(smass, 0.0)
    sx[0] = sm
    fx = strip_x(fs, 0.0)
    sx[1] = fx
    sinv = strip_not_shared(inverse_mass(strip_y(sm)))
    partial = strip_forces(us - sinv * strip_y(fx), mods, cf_ref)
    strip_send(send, STRIP, strip_faces(fs), strip_faces(partial))

    def put_mass(n, total):
        inv_ref[n] = not_shared(n, inverse_mass(total), mk)

    assemble(lambda n: mass2_ref[n], None, sx.at[0], mk, put_mass)

    def put(n, total):
        vel = -inv_ref[n] * total
        v1_ref[n] = vel
        u1_ref[n] = u0_ref[n] + vel

    assemble(lambda n: f0_ref[n], None, sx.at[1], mk, put)
    forces(lambda n: u1_ref[n], into(f), lambda p: mod_ref[p], mk, planes=(0, 3))
    pack_faces(send, 0, lambda q: face_tile(lambda n: f0_ref[n], q, mk), mk)
    pack_faces(send, 8, lambda q: face_tile(lambda n: f[n], q, mk), mk)
    pack_faces(send, CONST, lambda q: const_ref[q], mk)
    pack_faces(send, CONST + 8, lambda q: const_ref[16 + q], mk)


def rim(n):
    return n if n < 16 else n - 32


def middle_kernel(
    odd_ref, far_in, near_in, base_ref, head_ref, u1p_ref, v1p_ref, invp_ref, strip_ref, smod_ref,
    mod_ref,
    far_ref, near_ref, inv_ref, u1_ref, u2_ref, rims_ref, inner_ref, resp_ref, sresp_ref, sstate_ref,
    v1, f, v2_ref, f2_ref, u3_ref, sx, beside,
):
    u0_ref, f0_ref = base_ref.at[U0:OWNER], head_ref.at[F0:MASS]
    mass2_ref, cf_ref = head_ref.at[MASS:FACES], base_ref.at[WEIGHTS:BASE]
    mk = masks()
    odd = odd_ref[0] == 1
    mr_ref, ml_ref = Receive(far_in, near_in, odd), Receive(near_in, far_in, odd)
    send = Send(far_ref, near_ref, odd)
    lo = mk["lo"]
    us, fs, smass = strip_ref[0], strip_ref[1], strip_ref[2]
    mods = smod_ref[...]
    sf0, sp1 = strip_beside(mr_ref, ml_ref, STRIP)
    smn, sresp0 = strip_beside(mr_ref, ml_ref, STRIP + 2)
    sresp1, sresp2 = strip_beside(mr_ref, ml_ref, STRIP + 4)
    sresp_ref[0] = sresp0
    sresp_ref[1] = sresp1
    sresp_ref[2] = sresp2
    for q in range(16):
        x = unpack_face(mr_ref, ml_ref, CONST, q, mk)
        r = rs(x, 4)
        beside[q] = jnp.where(lo, x, r)
        resp_ref[0, q] = jnp.where(lo, r, x)
        x = unpack_face(mr_ref, ml_ref, CONST + 8, q, mk)
        r = rs(x, 4)
        resp_ref[1, q] = jnp.where(lo, x, r)
        resp_ref[2, q] = jnp.where(lo, r, x)
    responses = [lambda q, d=d: resp_ref[d, q] for d in range(3)]
    sm = strip_x(smass, smn)
    sx[0] = sm
    sinv = inverse_mass(strip_y(sm))
    for n in range(16, 48):
        inv_ref[n] = invp_ref[n]
        u1_ref[n] = u1p_ref[n]
        v1[n] = v1p_ref[n]

    def put_mass(n, total):
        inv_ref[n] = inverse_mass(total)

    assemble(lambda n: mass2_ref[n], lambda q: beside[q], sx.at[0], mk, put_mass, (0, 3))
    fs = strip_x(fs, sf0)
    sx[1] = fs
    svel = -sinv * strip_y(fs)
    us = us + svel

    def put0(n, total):
        vel = -inv_ref[n] * total
        v1[n] = vel
        u1_ref[n] = u0_ref[n] + vel

    assemble(
        lambda n: f0_ref[n], lambda q: unpack_face(mr_ref, ml_ref, 0, q, mk), sx.at[1], mk, put0,
        (0, 3),
    )
    forces(lambda n: u1_ref[n], into(f), lambda p: mod_ref[p], mk)
    delta = [face_tile(lambda n: v1[n], q, mk) for q in range(16)]
    for q, x in enumerate(face_response(delta, *responses)):
        beside[q] = unpack_face(mr_ref, ml_ref, 8, q, mk) + x
    sbeside = sp1 + strip_response(strip_faces(svel), sresp0, sresp1, sresp2, cf_ref)
    fs = strip_x(strip_forces(us, mods, cf_ref), sbeside)
    sx[2] = fs
    svel = svel - sinv * strip_y(fs)
    us = us + svel

    def put1(n, total):
        vel = v1[n] - inv_ref[n] * total
        v2_ref[n] = vel
        u2_ref[n] = u1_ref[n] + vel

    assemble(lambda n: f[n], lambda q: beside[q], sx.at[2], mk, put1)
    forces(lambda n: u2_ref[n], into(f2_ref), lambda p: mod_ref[p], mk)
    fs = strip_forces(us, mods, cf_ref)
    sstate_ref[0] = us
    sstate_ref[1] = svel
    sstate_ref[2] = fs
    sstate_ref[3] = sinv
    fx = strip_x(fs, 0.0)
    sx[3] = fx
    partial = strip_forces(
        us + (svel - strip_not_shared(sinv) * strip_y(fx)), mods, cf_ref
    )

    def put2(n, total):
        vel = v2_ref[n] - not_shared(n, inv_ref[n], mk) * total
        u3_ref[n] = u2_ref[n] + vel
        if 16 <= n < 48:
            inner_ref[0, n - 16] = u3_ref[n]
            inner_ref[1, n - 16] = vel

    assemble(lambda n: f2_ref[n], None, sx.at[3], mk, put2)
    for n in list(range(16)) + list(range(48, 64)):
        rims_ref[0, rim(n)] = v2_ref[n]
        rims_ref[1, rim(n)] = f2_ref[n]
    forces(lambda n: u3_ref[n], into(f), lambda p: mod_ref[p], mk, planes=(0, 3))
    pack_faces(send, 0, lambda q: face_tile(lambda n: f2_ref[n], q, mk), mk)
    pack_faces(send, 8, lambda q: face_tile(lambda n: f[n], q, mk), mk)
    strip_send(send, STRIP_B, strip_faces(fs), strip_faces(partial))


def three_way(x):
    hi = x.astype(jnp.bfloat16)
    rest = x - hi.astype(jnp.float32)
    mid = rest.astype(jnp.bfloat16)
    return hi, mid, (rest - mid.astype(jnp.float32)).astype(jnp.bfloat16)


def density_kernel(
    mod_ref, base_ref, u1_ref, u2_ref, basis_ref, d2_ref, x0_ref, x1_ref, hot_ref, stack_ref
):
    mk = masks()
    lo = mk["lo"]
    for direction in (2, 1, 0):
        for a in range(4):
            for b in range(4):
                nodes = line_nodes(direction, a, b)
                g0 = d_line(*[base_ref[U0 + n] for n in nodes])
                g1 = d_line(*[u1_ref[n] for n in nodes])
                g2 = d_line(*[u2_ref[n] for n in nodes])
                for e, n in enumerate(nodes):
                    at = 64 * direction + n
                    m = expanded(mod_ref[at // 2], at % 2, mk)
                    x0_ref[at] = jnp.where(lo, m * rs(g0[e], 4), 0.0)
                    x1_ref[at] = m * rs(g1[e], 4)
                    t = jnp.where(lo, m * g2[e] * rs(g2[e], 4), 0.0)
                    d2_ref[n] = t if direction == 2 else d2_ref[n] + t
    block = lax.broadcasted_iota(jnp.int32, (512, 128), 0).astype(jnp.float32)
    for s in range(4):
        owner = jnp.broadcast_to(base_ref[OWNER][s : s + 1, :], (512, 128))
        hot_ref[:, 128 * s : 128 * s + 128] = (
            (block == owner).astype(jnp.float32).astype(jnp.bfloat16)
        )
    b0, b1, b2 = three_way(basis_ref[...])
    stack_ref[...] = jnp.concatenate([b0, b1, b0, b1, b0, b2], axis=1)


def last_kernel(
    odd_ref, far_in, near_in, mod_ref, inv_ref, u2_ref, rims_ref, inner_ref, resp_ref,
    sresp_ref, sstate_ref, smod_ref, d2_ref, x0_ref, x1_ref, hot_ref, base_ref,
    out_u_ref, out_w_ref, sums_ref,
    u, v, f, sx, beside, dens, finals, sems,
):
    cf_ref = base_ref.at[WEIGHTS:BASE]
    mk = masks()
    odd = odd_ref[0] == 1
    br_ref, bl_ref = Receive(far_in, near_in, odd), Receive(near_in, far_in, odd)
    lo = mk["lo"]
    mods = smod_ref[...]
    us, svel, fs, sinv = sstate_ref[0], sstate_ref[1], sstate_ref[2], sstate_ref[3]
    sf2, sp3 = strip_beside(br_ref, bl_ref, STRIP_B)
    fs = strip_x(fs, sf2)
    sx[0] = fs
    spush = -sinv * strip_y(fs)
    us = us + (svel + spush)
    for n in range(16, 48):
        u[n] = inner_ref[0, n - 16]
        v[n] = inner_ref[1, n - 16]

    def put2(n, total):
        vel = rims_ref[0, rim(n)] - inv_ref[n] * total
        v[n] = vel
        u[n] = u2_ref[n] + vel

    assemble(
        lambda n: rims_ref[1, rim(n)], lambda q: unpack_face(br_ref, bl_ref, 0, q, mk), sx.at[0],
        mk, put2, (0, 3),
    )

    def add_third(direction, n, g):
        at = pl.ds(8 * n, 8)
        before = d2_ref[n] if direction == 2 else dens[at, :]
        dens[at, :] = before + x1_ref[64 * direction + n] * g

    forces(lambda n: u[n], into(f), lambda p: mod_ref[p], mk, hook=add_third)
    delta = [face_tile(lambda n: v[n] - rims_ref[0, rim(n)], q, mk) for q in range(16)]
    for q, x in enumerate(face_response(delta, *[lambda q, d=d: resp_ref[d, q] for d in range(3)])):
        beside[q] = unpack_face(br_ref, bl_ref, 8, q, mk) + x
    sbeside = sp3 + strip_response(
        strip_faces(spush), sresp_ref[0], sresp_ref[1], sresp_ref[2], cf_ref
    )
    sx[1] = strip_x(strip_forces(us, mods, cf_ref), sbeside)

    def put3(n, total):
        u[n] = u[n] + (v[n] - inv_ref[n] * total)

    assemble(lambda n: f[n], lambda q: beside[q], sx.at[1], mk, put3)
    for p in range(32):
        a, b = u[2 * p], u[2 * p + 1]
        finals[0, p] = jnp.where(lo, a, rs(b, 4))
        finals[1, p] = jnp.where(lo, rs(a, 4), b)
    copies = [
        pltpu.make_async_copy(finals.at[i], out, sems.at[i])
        for i, out in enumerate((out_u_ref, out_w_ref))
    ]
    for c in copies:
        c.start()
    for direction in (2, 1, 0):
        for a in range(4):
            for b in range(4):
                nodes = line_nodes(direction, a, b)
                for n, g in zip(nodes, d_line(*[u[n] for n in nodes])):
                    at = pl.ds(8 * n, 8)
                    dens[at, :] = dens[at, :] + x0_ref[64 * direction + n] * g
    cols = [
        dens[pl.ds(s, 64, stride=8), :] + dens[pl.ds(s + 4, 64, stride=8), :] for s in range(4)
    ]
    split = jnp.concatenate(three_way(jnp.concatenate(cols, axis=1)), axis=0)
    res = lax.dot_general(
        split, hot_ref[...], (((1,), (1,)), ((), ())), preferred_element_type=jnp.float32
    )
    sums = res[0:64] + (res[64:128] + res[128:192])
    for q in range(4):
        sums_ref[q] = sums[:, 128 * q : 128 * q + 128]
    for c in copies:
        c.wait()


def project_kernel(sub_ref, x_ref, stack_ref, out_ref):
    sub = sub_ref[0]
    total = (x_ref[0, sub] + x_ref[1, sub]) + (x_ref[2, sub] + x_ref[3, sub])
    t0, t1, t2 = three_way(total)
    out_ref[...] = KERNEL_SCALE * jnp.dot(
        stack_ref[...], jnp.concatenate([t0, t0, t1, t1, t2, t0], axis=0),
        preferred_element_type=jnp.float32,
    )


VMEM = pl.BlockSpec(memory_space=pltpu.VMEM)
SMEM = pl.BlockSpec(memory_space=pltpu.SMEM)
HBM = pl.BlockSpec(memory_space=pltpu.HBM)
F32, BF16 = jnp.float32, jnp.bfloat16


def call(kernel, outs, ins, scratch=(), specs=(), limit=24, space=None, out_specs=()):
    specs = list(specs) + [VMEM] * (len(ins) - len(specs))
    outs = [o if isinstance(o, jax.ShapeDtypeStruct) else jax.ShapeDtypeStruct(o, F32) for o in outs]
    if space is not None:
        outs = [space(o.shape, o.dtype) for o in outs]
    return pl.pallas_call(
        kernel,
        out_shape=outs,
        in_specs=specs,
        out_specs=list(out_specs) + [VMEM] * (len(outs) - len(out_specs)),
        scratch_shapes=list(scratch),
        compiler_params=pltpu.CompilerParams(vmem_limit_bytes=limit * 1024 * 1024),
    )(*ins)


def raw_tiles(x):
    lead = int(np.prod(x.shape[:-2]))
    return x.reshape(lead, 2, 2, 128).transpose(0, 2, 1, 3).reshape(lead * 4, 128)


def from_tiles(x):
    return x.reshape(64, 2, 2, 128).transpose(0, 2, 1, 3).reshape(64, 2, 256)


def on_device(initial_field, adjoint_source, moduli, node_mass, block_owner, spline_basis):
    count = lax.axis_size("dom")
    near_pairs = [(i, i ^ 1) for i in range(count)]
    far_pairs = [(i, ((i + 1) ^ 1) - 1) for i in range(1, count - 1)]
    cf = jnp.asarray(COEFFICIENTS)
    sub = lax.axis_index("sub").astype(jnp.int32).reshape(1)
    odd = (lax.axis_index("dom") & 1).astype(jnp.int32).reshape(1)
    u2d, w2d, m2d, mass2d = map(raw_tiles, (initial_field, adjoint_source, moduli, node_mass))
    owner = raw_tiles(block_owner[None])
    mod = m2d.reshape(96, 8, 128)
    full, face = (64, 8, 128), (16, 8, 128)

    def swap_rows(far, near):
        return lax.ppermute(far, "dom", far_pairs), lax.ppermute(near, "dom", near_pairs)

    edges, base, head = call(
        first_kernel,
        [(2, 64, 128), (BASE, 8, 128), (HEAD, 8, 128)],
        [u2d, w2d, m2d, mass2d, owner, cf],
        [pltpu.VMEM((n, 128), F32) for n in (256, 256, 768, 256)]
        + [pltpu.VMEM((4, 128), jnp.int32), pltpu.VMEM((BASE - WEIGHTS, 8, 128), F32)]
        + [pltpu.SemaphoreType.DMA((6,))],
        [HBM] * 6,
        limit=FIRST_LIMIT,
        space=pltpu.VMEM,
    )
    edges = lax.all_gather(edges, "sub")
    far, near, u1p, v1p, invp, strips, smod = call(
        open_kernel,
        [(MSG, 8, 128), (MSG, 8, 128), full, full, full, (3, 64, 128), (192, 128)],
        [odd, sub, edges, base, head, mod],
        [pltpu.VMEM(full, F32), pltpu.VMEM((2, 64, 128), F32)],
        specs=[SMEM, SMEM],
        space=pltpu.VMEM,
    )
    far, near = swap_rows(far, near)
    far, near, inv, u1, u2, rims, inner, resp, sresp, sstate = call(
        middle_kernel,
        [
            (MSG_B, 8, 128), (MSG_B, 8, 128), full, full, full, (2, 32, 8, 128),
            (2, 32, 8, 128), (3, 16, 8, 128), (3, 16, 128), (4, 64, 128),
        ],
        [odd, far, near, base, head, u1p, v1p, invp, strips, smod, mod],
        [pltpu.VMEM(full, F32)] * 5 + [pltpu.VMEM((4, 64, 128), F32), pltpu.VMEM(face, F32)],
        specs=[SMEM],
        space=pltpu.VMEM,
    )
    far, near = swap_rows(far, near)
    wide = jax.ShapeDtypeStruct((512, 512), BF16)
    d2, x0, x1, hot, stack = call(
        density_kernel,
        [full, (192, 8, 128), (192, 8, 128), wide, jax.ShapeDtypeStruct((64, 384), BF16)],
        [mod, base, u1, u2, spline_basis.T],
        space=pltpu.VMEM,
    )
    out_u, out_w, sums = call(
        last_kernel,
        [(32, 8, 128), (32, 8, 128), (4, 64, 128)],
        [
            odd, far, near, mod, inv, u2, rims, inner, resp, sresp, sstate, smod,
            d2, x0, x1, hot, base,
        ],
        [pltpu.VMEM(full, F32)] * 3
        + [pltpu.VMEM((2, 64, 128), F32), pltpu.VMEM(face, F32), pltpu.VMEM((512, 128), F32)]
        + [pltpu.VMEM((2, 32, 8, 128), F32), pltpu.SemaphoreType.DMA((2,))],
        specs=[SMEM],
        out_specs=[HBM, HBM],
    )
    sums = lax.all_gather(sums, "sub")
    (kernel,) = call(project_kernel, [(64, 128)], [sub, sums, stack], specs=[SMEM])
    return from_tiles(out_u), from_tiles(out_w), kernel


def solution(mesh):
    in_specs = (
        P(None, "dom", "sub"),
        P(None, "dom", "sub"),
        P(None, None, "dom", "sub"),
        P(None, "dom", "sub"),
        P("dom", "sub"),
        P(),
    )
    out_specs = (P(None, "dom", "sub"), P(None, "dom", "sub"), P(None, ("dom", "sub")))
    return jax.shard_map(
        on_device, mesh=mesh, in_specs=in_specs, out_specs=out_specs, check_vma=False
    )
```
